256 devices in a mesh: lat: 8 (over z), lon: 8 (over x, core), mem: 4 (over y).
Axes of the slice: x: 4, y: 4, z: 8, core: 2. Of those that a mesh axis runs over, the one named last changes fastest.
Arguments:
- latent: bfloat16 [4, 96, 1024, 1024], P('mem', 'lat', 'lon'), may hold values from -6 to 6
- norm_gain: float32 [1024], replicated, may hold values from 0.1 to 1.9
- hidden_weight: bfloat16 [1024, 1024], replicated, may hold values from -0.1875 to 0.1875
- hidden_bias: float32 [1024], replicated, may hold values from -3 to 3
- output_weight: bfloat16 [1024, 80], replicated, may hold values from -0.1875 to 0.1875
- flux_table: float32 [3, 80], replicated, may hold values from -4 to 4
- target: float32 [4, 96], P('mem', 'lat'), may hold values from -8 to 8
- land_sea: int32 [96, 1024], P('lat', 'lon'), may hold values from 0 to 2
- band_index: int32 [96], P('lat'), may hold values from 1 to 719, as said below
Outputs:
- grad_latent: bfloat16 [4, 96, 1024, 1024], P('mem', 'lat', 'lon')
- grad_hidden_weight: float32 [1024, 1024], P('mem')
- grad_output_weight: float32 [1024, 80], replicated
- grad_gain: float32 [1024], replicated
- grad_hidden_bias: float32 [1024], replicated
The draws below stay inside these ranges and needn't reach their ends.
Inputs may be any that keep to these rules, and one draw needn't show every extreme that they name: `band_index`: strictly increasing along the rows; the first row is band 1 and the last band 719.
All inputs are finite; a program needn't handle non-finite values.
Results may differ from the reference program's by a relative error of at most 0.006.
Values sent between devices are 32-bit elements; how exact they have to be, the bound alone decides.
A program may use at most 128 MiB of HBM per device.

```python
import jax
import jax.numpy as jnp
from jax import lax

D = 1024
HID = 1024
CH = 80
MEMBERS = 4
LATS = 96
NLON = 1024


def draw_band_index(key, part):
    key = jax.random.fold_in(key, 5)
    interior = jax.random.permutation(key, 717)[:LATS - 2].astype(jnp.int32) + 2
    extremes = jnp.array([1, 719], dtype=jnp.int32)
    return jnp.sort(jnp.concatenate([extremes, interior])).astype(jnp.int32)


def plant(result, rng, least, largest):
    extent = result.shape
    index_at = [jax.random.randint(jax.random.fold_in(rng, axis), (), 0, extent[axis]) for axis in range(len(extent))]
    result = result.at[tuple(index_at)].set(least)
    longest = extent.index(max(extent))
    index_at[longest] = (index_at[longest] + 1) % extent[longest]
    return result.at[tuple(index_at)].set(largest)


def shard_levels(stream_key, shape, cuts, smallest, largest):
    level, own = 1.0, jax.random.fold_in(stream_key, 6)
    for dim, parts in cuts:
        steps = jnp.exp(jax.random.uniform(jax.random.fold_in(own, dim), (parts,), jnp.float32, smallest / len(cuts), largest / len(cuts)))
        level = level * jnp.repeat(steps, shape[dim] // parts).reshape([-1 if axis == dim else 1 for axis in range(len(shape))])
    return level


def centred(rng, shape, scale, most, cuts=(), held_as=jnp.bfloat16):
    values = scale * jax.random.normal(rng, shape, jnp.float32)
    if cuts:
        values = values * shard_levels(rng, shape, cuts, -0.22, 0.18)
    return jnp.clip(values, -most, most).astype(held_as)


def setup_inputs(seed: int = 0) -> dict:
    key_of = jax.random.split(jax.random.key(seed), 10)
    latent = centred(key_of[0], (MEMBERS, LATS, NLON, D), 1.0, 6.0, ((0, 4), (1, 8), (2, 8)))
    norm_gain = jnp.clip(1.0 + 0.18 * jax.random.normal(key_of[1], (D,), jnp.float32), 0.1, 1.9)
    hidden_weight = centred(key_of[2], (D, HID), D ** -0.5, 0.1875)
    hidden_bias = centred(key_of[3], (HID,), 0.5, 3.0, (), jnp.float32)
    output_weight = centred(key_of[4], (HID, CH), HID ** -0.5, 0.1875)
    flux_table = centred(key_of[5], (3, CH), 1.0, 4.0, (), jnp.float32)
    target = centred(key_of[6], (MEMBERS, LATS), 2.0, 8.0, ((0, 4), (1, 8)), jnp.float32)
    land_sea = plant(jax.random.randint(key_of[7], (LATS, NLON), 0, 3), jax.random.fold_in(key_of[7], 1), 0, 2).astype(jnp.int32)
    band_index = draw_band_index(jax.random.fold_in(key_of[9], 71), 0)
    return {"latent": latent, "norm_gain": norm_gain, "hidden_weight": hidden_weight, "hidden_bias": hidden_bias, "output_weight": output_weight, "flux_table": flux_table, "target": target, "land_sea": land_sea, "band_index": band_index}


def contract_cells(left, right):
    return lax.dot_general(left, right, (((0,), (0,)), ((), ())), preferred_element_type=jnp.float32)

def decode(flat_cells, norm_gain, hidden_weight, hidden_bias, output_weight):
    features = flat_cells.astype(jnp.float32)
    inv_rms = lax.rsqrt(lax.optimization_barrier(jnp.mean(features * features, axis=-1, keepdims=True)) + 1e-05)
    normed = (features * inv_rms * norm_gain).astype(jnp.bfloat16)
    preact = jnp.dot(normed, hidden_weight, preferred_element_type=jnp.float32) + hidden_bias
    active = jax.nn.silu(preact).astype(jnp.bfloat16)
    decoded = jnp.dot(active, output_weight, preferred_element_type=jnp.float32)
    return (features, inv_rms, normed, preact, active, decoded)

def surface_table(cell_types, flux_table):
    onehot = (cell_types[:, None] == jnp.arange(3, dtype=jnp.int32)[None, :]).astype(jnp.float32)
    return jnp.dot(onehot, flux_table, precision=lax.Precision.HIGHEST)

def backward_cells(pieces, table, flux_grad, norm_gain, hidden_weight, output_weight):
    features, inv_rms, normed, preact, active, decoded = pieces
    decoded_grad = (flux_grad[:, None] * table).astype(jnp.bfloat16)
    grad_out = contract_cells(active, decoded_grad)
    active_grad = lax.dot_general(decoded_grad, output_weight, (((1,), (1,)), ((), ())), preferred_element_type=jnp.float32)
    sigma = jax.nn.sigmoid(preact)
    preact_grad = (active_grad * sigma * (1.0 + preact * (1.0 - sigma))).astype(jnp.bfloat16)
    grad_bias = lax.optimization_barrier(jnp.sum(preact_grad.astype(jnp.float32), axis=0))
    grad_hidden = contract_cells(normed, preact_grad)
    normed_grad = lax.dot_general(preact_grad, hidden_weight, (((1,), (1,)), ((), ())), preferred_element_type=jnp.float32)
    grad_gain = lax.optimization_barrier(jnp.sum(normed_grad * features * inv_rms, axis=0))
    scaled = normed_grad * norm_gain
    grad_cells = inv_rms * scaled - features * inv_rms ** 3 * lax.optimization_barrier(jnp.mean(scaled * features, axis=-1, keepdims=True))
    return (grad_cells.astype(jnp.bfloat16), grad_hidden, grad_out, grad_gain, grad_bias)

def reference(latent, norm_gain, hidden_weight, hidden_bias, output_weight, flux_table, target, land_sea, band_index):
    members, lats, nlon, width = latent.shape
    row_ids = jnp.arange(lats, dtype=jnp.int32)

    def row_pieces(row):
        row_latent = lax.dynamic_index_in_dim(latent, row, 1, keepdims=False).reshape(-1, width)
        row_types = lax.dynamic_index_in_dim(land_sea, row, 0, keepdims=False)
        cell_types = jnp.broadcast_to(row_types[None, :], (members, nlon)).reshape(-1)
        pieces = decode(row_latent, norm_gain, hidden_weight, hidden_bias, output_weight)
        return (pieces, surface_table(cell_types, flux_table))

    def forward_row(row):
        pieces, table = row_pieces(row)
        return lax.optimization_barrier(jnp.sum((pieces[5] * table).reshape(members, nlon, -1), axis=(1, 2)))
    row_sums = lax.map(forward_row, row_ids)
    zonal = row_sums.T / nlon
    coslat = jnp.cos(jnp.pi * (band_index.astype(jnp.float32) / 720.0 - 0.5))
    transport = jnp.cumsum(coslat[None, :] * zonal, axis=1)
    misfit = transport - target
    southward = lax.cumsum(misfit, axis=1, reverse=True)
    flux_grad = coslat[None, :] * southward / lats

    def backward_row(totals, row):
        pieces, table = row_pieces(row)
        row_grad = jnp.broadcast_to(lax.dynamic_index_in_dim(flux_grad, row, 1, keepdims=True), (members, nlon)).reshape(-1)
        grad_cells, grad_hidden, grad_out, grad_gain, grad_bias = backward_cells(pieces, table, row_grad, norm_gain, hidden_weight, output_weight)
        totals = (totals[0] + grad_hidden, totals[1] + grad_out, totals[2] + grad_gain, totals[3] + grad_bias)
        return (totals, grad_cells.reshape(members, nlon, width))
    start = (jnp.zeros(hidden_weight.shape, jnp.float32), jnp.zeros(output_weight.shape, jnp.float32), jnp.zeros((width,), jnp.float32), jnp.zeros(hidden_bias.shape, jnp.float32))
    totals, grad_rows = lax.scan(backward_row, start, row_ids)
    grad_latent = jnp.moveaxis(grad_rows, 0, 1)
    return (grad_latent, totals[0], totals[1], totals[2], totals[3])
```

```python
import functools
import math

import jax
import jax.numpy as jnp
from jax import lax
from jax.experimental import pallas as pl
from jax.experimental.pallas import tpu as pltpu
from jax.sharding import PartitionSpec as P

MESH = pl.DeviceIdType.MESH
F32 = jnp.float32
BF16 = jnp.bfloat16
HIGH = lax.Precision.HIGHEST

CELLS = 1536
ROWS = 12
COLS = 128
D = 1024
CHUNK = 256
NCHUNK = CELLS // CHUNK
LANES = 128
TILES = D // LANES
NX, NY, NZ, NLON = 4, 4, 8, 8


def remote(src, dst, send_sem, recv_sem, **where):
    return pltpu.make_async_remote_copy(
        src_ref=src,
        dst_ref=dst,
        send_sem=send_sem,
        recv_sem=recv_sem,
        device_id=where,
        device_id_type=MESH,
    )


def kernel(
    lat_hbm, gain_ref, w1_hbm, bias_ref, w2_ref, table_ref, target_ref, types_ref, band_ref,
    outlat_hbm, outhid_hbm, outw_ref, outgain_ref, outbias_ref,
    x_ref, w1_ref, n_ref, nt_ref, v_ref, u_ref, inv_ref, coef_ref, tcol_ref, square_ref,
    q_ref, tab_ref, s_ref, b_ref, fb_ref, gacc_ref, stage_ref,
    mine_ref, ex1_ref, line_ref, ex2_ref,
    give_ref, take_ref, own_ref, pass_ref, plain_ref, agg_ref, part_ref, cross_ref, piece_ref, depth_ref,
    hid_ref, sm_ref, sm1_ref, t1_ref, sm2_ref, t2_ref, sm3_ref, smo_ref,
    xsem, wsem, osem, hsem,
    ex1_s, ex1_r, ex2_s, ex2_r, core_s, core_r, r4_s, r4_r, cross_s, cross_r, depth_s, depth_r,
    agz_s, agz_r, agx_s, agx_r, agc_s, agc_r, sm1_s, sm1_r, sm2_s, sm2_r, sm3_s, sm3_r, sm4_s, sm4_r,
):
    z = lax.axis_index("lat")
    lon = lax.axis_index("lon")
    y = lax.axis_index("mem")
    x = lon // 2
    core = lon % 2

    def lon_at(step):
        return lax.rem(x + step, NX) * 2 + core

    def chunk_rows(i):
        return pl.ds(i * CHUNK, CHUNK)

    loads = [pltpu.make_async_copy(lat_hbm.at[chunk_rows(i)], x_ref.at[chunk_rows(i)], xsem.at[i]) for i in range(NCHUNK)]
    wload = pltpu.make_async_copy(w1_hbm, w1_ref, wsem)
    loads[0].start()
    wload.start()
    for i in range(1, NCHUNK):
        loads[i].start()

    barrier = pltpu.get_barrier_semaphore()
    for k in range(1, NLON):
        pl.semaphore_signal(barrier, inc=1, device_id={"lon": lax.rem(lon + k, NLON)}, device_id_type=MESH)
    for k in range(1, NZ):
        pl.semaphore_signal(barrier, inc=1, device_id={"lat": lax.rem(z + k, NZ)}, device_id_type=MESH)
    for k in range(1, NY):
        pl.semaphore_signal(barrier, inc=1, device_id={"mem": lax.rem(y + k, NY)}, device_id_type=MESH)

    tab_ref[...] = jnp.zeros_like(tab_ref)
    tab_ref[0:3, :] = table_ref[...]
    table = tab_ref[...]
    high = table.astype(BF16)
    rest = table - high.astype(F32)
    middle = rest.astype(BF16)
    w2 = w2_ref[...]
    dims = (((1,), (1,)), ((), ()))
    q_ref[...] = lax.dot_general(high, w2, dims, preferred_element_type=F32) + lax.dot_general(
        middle, w2, dims, preferred_element_type=F32
    )
    square_ref[...] = jnp.zeros_like(square_ref)
    square_ref[0:ROWS, :] = types_ref[...].astype(F32)
    turned = square_ref[...].T
    for r in range(ROWS):
        tcol_ref[r * COLS : (r + 1) * COLS, :] = jnp.broadcast_to(turned[:, r : r + 1], (COLS, LANES))

    gain = gain_ref[...]
    bias = bias_ref[...]

    def normalise(i):
        rows = chunk_rows(i)
        loads[i].wait()
        xf = x_ref[rows, :].astype(F32)
        inv = lax.rsqrt(jnp.mean(xf * xf, axis=-1, keepdims=True) + 1e-05)
        inv_ref[rows, :] = jnp.broadcast_to(inv, (CHUNK, LANES))
        n_ref[rows, :] = (xf * inv * gain).astype(BF16)

    def first_dot(i):
        rows = chunk_rows(i)
        v_ref[rows, :] = jnp.dot(n_ref[rows, :], w1_ref[...], preferred_element_type=F32)

    kind = lax.broadcasted_iota(jnp.int32, (16, COLS), 0)

    def activate(i):
        rows = chunk_rows(i)
        p = v_ref[rows, :] + bias
        act = (p * (0.5 * jnp.tanh(0.5 * p) + 0.5)).astype(BF16)
        left = kind == types_ref[2 * i : 2 * i + 1, :]
        right = (kind - 8) == types_ref[2 * i + 1 : 2 * i + 2, :]
        onehot = jnp.concatenate([left.astype(F32), right.astype(F32)], axis=1).astype(BF16)
        s_ref[i * 16 : (i + 1) * 16, :] = jnp.dot(onehot, act, preferred_element_type=F32)

    normalise(0)
    wload.wait()
    for i in range(NCHUNK):
        first_dot(i)
        if i + 1 < NCHUNK:
            normalise(i + 1)
        if i >= 1:
            activate(i - 1)
    activate(NCHUNK - 1)

    lanes16 = lax.broadcasted_iota(jnp.int32, (16, LANES), 1)
    subs16 = lax.broadcasted_iota(jnp.int32, (16, LANES), 0)
    diagonal = lanes16 == subs16
    net = jnp.sum(s_ref[...].reshape(ROWS, 8, D) * q_ref[...][None], axis=1)
    net = jnp.sum(net, axis=1, keepdims=True)
    net = jnp.concatenate([net, jnp.zeros((16 - ROWS, 1), F32)], axis=0)
    net = jnp.sum(jnp.where(diagonal, net, 0.0), axis=0, keepdims=True)
    mine_ref[...] = jnp.zeros_like(mine_ref)
    mine_ref[0:1, 0:ROWS] = band_ref[...].astype(F32)
    mine_ref[1:2, 0:ROWS] = target_ref[...]
    lane1 = lax.broadcasted_iota(jnp.int32, (1, LANES), 1)
    coslat = jnp.cos(math.pi * (mine_ref[0:1, :] / 720.0 - 0.5))
    coslat = jnp.where(lane1 < ROWS, coslat, 0.0)
    mine_ref[0:1, :] = coslat * net * (1.0 / (NLON * COLS))

    pl.semaphore_wait(barrier, (NLON - 1) + (NZ - 1) + (NY - 1))
    sent = []

    def launch(copy):
        copy.start()
        sent.append(copy)
        return copy

    ex1 = [
        launch(remote(mine_ref, ex1_ref.at[lon], ex1_s.at[k - 1], ex1_r.at[k - 1], lon=lax.rem(lon + k, NLON)))
        for k in range(1, NLON)
    ]
    ex1_ref[lon] = mine_ref[...]

    def unscaled(i):
        rows = chunk_rows(i)
        kinds = tcol_ref[rows, :]
        is_one = kinds == 1.0
        is_two = kinds == 2.0
        inner = jnp.zeros((CHUNK, LANES), F32)
        for tile in range(TILES):
            cols = slice(tile * LANES, (tile + 1) * LANES)
            before = v_ref[rows, cols]
            p = before + bias_ref[0:1, cols]
            sigma = 0.5 * jnp.tanh(0.5 * p) + 0.5
            slope = sigma + (p * sigma) * (1.0 - sigma)
            weight = jnp.where(is_one, q_ref[1:2, cols], jnp.where(is_two, q_ref[2:3, cols], q_ref[0:1, cols]))
            grad = slope * weight
            inner += grad * before
            b_ref[2 * i : 2 * i + 2, cols] = jnp.sum(grad.reshape(2, COLS, LANES), axis=1)
            u_ref[rows, cols] = grad.astype(BF16)
        inv = inv_ref[rows, :]
        inner = jnp.sum(inner, axis=1, keepdims=True)
        coef_ref[rows, :] = inv * inv * (inner * (1.0 / D))

    def turn(i):
        rows = chunk_rows(i)
        nt_ref[:, rows] = n_ref[rows, :].T

    for i in range(NCHUNK // 2):
        unscaled(i)
        turn(i)
    for copy in ex1:
        copy.wait_recv()
    line = ex1_ref[0]
    for k in range(1, NLON):
        line = line + ex1_ref[k]
    sub8 = lax.broadcasted_iota(jnp.int32, (8, LANES), 0)
    line_ref[...] = jnp.where(sub8 == 0, line, mine_ref[...])
    ex2 = [
        launch(remote(line_ref, ex2_ref.at[z], ex2_s.at[k - 1], ex2_r.at[k - 1], lat=lax.rem(z + k, NZ)))
        for k in range(1, NZ)
    ]
    ex2_ref[z] = line_ref[...]
    for i in range(NCHUNK // 2, NCHUNK):
        unscaled(i)
        turn(i)
    for copy in ex2:
        copy.wait_recv()

    lanes8 = lax.broadcasted_iota(jnp.int32, (8, LANES), 1)
    weighted = jnp.concatenate([ex2_ref[k][0:1, :] for k in range(NZ)], axis=0)
    targets = jnp.concatenate([ex2_ref[k][1:2, :] for k in range(NZ)], axis=0)
    above_lane = lax.broadcasted_iota(jnp.int32, (LANES, LANES), 0)
    here_lane = lax.broadcasted_iota(jnp.int32, (LANES, LANES), 1)
    upto = (above_lane <= here_lane).astype(F32)
    local = jnp.dot(weighted, upto, precision=HIGH, preferred_element_type=F32)
    totals = jnp.sum(weighted, axis=1, keepdims=True)
    before8 = (lax.broadcasted_iota(jnp.int32, (8, 8), 1) < lax.broadcasted_iota(jnp.int32, (8, 8), 0)).astype(F32)
    below = jnp.dot(before8, jnp.broadcast_to(totals, (8, LANES)), precision=HIGH, preferred_element_type=F32)
    misfit = jnp.where(lanes8 < ROWS, local + below - targets, 0.0)
    onward = (above_lane >= here_lane).astype(F32)
    from_here = jnp.dot(misfit, onward, precision=HIGH, preferred_element_type=F32)
    north = jnp.where(sub8 > z, jnp.sum(misfit, axis=1, keepdims=True), jnp.where(sub8 == z, from_here, 0.0))
    southward = jnp.sum(north, axis=0, keepdims=True)
    flux = coslat * southward * (1.0 / (ROWS * NZ))
    flux = jnp.sum(jnp.where(diagonal, flux, 0.0), axis=1, keepdims=True)
    fb_ref[...] = jnp.broadcast_to(flux, (16, LANES))

    for r in range(ROWS):
        rows = pl.ds(r * COLS, COLS)
        scale = fb_ref[r : r + 1, 0:1]
        u_ref[rows, :] = (u_ref[rows, :].astype(F32) * scale).astype(BF16)

    def hidden_tile(half, j):
        cols = pl.ds(pl.multiple_of(half * 512 + j * 256, 256), 256)
        tile = jnp.dot(nt_ref[...], u_ref[:, cols], preferred_element_type=F32)
        return tile.reshape(NY, NX, 64, 256)

    to_core = []
    for j in range(2):
        give_ref[j] = hidden_tile(1 - core, j)
        to_core.append(
            launch(remote(give_ref.at[j], take_ref.at[j], core_s.at[j], core_r.at[j], lon=x * 2 + 1 - core))
        )
    for j in range(2):
        own_ref[j] = hidden_tile(core, j)

    def place(j):
        return y if j == 0 else x

    def toward(j, step):
        if j == 0:
            return {"mem": lax.rem(y + step, NY)}
        return {"lon": lon_at(step)}

    def block(j, owner, half):
        rows = pl.ds(32 * half, 32)
        if j == 0:
            return own_ref.at[j, owner, :, rows, :]
        return own_ref.at[j, :, owner, rows, :]

    passes, plains, aggs = {}, {}, {}
    for j in range(2):
        to_core[j].wait_recv()
        own_ref[j] = own_ref[j] + take_ref[j]
        me = place(j)
        opposite = lax.rem(me + 2, 4)
        following, previous = lax.rem(me + 1, 4), lax.rem(me + 3, 4)
        passes[j, 0] = launch(
            remote(block(j, opposite, 0), pass_ref.at[j, 0], r4_s.at[j, 0], r4_r.at[j, 0], **toward(j, 1))
        )
        passes[j, 1] = launch(
            remote(block(j, opposite, 1), pass_ref.at[j, 1], r4_s.at[j, 1], r4_r.at[j, 1], **toward(j, 3))
        )
        plains[j, 1] = launch(
            remote(block(j, following, 1), plain_ref.at[j, 1], r4_s.at[j, 2], r4_r.at[j, 2], **toward(j, 1))
        )
        plains[j, 0] = launch(
            remote(block(j, previous, 0), plain_ref.at[j, 0], r4_s.at[j, 3], r4_r.at[j, 3], **toward(j, 3))
        )

    gacc_ref[...] = jnp.zeros_like(gacc_ref)
    stores = []

    def latent_grad(i):
        rows = chunk_rows(i)
        back = lax.dot_general(u_ref[rows, :], w1_ref[...], dims, preferred_element_type=F32)
        inv = inv_ref[rows, :]
        coef = coef_ref[rows, :]
        coef = jnp.concatenate(
            [coef[k * COLS : (k + 1) * COLS] * fb_ref[2 * i + k : 2 * i + k + 1, :] for k in range(2)], axis=0
        )
        for tile in range(TILES):
            cols = slice(tile * LANES, (tile + 1) * LANES)
            xf = x_ref[rows, cols].astype(F32)
            scaled = back[:, cols] * inv
            gacc_ref[:, cols] += jnp.sum((scaled * xf).reshape(CHUNK // 8, 8, LANES), axis=0)
            stage_ref[rows, cols] = (scaled * gain_ref[0:1, cols] - xf * coef).astype(BF16)
        store = pltpu.make_async_copy(stage_ref.at[rows], outlat_hbm.at[rows], osem.at[i])
        store.start()
        stores.append(store)

    for i in range(NCHUNK // 2):
        latent_grad(i)

    for j in range(2):
        me = place(j)
        for half, step in ((0, 1), (1, 3)):
            passes[j, half].wait_recv()
            mid = block(j, lax.rem(me + step, 4), half)
            mid[...] = mid[...] + pass_ref[j, half]
            aggs[j, half] = launch(
                remote(mid, agg_ref.at[j, half], r4_s.at[j, 4 + half], r4_r.at[j, 4 + half], **toward(j, step))
            )

    for i in range(NCHUNK // 2, NCHUNK):
        latent_grad(i)

    small = jnp.zeros((8, D), F32)
    bias_sum = jnp.zeros((1, D), F32)
    for r in range(ROWS):
        scale = fb_ref[r : r + 1, 0:1]
        small = small + s_ref[r * 8 : (r + 1) * 8, :] * scale
        bias_sum = bias_sum + b_ref[r : r + 1, :] * scale
    gain_sum = jnp.sum(gacc_ref[...], axis=0, keepdims=True)
    row8 = lax.broadcasted_iota(jnp.int32, (8, D), 0)
    small = jnp.where(row8 == 3, bias_sum, jnp.where(row8 == 4, gain_sum, small))
    for k in range(NLON):
        sm_ref[k] = small[:, k * LANES : (k + 1) * LANES]
    sm1 = []
    for k in range(1, NLON):
        peer = lax.rem(lon + k, NLON)
        sm1.append(launch(remote(sm_ref.at[peer], sm1_ref.at[lon], sm1_s.at[k - 1], sm1_r.at[k - 1], lon=peer)))
    sm1_ref[lon] = sm_ref[lon]

    crosses = []
    for j in range(2):
        for half in range(2):
            plains[j, half].wait_recv()
            aggs[j, half].wait_recv()
            kept = block(j, place(j), half)
            part_ref[j, :, 32 * half : 32 * (half + 1), :] = kept[...] + plain_ref[j, half] + agg_ref[j, half]
        other = 1 - j
        for k in range(1, 4):
            peer = lax.rem(place(other) + k, 4)
            crosses.append(
                launch(
                    remote(
                        part_ref.at[j, peer],
                        cross_ref.at[j, k - 1],
                        cross_s.at[j, k - 1],
                        cross_r.at[j, k - 1],
                        **toward(other, k),
                    )
                )
            )

    for copy in sm1:
        copy.wait_recv()
    total = sm1_ref[0]
    for k in range(1, NLON):
        total = total + sm1_ref[k]
    t1_ref[...] = total
    sm2 = [
        launch(remote(t1_ref, sm2_ref.at[z], sm2_s.at[k - 1], sm2_r.at[k - 1], lat=lax.rem(z + k, NZ)))
        for k in range(1, NZ)
    ]
    sm2_ref[z] = t1_ref[...]

    depths = []
    for j in range(2):
        for k in range(3):
            crosses[3 * j + k].wait_recv()
        piece = part_ref[j, place(1 - j)] + cross_ref[j, 0] + cross_ref[j, 1] + cross_ref[j, 2]
        piece_ref[j] = piece.reshape(NZ, 8, 256)
        for k in range(1, NZ):
            peer = lax.rem(z + k, NZ)
            depths.append(
                launch(
                    remote(
                        piece_ref.at[j, peer],
                        depth_ref.at[j, k - 1],
                        depth_s.at[j, k - 1],
                        depth_r.at[j, k - 1],
                        lat=peer,
                    )
                )
            )

    for copy in sm2:
        copy.wait_recv()
    total = sm2_ref[0]
    for k in range(1, NZ):
        total = total + sm2_ref[k]
    t2_ref[...] = total
    sm3 = [
        launch(remote(t2_ref, sm3_ref.at[y], sm3_s.at[k - 1], sm3_r.at[k - 1], mem=lax.rem(y + k, NY)))
        for k in range(1, NY)
    ]
    sm3_ref[y] = t2_ref[...]

    agz = []
    for j in range(2):
        for k in range(NZ - 1):
            depths[(NZ - 1) * j + k].wait_recv()
        piece = piece_ref[j, z]
        for k in range(NZ - 1):
            piece = piece + depth_ref[j, k]
        rows = pl.ds(pl.multiple_of(x * 64 + z * 8, 8), 8)
        hid_ref[core, j, rows, :] = piece
        spot = hid_ref.at[core, j, rows, :]
        for k in range(1, NZ):
            agz.append(
                launch(remote(spot, spot, agz_s.at[j, k - 1], agz_r.at[j, k - 1], lat=lax.rem(z + k, NZ)))
            )

    for copy in sm3:
        copy.wait_recv()
    total = sm3_ref[0]
    for k in range(1, NY):
        total = total + sm3_ref[k]
    smo_ref[lon] = total
    sm4 = [
        launch(remote(smo_ref.at[lon], smo_ref.at[lon], sm4_s.at[k - 1], sm4_r.at[k - 1], lon=lax.rem(lon + k, NLON)))
        for k in range(1, NLON)
    ]

    def span(step, half):
        start = lax.rem(x + step, NX) * 64
        if half is None:
            return hid_ref.at[core, :, pl.ds(pl.multiple_of(start, 64), 64), :]
        return hid_ref.at[core, :, pl.ds(pl.multiple_of(start + 32 * half, 32), 32), :]

    sibling = x * 2 + 1 - core
    for copy in agz:
        copy.wait_recv()
    right = launch(remote(span(0, None), span(0, None), agx_s.at[0], agx_r.at[0], lon=lon_at(1)))
    left = launch(remote(span(0, None), span(0, None), agx_s.at[1], agx_r.at[1], lon=lon_at(3)))
    agc = [launch(remote(span(0, None), span(0, None), agc_s.at[0], agc_r.at[0], lon=sibling))]
    right.wait_recv()
    on_right = launch(remote(span(3, 0), span(3, 0), agx_s.at[2], agx_r.at[2], lon=lon_at(1)))
    agc.append(launch(remote(span(3, None), span(3, None), agc_s.at[1], agc_r.at[1], lon=sibling)))
    left.wait_recv()
    on_left = launch(remote(span(1, 1), span(1, 1), agx_s.at[3], agx_r.at[3], lon=lon_at(3)))
    agc.append(launch(remote(span(1, None), span(1, None), agc_s.at[2], agc_r.at[2], lon=sibling)))

    for copy in sm4:
        copy.wait_recv()
    for k in range(NLON):
        cols = slice(k * LANES, (k + 1) * LANES)
        outbias_ref[0:1, cols] = smo_ref[k][3:4, :]
        outgain_ref[0:1, cols] = smo_ref[k][4:5, :]
        outw_ref[cols, :] = lax.dot_general(
            smo_ref[k], tab_ref[...], (((0,), (0,)), ((), ())), precision=HIGH, preferred_element_type=F32
        )

    on_right.wait_recv()
    agc.append(launch(remote(span(2, 0), span(2, 0), agc_s.at[3], agc_r.at[3], lon=sibling)))
    on_left.wait_recv()
    agc.append(launch(remote(span(2, 1), span(2, 1), agc_s.at[4], agc_r.at[4], lon=sibling)))
    for copy in agc:
        copy.wait_recv()
    out = []
    for half in range(2):
        for j in range(2):
            cols = pl.ds(half * 512 + j * 256, 256)
            copy = pltpu.make_async_copy(hid_ref.at[half, j], outhid_hbm.at[:, cols], hsem.at[half, j])
            copy.start()
            out.append(copy)
    for copy in sent:
        copy.wait_send()
    for copy in stores:
        copy.wait()
    for copy in out:
        copy.wait()


def on_device(latent, norm_gain, hidden_weight, hidden_bias, output_weight, flux_table, target, land_sea, band_index):
    vmem = pl.BlockSpec(memory_space=pltpu.VMEM)
    hbm = pl.BlockSpec(memory_space=pl.ANY)
    dma = pltpu.SemaphoreType.DMA
    scratch = [
        pltpu.VMEM((CELLS, D), BF16),
        pltpu.VMEM((D, D), BF16),
        pltpu.VMEM((CELLS, D), BF16),
        pltpu.VMEM((D, CELLS), BF16),
        pltpu.VMEM((CELLS, D), F32),
        pltpu.VMEM((CELLS, D), BF16),
        pltpu.VMEM((CELLS, LANES), F32),
        pltpu.VMEM((CELLS, LANES), F32),
        pltpu.VMEM((CELLS, LANES), F32),
        pltpu.VMEM((LANES, LANES), F32),
        pltpu.VMEM((8, D), F32),
        pltpu.VMEM((8, 80), F32),
        pltpu.VMEM((ROWS * 8, D), F32),
        pltpu.VMEM((16, D), F32),
        pltpu.VMEM((16, LANES), F32),
        pltpu.VMEM((8, D), F32),
        pltpu.VMEM((CELLS, D), BF16),
        pltpu.VMEM((8, LANES), F32),
        pltpu.VMEM((NLON, 8, LANES), F32),
        pltpu.VMEM((8, LANES), F32),
        pltpu.VMEM((NZ, 8, LANES), F32),
        pltpu.VMEM((2, NY, NX, 64, 256), F32),
        pltpu.VMEM((2, NY, NX, 64, 256), F32),
        pltpu.VMEM((2, NY, NX, 64, 256), F32),
        pltpu.VMEM((2, 2, 4, 32, 256), F32),
        pltpu.VMEM((2, 2, 4, 32, 256), F32),
        pltpu.VMEM((2, 2, 4, 32, 256), F32),
        pltpu.VMEM((2, 4, 64, 256), F32),
        pltpu.VMEM((2, 3, 64, 256), F32),
        pltpu.VMEM((2, NZ, 8, 256), F32),
        pltpu.VMEM((2, NZ - 1, 8, 256), F32),
        pltpu.VMEM((2, 2, 256, 256), F32),
        pltpu.VMEM((NLON, 8, LANES), F32),
        pltpu.VMEM((NLON, 8, LANES), F32),
        pltpu.VMEM((8, LANES), F32),
        pltpu.VMEM((NZ, 8, LANES), F32),
        pltpu.VMEM((8, LANES), F32),
        pltpu.VMEM((NY, 8, LANES), F32),
        pltpu.VMEM((NLON, 8, LANES), F32),
        dma((NCHUNK,)),
        dma,
        dma((NCHUNK,)),
        dma((2, 2)),
        dma((7,)), dma((7,)),
        dma((7,)), dma((7,)),
        dma((2,)), dma((2,)),
        dma((2, 6)), dma((2, 6)),
        dma((2, 3)), dma((2, 3)),
        dma((2, 7)), dma((2, 7)),
        dma((2, 7)), dma((2, 7)),
        dma((4,)), dma((4,)),
        dma((5,)), dma((5,)),
        dma((7,)), dma((7,)),
        dma((7,)), dma((7,)),
        dma((3,)), dma((3,)),
        dma((7,)), dma((7,)),
    ]
    grad_cells, grad_hidden, grad_out, grad_gain, grad_bias = pl.pallas_call(
        kernel,
        out_shape=(
            jax.ShapeDtypeStruct((CELLS, D), BF16),
            jax.ShapeDtypeStruct((D // NY, D), F32),
            jax.ShapeDtypeStruct((D, 80), F32),
            jax.ShapeDtypeStruct((1, D), F32),
            jax.ShapeDtypeStruct((1, D), F32),
        ),
        in_specs=[hbm, vmem, hbm, vmem, vmem, vmem, vmem, vmem, vmem],
        out_specs=(hbm, hbm, vmem, vmem, vmem),
        scratch_shapes=scratch,
        compiler_params=pltpu.CompilerParams(
            collective_id=0, has_side_effects=True, vmem_limit_bytes=60 * 1024 * 1024
        ),
        cost_estimate=pl.CostEstimate(flops=10_000_000_000, bytes_accessed=9_000_000, transcendentals=3_000_000),
    )(
        latent.reshape(CELLS, D),
        norm_gain.reshape(1, D),
        hidden_weight,
        hidden_bias.reshape(1, D),
        output_weight,
        flux_table,
        target,
        land_sea,
        band_index.reshape(1, ROWS),
    )
    return (
        grad_cells.reshape(latent.shape),
        grad_hidden,
        grad_out,
        grad_gain.reshape(D),
        grad_bias.reshape(D),
    )


def solution(mesh):
    return jax.shard_map(
        on_device,
        mesh=mesh,
        in_specs=(
            P("mem", "lat", "lon", None),
            P(),
            P(),
            P(),
            P(),
            P(),
            P("mem", "lat"),
            P("lat", "lon"),
            P("lat"),
        ),
        out_specs=(P("mem", "lat", "lon", None), P("mem", None), P(), P(), P()),
        check_vma=False,
    )
```

```python
import functools
import math

import jax
import jax.numpy as jnp
from jax import lax
from jax.experimental import pallas as pl
from jax.experimental.pallas import tpu as pltpu
from jax.sharding import PartitionSpec as P

MESH = pl.DeviceIdType.MESH
F32 = jnp.float32
BF16 = jnp.bfloat16
HIGH = lax.Precision.HIGHEST

CELLS = 1536
ROWS = 12
COLS = 128
D = 1024
CHUNK = 256
NCHUNK = CELLS // CHUNK
LANES = 128
TILES = D // LANES
NX, NY, NZ, NLON = 4, 4, 8, 8


def remote(src, dst, send_sem, recv_sem, **where):
    return pltpu.make_async_remote_copy(
        src_ref=src,
        dst_ref=dst,
        send_sem=send_sem,
        recv_sem=recv_sem,
        device_id=where,
        device_id_type=MESH,
    )


def kernel(
    lat_hbm, gain_ref, w1_hbm, bias_ref, w2_ref, table_ref, target_ref, types_ref, band_ref,
    outlat_ref, outhid_ref, outw_ref, outgain_ref, outbias_ref,
    x_ref, w1_ref, n_ref, nt_ref, v_ref, u_ref, inv_ref, coef_ref, tcol_ref, square_ref,
    q_ref, tab_ref, s_ref, b_ref, fb_ref, gacc_ref,
    mine_ref, ex1_ref, line_ref, ex2_ref,
    give_ref, take_ref, own_ref, first_ref, part_ref, cross_ref, piece_ref, depth_ref,
    hid_ref, sm_ref, sm1_ref, t1_ref, sm2_ref, t2_ref, sm3_ref, smo_ref,
    xsem, wsem,
    ex1_s, ex1_r, ex2_s, ex2_r, core_s, core_r, first_s, first_r, cross_s, cross_r, depth_s, depth_r,
    agz_s, agz_r, agx_s, agx_r, agc_s, agc_r, sm1_s, sm1_r, sm2_s, sm2_r, sm3_s, sm3_r, sm4_s, sm4_r,
):
    z = lax.axis_index("lat")
    lon = lax.axis_index("lon")
    y = lax.axis_index("mem")
    x = lon // 2
    core = lon % 2

    def lon_at(step):
        return lax.rem(x + step, NX) * 2 + core

    def chunk_rows(i):
        return pl.ds(i * CHUNK, CHUNK)

    loads = [pltpu.make_async_copy(lat_hbm.at[chunk_rows(i)], x_ref.at[chunk_rows(i)], xsem.at[i]) for i in range(NCHUNK)]
    wload = pltpu.make_async_copy(w1_hbm, w1_ref, wsem)
    loads[0].start()
    wload.start()
    for i in range(1, NCHUNK):
        loads[i].start()

    barrier = pltpu.get_barrier_semaphore()
    for k in range(1, NLON):
        pl.semaphore_signal(barrier, inc=1, device_id={"lon": lax.rem(lon + k, NLON)}, device_id_type=MESH)
    for k in range(1, NZ):
        pl.semaphore_signal(barrier, inc=1, device_id={"lat": lax.rem(z + k, NZ)}, device_id_type=MESH)
    for k in range(1, NY):
        pl.semaphore_signal(barrier, inc=1, device_id={"mem": lax.rem(y + k, NY)}, device_id_type=MESH)

    tab_ref[...] = jnp.zeros_like(tab_ref)
    tab_ref[0:3, :] = table_ref[...]
    table = tab_ref[...]
    high = table.astype(BF16)
    rest = table - high.astype(F32)
    middle = rest.astype(BF16)
    w2 = w2_ref[...]
    dims = (((1,), (0,)), ((), ()))
    q_ref[...] = lax.dot_general(high, w2, dims, preferred_element_type=F32) + lax.dot_general(
        middle, w2, dims, preferred_element_type=F32
    )
    square_ref[...] = jnp.zeros_like(square_ref)
    square_ref[0:ROWS, :] = types_ref[...].astype(F32)
    turned = square_ref[...].T
    for r in range(ROWS):
        tcol_ref[r * COLS : (r + 1) * COLS, :] = jnp.broadcast_to(turned[:, r : r + 1], (COLS, LANES))

    gain = gain_ref[...]
    bias = bias_ref[...]

    def normalise(i):
        rows = chunk_rows(i)
        loads[i].wait()
        xf = x_ref[rows, :].astype(F32)
        inv = lax.rsqrt(jnp.mean(xf * xf, axis=-1, keepdims=True) + 1e-05)
        inv_ref[rows, :] = jnp.broadcast_to(inv, (CHUNK, LANES))
        n_ref[rows, :] = (xf * inv * gain).astype(BF16)

    def first_dot(i):
        rows = chunk_rows(i)
        v_ref[rows, :] = jnp.dot(n_ref[rows, :], w1_ref[...], preferred_element_type=F32)

    kind = lax.broadcasted_iota(jnp.int32, (16, COLS), 0)

    def activate(i):
        rows = chunk_rows(i)
        p = v_ref[rows, :] + bias
        act = (p * (0.5 * jnp.tanh(0.5 * p) + 0.5)).astype(BF16)
        left = kind == types_ref[2 * i : 2 * i + 1, :]
        right = (kind - 8) == types_ref[2 * i + 1 : 2 * i + 2, :]
        onehot = jnp.concatenate([left.astype(F32), right.astype(F32)], axis=1).astype(BF16)
        s_ref[i * 16 : (i + 1) * 16, :] = jnp.dot(onehot, act, preferred_element_type=F32)

    normalise(0)
    wload.wait()
    for i in range(NCHUNK):
        first_dot(i)
        if i + 1 < NCHUNK:
            normalise(i + 1)
        if i >= 1:
            activate(i - 1)
    activate(NCHUNK - 1)

    lanes16 = lax.broadcasted_iota(jnp.int32, (16, LANES), 1)
    subs16 = lax.broadcasted_iota(jnp.int32, (16, LANES), 0)
    diagonal = lanes16 == subs16
    net = jnp.sum(s_ref[...].reshape(ROWS, 8, D) * q_ref[...][None], axis=1)
    net = jnp.sum(net, axis=1, keepdims=True)
    net = jnp.concatenate([net, jnp.zeros((16 - ROWS, 1), F32)], axis=0)
    net = jnp.sum(jnp.where(diagonal, net, 0.0), axis=0, keepdims=True)
    mine_ref[...] = jnp.zeros_like(mine_ref)
    mine_ref[0:1, 0:ROWS] = band_ref[...].astype(F32)
    mine_ref[1:2, 0:ROWS] = target_ref[...]
    lane1 = lax.broadcasted_iota(jnp.int32, (1, LANES), 1)
    coslat = jnp.cos(math.pi * (mine_ref[0:1, :] / 720.0 - 0.5))
    coslat = jnp.where(lane1 < ROWS, coslat, 0.0)
    mine_ref[0:1, :] = coslat * net * (1.0 / (NLON * COLS))

    pl.semaphore_wait(barrier, (NLON - 1) + (NZ - 1) + (NY - 1))
    sent = []

    def launch(copy):
        copy.start()
        sent.append(copy)
        return copy

    ex1 = [
        launch(remote(mine_ref, ex1_ref.at[lon], ex1_s.at[k - 1], ex1_r.at[k - 1], lon=lax.rem(lon + k, NLON)))
        for k in range(1, NLON)
    ]
    ex1_ref[lon] = mine_ref[...]

    def unscaled(i):
        rows = chunk_rows(i)
        kinds = tcol_ref[rows, :]
        is_one = kinds == 1.0
        is_two = kinds == 2.0
        inner = jnp.zeros((CHUNK, LANES), F32)
        for tile in range(TILES):
            cols = slice(tile * LANES, (tile + 1) * LANES)
            before = v_ref[rows, cols]
            p = before + bias_ref[0:1, cols]
            sigma = 0.5 * jnp.tanh(0.5 * p) + 0.5
            slope = sigma + (p * sigma) * (1.0 - sigma)
            weight = jnp.where(is_one, q_ref[1:2, cols], jnp.where(is_two, q_ref[2:3, cols], q_ref[0:1, cols]))
            grad = slope * weight
            inner += grad * before
            b_ref[2 * i : 2 * i + 2, cols] = jnp.sum(grad.reshape(2, COLS, LANES), axis=1)
            u_ref[rows, cols] = grad.astype(BF16)
        inv = inv_ref[rows, :]
        inner = jnp.sum(inner, axis=1, keepdims=True)
        coef_ref[rows, :] = inv * inv * (inner * (1.0 / D))

    def turn(i):
        rows = chunk_rows(i)
        nt_ref[:, rows] = n_ref[rows, :].T

    for i in range(NCHUNK // 2):
        unscaled(i)
        turn(i)
    for copy in ex1:
        copy.wait_recv()
    line = ex1_ref[0]
    for k in range(1, NLON):
        line = line + ex1_ref[k]
    sub8 = lax.broadcasted_iota(jnp.int32, (8, LANES), 0)
    line_ref[...] = jnp.where(sub8 == 0, line, mine_ref[...])
    ex2 = [
        launch(remote(line_ref, ex2_ref.at[z], ex2_s.at[k - 1], ex2_r.at[k - 1], lat=lax.rem(z + k, NZ)))
        for k in range(1, NZ)
    ]
    ex2_ref[z] = line_ref[...]
    for i in range(NCHUNK // 2, NCHUNK):
        unscaled(i)
        turn(i)
    for copy in ex2:
        copy.wait_recv()

    lanes8 = lax.broadcasted_iota(jnp.int32, (8, LANES), 1)
    weighted = jnp.concatenate([ex2_ref[k][0:1, :] for k in range(NZ)], axis=0)
    targets = jnp.concatenate([ex2_ref[k][1:2, :] for k in range(NZ)], axis=0)
    above_lane = lax.broadcasted_iota(jnp.int32, (LANES, LANES), 0)
    here_lane = lax.broadcasted_iota(jnp.int32, (LANES, LANES), 1)
    upto = (above_lane <= here_lane).astype(F32)
    local = jnp.dot(weighted, upto, precision=HIGH, preferred_element_type=F32)
    totals = jnp.sum(weighted, axis=1, keepdims=True)
    before8 = (lax.broadcasted_iota(jnp.int32, (8, 8), 1) < lax.broadcasted_iota(jnp.int32, (8, 8), 0)).astype(F32)
    below = jnp.dot(before8, jnp.broadcast_to(totals, (8, LANES)), precision=HIGH, preferred_element_type=F32)
    misfit = jnp.where(lanes8 < ROWS, local + below - targets, 0.0)
    onward = (above_lane >= here_lane).astype(F32)
    from_here = jnp.dot(misfit, onward, precision=HIGH, preferred_element_type=F32)
    north = jnp.where(sub8 > z, jnp.sum(misfit, axis=1, keepdims=True), jnp.where(sub8 == z, from_here, 0.0))
    southward = jnp.sum(north, axis=0, keepdims=True)
    flux = coslat * southward * (1.0 / (ROWS * NZ))
    flux = jnp.sum(jnp.where(diagonal, flux, 0.0), axis=1, keepdims=True)
    fb_ref[...] = jnp.broadcast_to(flux, (16, LANES))

    for r in range(ROWS):
        rows = pl.ds(r * COLS, COLS)
        scale = fb_ref[r : r + 1, 0:1]
        u_ref[rows, :] = (u_ref[rows, :].astype(F32) * scale).astype(BF16)

    def hidden_tile(ref, half, t):
        cols = pl.ds(pl.multiple_of(half * 512 + t * 256, 256), 256)
        tile = jnp.dot(nt_ref[...], u_ref[:, cols], preferred_element_type=F32)
        for way in range(2):
            ref[t, way] = tile[:, way * LANES : (way + 1) * LANES].reshape(NY, NX, 64, LANES)

    sibling = x * 2 + 1 - core

    to_core = []
    for t in range(2):
        hidden_tile(give_ref, 1 - core, t)
        to_core.append(launch(remote(give_ref.at[t], take_ref.at[t], core_s.at[t], core_r.at[t], lon=sibling)))
    for t in range(2):
        hidden_tile(own_ref, core, t)

    def place(way):
        return y if way == 0 else x

    def toward(way, step):
        if way == 0:
            return {"mem": lax.rem(y + step, NY)}
        return {"lon": lon_at(step)}

    def share(t, way, owner):
        return own_ref.at[t, way, owner] if way == 0 else own_ref.at[t, way, :, owner]

    firsts = {}
    for t in range(2):
        to_core[t].wait_recv()
        own_ref[t] = own_ref[t] + take_ref[t]
        for way in range(2):
            for k in (2, 1, 3):
                firsts[t, way, k] = launch(
                    remote(
                        share(t, way, lax.rem(place(way) + k, 4)),
                        first_ref.at[t, way, k - 1],
                        first_s.at[t, way, k - 1],
                        first_r.at[t, way, k - 1],
                        **toward(way, k),
                    )
                )

    gacc_ref[...] = jnp.zeros_like(gacc_ref)

    def latent_grad(i):
        rows = chunk_rows(i)
        back = lax.dot_general(
            u_ref[rows, :], w1_ref[...], (((1,), (1,)), ((), ())), preferred_element_type=F32
        )
        inv = inv_ref[rows, :]
        coef = coef_ref[rows, :]
        coef = jnp.concatenate(
            [coef[k * COLS : (k + 1) * COLS] * fb_ref[2 * i + k : 2 * i + k + 1, :] for k in range(2)], axis=0
        )
        for tile in range(TILES):
            cols = slice(tile * LANES, (tile + 1) * LANES)
            xf = x_ref[rows, cols].astype(F32)
            scaled = back[:, cols] * inv
            gacc_ref[:, cols] += jnp.sum((scaled * xf).reshape(CHUNK // 8, 8, LANES), axis=0)
            outlat_ref[rows, cols] = (scaled * gain_ref[0:1, cols] - xf * coef).astype(BF16)

    for i in range(NCHUNK):
        latent_grad(i)

    small = jnp.zeros((8, D), F32)
    bias_sum = jnp.zeros((1, D), F32)
    for r in range(ROWS):
        scale = fb_ref[r : r + 1, 0:1]
        small = small + s_ref[r * 8 : (r + 1) * 8, :] * scale
        bias_sum = bias_sum + b_ref[r : r + 1, :] * scale
    gain_sum = jnp.sum(gacc_ref[...], axis=0, keepdims=True)
    row8 = lax.broadcasted_iota(jnp.int32, (8, D), 0)
    small = jnp.where(row8 == 3, bias_sum, jnp.where(row8 == 4, gain_sum, small))
    for k in range(NLON):
        sm_ref[k] = small[:, k * LANES : (k + 1) * LANES]
    sm1 = []
    for k in range(1, NLON):
        peer = lax.rem(lon + k, NLON)
        sm1.append(launch(remote(sm_ref.at[peer], sm1_ref.at[lon], sm1_s.at[k - 1], sm1_r.at[k - 1], lon=peer)))
    sm1_ref[lon] = sm_ref[lon]

    crosses, depths, agz = {}, {}, {}

    def cross(t):
        for way in range(2):
            for k in range(1, 4):
                firsts[t, way, k].wait_recv()
            part_ref[t, way] = (
                share(t, way, place(way))[...] + first_ref[t, way, 0] + first_ref[t, way, 1] + first_ref[t, way, 2]
            )
            other = 1 - way
            for k in (2, 1, 3):
                crosses[t, way, k] = launch(
                    remote(
                        part_ref.at[t, way, lax.rem(place(other) + k, 4)],
                        cross_ref.at[t, way, k - 1],
                        cross_s.at[t, way, k - 1],
                        cross_r.at[t, way, k - 1],
                        **toward(other, k),
                    )
                )

    by_distance = (4, 3, 5, 2, 6, 1, 7)

    def deepen(t):
        for way in range(2):
            for k in range(1, 4):
                crosses[t, way, k].wait_recv()
            piece = part_ref[t, way, place(1 - way)] + cross_ref[t, way, 0] + cross_ref[t, way, 1] + cross_ref[t, way, 2]
            piece_ref[t, :, way] = piece.reshape(NZ, 8, LANES)
        for k in by_distance:
            peer = lax.rem(z + k, NZ)
            depths[t, k] = launch(
                remote(
                    piece_ref.at[t, peer], depth_ref.at[t, k - 1], depth_s.at[t, k - 1], depth_r.at[t, k - 1], lat=peer
                )
            )

    slots = (0, 1, 7, 2, 6, 3, 5, 4)
    slot_of = {k: slots.index(k) for k in range(NZ)}

    def finish(t):
        for k in range(1, NZ):
            depths[t, k].wait_recv()
        piece = piece_ref[t, z]
        for k in range(NZ - 1):
            piece = piece + depth_ref[t, k]
        hid_ref[core, t, x, 0] = piece
        for k in by_distance:
            agz[t, k] = launch(
                remote(
                    hid_ref.at[core, t, x, 0],
                    hid_ref.at[core, t, x, slot_of[NZ - k]],
                    agz_s.at[t, k - 1],
                    agz_r.at[t, k - 1],
                    lat=lax.rem(z + k, NZ),
                )
            )

    groups = (slice(0, 5), slice(5, 8))
    agx, agc = {}, {}

    def spread(t, g):
        part = groups[g]
        for k in range(1, NZ):
            if part.start <= slot_of[NZ - k] < part.stop:
                agz[t, k].wait_recv()
        many = pl.ds(part.start, part.stop - part.start)
        spot = hid_ref.at[core, t, x, many]
        for k in (2, 1, 3):
            agx[t, g, k] = launch(
                remote(spot, spot, agx_s.at[t, g, k - 1], agx_r.at[t, g, k - 1], lon=lon_at(k))
            )
        agc[t, g, 0] = launch(remote(spot, spot, agc_s.at[t, g, 0], agc_r.at[t, g, 0], lon=sibling))

    def to_sibling(t, g):
        part = groups[g]
        many = pl.ds(part.start, part.stop - part.start)
        for k in (1, 3, 2):
            agx[t, g, k].wait_recv()
            spot = hid_ref.at[core, t, lax.rem(x + 4 - k, NX), many]
            agc[t, g, k] = launch(remote(spot, spot, agc_s.at[t, g, k], agc_r.at[t, g, k], lon=sibling))

    def place_rows(half, t):
        for xi in range(NX):
            for k in range(NZ):
                rows = pl.ds(pl.multiple_of(xi * 64 + lax.rem(z + k, NZ) * 8, 8), 8)
                for way in range(2):
                    cols = pl.ds(pl.multiple_of(half * 512 + t * 256 + way * LANES, LANES), LANES)
                    outhid_ref[rows, cols] = hid_ref[half, t, xi, slot_of[k], way]

    cross(0)
    for copy in sm1:
        copy.wait_recv()
    total = sm1_ref[0]
    for k in range(1, NLON):
        total = total + sm1_ref[k]
    t1_ref[...] = total
    sm2 = [
        launch(remote(t1_ref, sm2_ref.at[z], sm2_s.at[k - 1], sm2_r.at[k - 1], lat=lax.rem(z + k, NZ)))
        for k in by_distance
    ]
    sm2_ref[z] = t1_ref[...]
    deepen(0)
    cross(1)
    deepen(1)
    for copy in sm2:
        copy.wait_recv()
    total = sm2_ref[0]
    for k in range(1, NZ):
        total = total + sm2_ref[k]
    t2_ref[...] = total
    sm3 = [
        launch(remote(t2_ref, sm3_ref.at[y], sm3_s.at[k - 1], sm3_r.at[k - 1], mem=lax.rem(y + k, NY)))
        for k in range(1, NY)
    ]
    sm3_ref[y] = t2_ref[...]
    finish(0)
    for copy in sm3:
        copy.wait_recv()
    total = sm3_ref[0]
    for k in range(1, NY):
        total = total + sm3_ref[k]
    smo_ref[lon] = total
    sm4 = [
        launch(remote(smo_ref.at[lon], smo_ref.at[lon], sm4_s.at[k - 1], sm4_r.at[k - 1], lon=lax.rem(lon + k, NLON)))
        for k in range(1, NLON)
    ]
    finish(1)
    spread(0, 0)
    spread(0, 1)
    for copy in sm4:
        copy.wait_recv()
    for k in range(NLON):
        cols = slice(k * LANES, (k + 1) * LANES)
        outbias_ref[0:1, cols] = smo_ref[k][3:4, :]
        outgain_ref[0:1, cols] = smo_ref[k][4:5, :]
        outw_ref[:, cols] = lax.dot_general(
            tab_ref[...], smo_ref[k], (((0,), (0,)), ((), ())), precision=HIGH, preferred_element_type=F32
        )
    to_sibling(0, 0)
    to_sibling(0, 1)
    spread(1, 0)
    spread(1, 1)
    place_rows(core, 0)
    to_sibling(1, 0)
    to_sibling(1, 1)
    for g in range(2):
        for k in range(4):
            agc[0, g, k].wait_recv()
    place_rows(1 - core, 0)
    place_rows(core, 1)
    for copy in sent:
        copy.wait_send()
    for g in range(2):
        for k in range(4):
            agc[1, g, k].wait_recv()
    place_rows(1 - core, 1)


def write_out(*refs):
    sems = refs[-1]
    half = len(refs) // 2
    copies = [pltpu.make_async_copy(refs[i], refs[half + i], sems.at[i]) for i in range(half)]
    for copy in copies:
        copy.start()
    for copy in copies:
        copy.wait()


def on_device(latent, norm_gain, hidden_weight, hidden_bias, output_weight, flux_table, target, land_sea, band_index):
    vmem = pl.BlockSpec(memory_space=pltpu.VMEM)
    hbm = pl.BlockSpec(memory_space=pl.ANY)
    dma = pltpu.SemaphoreType.DMA
    scratch = [
        pltpu.VMEM((CELLS, D), BF16),
        pltpu.VMEM((D, D), BF16),
        pltpu.VMEM((CELLS, D), BF16),
        pltpu.VMEM((D, CELLS), BF16),
        pltpu.VMEM((CELLS, D), F32),
        pltpu.VMEM((CELLS, D), BF16),
        pltpu.VMEM((CELLS, LANES), F32),
        pltpu.VMEM((CELLS, LANES), F32),
        pltpu.VMEM((CELLS, LANES), F32),
        pltpu.VMEM((LANES, LANES), F32),
        pltpu.VMEM((8, D), F32),
        pltpu.VMEM((8, 80), F32),
        pltpu.VMEM((ROWS * 8, D), F32),
        pltpu.VMEM((16, D), F32),
        pltpu.VMEM((16, LANES), F32),
        pltpu.VMEM((8, D), F32),
        pltpu.VMEM((8, LANES), F32),
        pltpu.VMEM((NLON, 8, LANES), F32),
        pltpu.VMEM((8, LANES), F32),
        pltpu.VMEM((NZ, 8, LANES), F32),
        pltpu.VMEM((2, 2, NY, NX, 64, LANES), F32),
        pltpu.VMEM((2, 2, NY, NX, 64, LANES), F32),
        pltpu.VMEM((2, 2, NY, NX, 64, LANES), F32),
        pltpu.VMEM((2, 2, 3, 4, 64, LANES), F32),
        pltpu.VMEM((2, 2, 4, 64, LANES), F32),
        pltpu.VMEM((2, 2, 3, 64, LANES), F32),
        pltpu.VMEM((2, NZ, 2, 8, LANES), F32),
        pltpu.VMEM((2, NZ - 1, 2, 8, LANES), F32),
        pltpu.VMEM((2, 2, NX, NZ, 2, 8, LANES), F32),
        pltpu.VMEM((NLON, 8, LANES), F32),
        pltpu.VMEM((NLON, 8, LANES), F32),
        pltpu.VMEM((8, LANES), F32),
        pltpu.VMEM((NZ, 8, LANES), F32),
        pltpu.VMEM((8, LANES), F32),
        pltpu.VMEM((NY, 8, LANES), F32),
        pltpu.VMEM((NLON, 8, LANES), F32),
        dma((NCHUNK,)),
        dma,
        dma((7,)), dma((7,)),
        dma((7,)), dma((7,)),
        dma((2,)), dma((2,)),
        dma((2, 2, 3)), dma((2, 2, 3)),
        dma((2, 2, 3)), dma((2, 2, 3)),
        dma((2, 7)), dma((2, 7)),
        dma((2, 7)), dma((2, 7)),
        dma((2, 2, 3)), dma((2, 2, 3)),
        dma((2, 2, 4)), dma((2, 2, 4)),
        dma((7,)), dma((7,)),
        dma((7,)), dma((7,)),
        dma((3,)), dma((3,)),
        dma((7,)), dma((7,)),
    ]
    shapes = (((CELLS, D), BF16), ((D // NY, D), F32), ((80, D), F32), ((1, D), F32), ((1, D), F32))
    held = pl.pallas_call(
        kernel,
        out_shape=tuple(pltpu.VMEM(*shape) for shape in shapes),
        in_specs=[hbm, vmem, hbm, vmem, vmem, vmem, vmem, vmem, vmem],
        out_specs=(vmem,) * 5,
        scratch_shapes=scratch,
        compiler_params=pltpu.CompilerParams(
            collective_id=0, has_side_effects=True, vmem_limit_bytes=56 * 1024 * 1024
        ),
        cost_estimate=pl.CostEstimate(flops=10_000_000_000, bytes_accessed=9_000_000, transcendentals=3_000_000),
    )(
        latent.reshape(CELLS, D),
        norm_gain.reshape(1, D),
        hidden_weight,
        hidden_bias.reshape(1, D),
        output_weight.T,
        flux_table,
        target,
        land_sea,
        band_index.reshape(1, ROWS),
    )
    grad_cells, grad_hidden, grad_out, grad_gain, grad_bias = pl.pallas_call(
        write_out,
        out_shape=tuple(jax.ShapeDtypeStruct(*shape) for shape in shapes),
        in_specs=[vmem] * 5,
        out_specs=(hbm,) * 5,
        scratch_shapes=[dma((5,))],
        compiler_params=pltpu.CompilerParams(vmem_limit_bytes=1024 * 1024),
    )(*[pltpu.with_memory_space_constraint(array, pltpu.VMEM) for array in held])
    return (
        grad_cells.reshape(latent.shape),
        grad_hidden,
        grad_out.T,
        grad_gain.reshape(D),
        grad_bias.reshape(D),
    )


def solution(mesh):
    return jax.shard_map(
        on_device,
        mesh=mesh,
        in_specs=(
            P("mem", "lat", "lon", None),
            P(),
            P(),
            P(),
            P(),
            P(),
            P("mem", "lat"),
            P("lat", "lon"),
            P("lat"),
        ),
        out_specs=(P("mem", "lat", "lon", None), P("mem", None), P(), P(), P()),
        check_vma=False,
    )
```

```python
import functools
import math

import jax
import jax.numpy as jnp
from jax import lax
from jax.experimental import pallas as pl
from jax.experimental.pallas import tpu as pltpu
from jax.sharding import PartitionSpec as P

MESH = pl.DeviceIdType.MESH
F32 = jnp.float32
BF16 = jnp.bfloat16
HIGH = lax.Precision.HIGHEST

CELLS = 1536
ROWS = 12
COLS = 128
D = 1024
CHUNK = 256
NCHUNK = CELLS // CHUNK
LANES = 128
TILES = D // LANES
NX, NY, NZ, NLON = 4, 4, 8, 8


def remote(src, dst, send_sem, recv_sem, **where):
    return pltpu.make_async_remote_copy(
        src_ref=src,
        dst_ref=dst,
        send_sem=send_sem,
        recv_sem=recv_sem,
        device_id=where,
        device_id_type=MESH,
    )


EARLY = 4


def contract(left, right):
    return lax.dot_general(left, right, (((0,), (0,)), ((), ())), preferred_element_type=F32)


def kernel(
    lat_hbm, gain_hbm, w1_hbm, bias_hbm, w2_hbm, table_hbm, target_hbm, types_hbm, band_hbm,
    outlat_ref, outhid_ref, outw_ref, outgain_ref, outbias_ref,
    x_ref, w1_ref, gain_ref, bias_ref, w2_ref, table_ref, target_ref, types_ref, band_ref,
    n_ref, v_ref, u_ref, p_ref, inv_ref, coef_ref, tcol_ref, square_ref,
    q_ref, tab_ref, s_ref, b_ref, fb_ref, gacc_ref, mine_ref, ex_ref,
    give_ref, take_ref, own_ref, first_ref, part_ref, cross_ref, piece_ref, depth_ref,
    hid_ref, sm_ref, sm1_ref, t1_ref, sm2_ref, t2_ref, sm3_ref, smo_ref,
    xsem, wsem, insem, ex_s, ex_r, core_s, core_r, first_s, first_r, cross_s, cross_r, depth_s, depth_r,
    agz_s, agz_r, agx_s, agx_r, agc_s, agc_r, sm1_s, sm1_r, sm2_s, sm2_r, sm3_s, sm3_r, sm4_s, sm4_r,
):
    z = lax.axis_index("lat")
    lon = lax.axis_index("lon")
    y = lax.axis_index("mem")
    x = lon // 2
    core = lon % 2

    def lon_at(step):
        return lax.rem(x + step, NX) * 2 + core

    def chunk_rows(i):
        return pl.ds(i * CHUNK, CHUNK)

    loads = [pltpu.make_async_copy(lat_hbm.at[chunk_rows(i)], x_ref.at[chunk_rows(i)], xsem.at[i]) for i in range(NCHUNK)]
    wload = pltpu.make_async_copy(w1_hbm, w1_ref, wsem)
    smalls = [
        pltpu.make_async_copy(source, target, insem.at[i])
        for i, (source, target) in enumerate(
            (
                (w2_hbm, w2_ref),
                (types_hbm, types_ref),
                (table_hbm, table_ref),
                (gain_hbm, gain_ref),
                (bias_hbm, bias_ref),
                (band_hbm, band_ref),
                (target_hbm, target_ref),
            )
        )
    ]
    loads[0].start()
    for copy in smalls:
        copy.start()
    wload.start()
    for i in range(1, NCHUNK):
        loads[i].start()

    barrier = pltpu.get_barrier_semaphore()
    away = [(dz, dl) for dz in (4, 3, 5, 2, 6, 1, 7, 0) for dl in (4, 5, 3, 2, 6, 7, 1, 0) if (dz, dl) != (0, 0)]

    def over(dz, dl):
        return {"lat": lax.rem(z + dz, NZ), "lon": lax.rem(lon + dl, NLON)}

    for dz, dl in away:
        pl.semaphore_signal(barrier, inc=1, device_id=over(dz, dl), device_id_type=MESH)
    for k in range(1, NY):
        pl.semaphore_signal(barrier, inc=1, device_id={"mem": lax.rem(y + k, NY)}, device_id_type=MESH)

    for copy in smalls:
        copy.wait()
    tab_ref[...] = jnp.zeros_like(tab_ref)
    tab_ref[0:3, :] = table_ref[...]
    table = tab_ref[...]
    high = table.astype(BF16)
    rest = table - high.astype(F32)
    middle = rest.astype(BF16)
    w2 = w2_ref[...]
    dims = (((1,), (0,)), ((), ()))
    q_ref[...] = lax.dot_general(high, w2, dims, preferred_element_type=F32) + lax.dot_general(
        middle, w2, dims, preferred_element_type=F32
    )
    square_ref[...] = jnp.zeros_like(square_ref)
    square_ref[0:ROWS, :] = types_ref[...].astype(F32)
    turned = square_ref[...].T
    for r in range(ROWS):
        tcol_ref[r * COLS : (r + 1) * COLS, :] = jnp.broadcast_to(turned[:, r : r + 1], (COLS, LANES))

    gain = gain_ref[...]
    bias = bias_ref[...]

    def normalise(i):
        rows = chunk_rows(i)
        loads[i].wait()
        xf = x_ref[rows, :].astype(F32)
        inv = lax.rsqrt(jnp.mean(xf * xf, axis=-1, keepdims=True) + 1e-05)
        inv_ref[rows, :] = jnp.broadcast_to(inv, (CHUNK, LANES))
        n_ref[rows, :] = (xf * inv * gain).astype(BF16)

    def first_dot(i):
        rows = chunk_rows(i)
        v_ref[rows, :] = jnp.dot(n_ref[rows, :], w1_ref[...], preferred_element_type=F32)

    kind = lax.broadcasted_iota(jnp.int32, (16, COLS), 0)

    def activate(i):
        rows = chunk_rows(i)
        p = v_ref[rows, :] + bias
        act = (p * (0.5 * jnp.tanh(0.5 * p) + 0.5)).astype(BF16)
        left = kind == types_ref[2 * i : 2 * i + 1, :]
        right = (kind - 8) == types_ref[2 * i + 1 : 2 * i + 2, :]
        onehot = jnp.concatenate([left.astype(F32), right.astype(F32)], axis=1).astype(BF16)
        s_ref[i * 16 : (i + 1) * 16, :] = jnp.dot(onehot, act, preferred_element_type=F32)

    normalise(0)
    wload.wait()
    for i in range(NCHUNK):
        first_dot(i)
        if i + 1 < NCHUNK:
            normalise(i + 1)
        if i >= 1:
            activate(i - 1)
    activate(NCHUNK - 1)

    lanes16 = lax.broadcasted_iota(jnp.int32, (16, LANES), 1)
    subs16 = lax.broadcasted_iota(jnp.int32, (16, LANES), 0)
    diagonal = lanes16 == subs16
    net = jnp.sum(s_ref[...].reshape(ROWS, 8, D) * q_ref[...][None], axis=1)
    net = jnp.sum(net, axis=1, keepdims=True)
    net = jnp.concatenate([net, jnp.zeros((16 - ROWS, 1), F32)], axis=0)
    net = jnp.sum(jnp.where(diagonal, net, 0.0), axis=0, keepdims=True)
    mine_ref[...] = jnp.zeros_like(mine_ref)
    mine_ref[0:1, 0:ROWS] = band_ref[...].astype(F32)
    mine_ref[1:2, 0:ROWS] = target_ref[...]
    lane1 = lax.broadcasted_iota(jnp.int32, (1, LANES), 1)
    coslat = jnp.cos(math.pi * (mine_ref[0:1, :] / 720.0 - 0.5))
    coslat = jnp.where(lane1 < ROWS, coslat, 0.0)
    mine_ref[0:1, :] = coslat * net * (1.0 / (NLON * COLS))

    pl.semaphore_wait(barrier, len(away) + NY - 1)
    sent = []

    def launch(copy):
        copy.start()
        sent.append(copy)
        return copy

    ex = [
        launch(remote(mine_ref, ex_ref.at[z, lon], ex_s.at[dz, dl], ex_r.at[dz, dl], **over(dz, dl)))
        for dz, dl in away
    ]
    ex_ref[z, lon] = mine_ref[...]

    def unscaled(i):
        rows = chunk_rows(i)
        kinds = tcol_ref[rows, :]
        is_one = kinds == 1.0
        is_two = kinds == 2.0
        inner = jnp.zeros((CHUNK, LANES), F32)
        for tile in range(TILES):
            cols = slice(tile * LANES, (tile + 1) * LANES)
            before = v_ref[rows, cols]
            p = before + bias_ref[0:1, cols]
            sigma = 0.5 * jnp.tanh(0.5 * p) + 0.5
            slope = sigma + (p * sigma) * (1.0 - sigma)
            weight = jnp.where(is_one, q_ref[1:2, cols], jnp.where(is_two, q_ref[2:3, cols], q_ref[0:1, cols]))
            grad = slope * weight
            inner += grad * before
            b_ref[2 * i : 2 * i + 2, cols] = jnp.sum(grad.reshape(2, COLS, LANES), axis=1)
            u_ref[rows, cols] = grad.astype(BF16)
        inv = inv_ref[rows, :]
        inner = jnp.sum(inner, axis=1, keepdims=True)
        coef_ref[rows, :] = inv * inv * (inner * (1.0 / D))

    def back(i):
        rows = chunk_rows(i)
        v_ref[rows, :] = lax.dot_general(
            u_ref[rows, :], w1_ref[...], (((1,), (1,)), ((), ())), preferred_element_type=F32
        )

    unscaled(0)
    for i in range(1, NCHUNK):
        if i <= EARLY:
            back(i - 1)
        unscaled(i)
    coscol = jnp.sum(jnp.where(diagonal, coslat, 0.0), axis=1, keepdims=True) * (1.0 / (ROWS * NZ))
    for copy in ex:
        copy.wait_recv()

    sums = [jnp.sum(ex_ref[k], axis=0) for k in range(NZ)]
    weighted = jnp.concatenate([sums[k][0:1, :] for k in range(NZ)], axis=0)
    targets = jnp.concatenate([ex_ref[k, 0][1:2, :] for k in range(NZ)], axis=0)
    sub8 = lax.broadcasted_iota(jnp.int32, (8, LANES), 0)
    lane8 = lax.broadcasted_iota(jnp.int32, (8, LANES), 1)
    count = (ROWS * NZ - ROWS * sub8 - lane8).astype(F32)
    south = jnp.sum(jnp.where(sub8 < z, weighted, 0.0), axis=0, keepdims=True)
    north = jnp.sum(jnp.where(sub8 > z, count * weighted - targets, 0.0), axis=0, keepdims=True)
    here = jnp.sum(jnp.where(sub8 == z, weighted, 0.0), axis=0, keepdims=True)
    goal = jnp.sum(jnp.where(sub8 == z, targets, 0.0), axis=0, keepdims=True)
    left_over = ROWS * NZ - ROWS * z
    both = (left_over - jnp.maximum(subs16, lanes16)).astype(F32) * here
    both = both + (left_over - subs16).astype(F32) * south + north - jnp.where(lanes16 >= subs16, goal, 0.0)
    flux = coscol * jnp.sum(both, axis=1, keepdims=True)
    fb_ref[...] = jnp.broadcast_to(flux, (16, LANES))

    def scale_tile(slot, half, t):
        for way in range(2):
            cols = pl.ds(pl.multiple_of(half * 512 + t * 256 + way * LANES, LANES), LANES)
            for r in range(ROWS):
                rows = pl.ds(r * COLS, COLS)
                p_ref[slot, rows, way * LANES : (way + 1) * LANES] = (
                    u_ref[rows, cols].astype(F32) * fb_ref[r : r + 1, :]
                ).astype(BF16)

    def hidden_tile(ref, slot, t):
        tile = contract(n_ref[...], p_ref[slot])
        for way in range(2):
            ref[t, way] = tile[:, way * LANES : (way + 1) * LANES].reshape(NY, NX, 64, LANES)

    sibling = x * 2 + 1 - core
    tiles = ((give_ref, 1 - core, 0), (give_ref, 1 - core, 1), (own_ref, core, 0), (own_ref, core, 1))

    to_core = []
    scale_tile(0, *tiles[0][1:])
    for slot in range(4):
        hidden_tile(tiles[slot][0], slot, tiles[slot][2])
        if slot < 3:
            scale_tile(slot + 1, *tiles[slot + 1][1:])
        if slot < 2:
            to_core.append(
                launch(remote(give_ref.at[slot], take_ref.at[slot], core_s.at[slot], core_r.at[slot], lon=sibling))
            )

    def place(way):
        return y if way == 0 else x

    def toward(way, step):
        if way == 0:
            return {"mem": lax.rem(y + step, NY)}
        return {"lon": lon_at(step)}

    def share(t, way, owner):
        return own_ref.at[t, way, owner] if way == 0 else own_ref.at[t, way, :, owner]

    firsts = {}

    def first(t):
        to_core[t].wait_recv()
        own_ref[t] = own_ref[t] + take_ref[t]
        for k in (2, 1, 3):
            for way in range(2):
                firsts[t, way, k] = launch(
                    remote(
                        share(t, way, lax.rem(place(way) + k, 4)),
                        first_ref.at[t, way, k - 1],
                        first_s.at[t, way, k - 1],
                        first_r.at[t, way, k - 1],
                        **toward(way, k),
                    )
                )

    first(0)

    gacc_ref[...] = jnp.zeros_like(gacc_ref)

    def latent_grad(i):
        rows = chunk_rows(i)
        flux = jnp.concatenate(
            [jnp.broadcast_to(fb_ref[2 * i + k : 2 * i + k + 1, :], (COLS, LANES)) for k in range(2)], axis=0
        )
        inv = inv_ref[rows, :] * flux
        coef = coef_ref[rows, :] * flux
        for tile in range(TILES):
            cols = slice(tile * LANES, (tile + 1) * LANES)
            xf = x_ref[rows, cols].astype(F32)
            scaled = v_ref[rows, cols] * inv
            gacc_ref[:, cols] += jnp.sum((scaled * xf).reshape(CHUNK // 8, 8, LANES), axis=0)
            outlat_ref[rows, cols] = (scaled * gain_ref[0:1, cols] - xf * coef).astype(BF16)

    for i in range(EARLY, NCHUNK):
        back(i)
    for i in range(NCHUNK):
        latent_grad(i)

    small = jnp.zeros((8, D), F32)
    bias_sum = jnp.zeros((1, D), F32)
    for r in range(ROWS):
        scale = fb_ref[r : r + 1, 0:1]
        small = small + s_ref[r * 8 : (r + 1) * 8, :] * scale
        bias_sum = bias_sum + b_ref[r : r + 1, :] * scale
    gain_sum = jnp.sum(gacc_ref[...], axis=0, keepdims=True)
    row8 = lax.broadcasted_iota(jnp.int32, (8, D), 0)
    small = jnp.where(row8 == 3, bias_sum, jnp.where(row8 == 4, gain_sum, small))
    for k in range(NLON):
        sm_ref[k] = small[:, k * LANES : (k + 1) * LANES]
    sm1 = []
    for k in range(1, NLON):
        peer = lax.rem(lon + k, NLON)
        sm1.append(launch(remote(sm_ref.at[peer], sm1_ref.at[lon], sm1_s.at[k - 1], sm1_r.at[k - 1], lon=peer)))
    sm1_ref[lon] = sm_ref[lon]

    crosses, depths, agz = {}, {}, {}

    def cross(t):
        for way in range(2):
            for k in range(1, 4):
                firsts[t, way, k].wait_recv()
            part_ref[t, way] = (
                share(t, way, place(way))[...] + first_ref[t, way, 0] + first_ref[t, way, 1] + first_ref[t, way, 2]
            )
            other = 1 - way
            for k in (2, 1, 3):
                crosses[t, way, k] = launch(
                    remote(
                        part_ref.at[t, way, lax.rem(place(other) + k, 4)],
                        cross_ref.at[t, way, k - 1],
                        cross_s.at[t, way, k - 1],
                        cross_r.at[t, way, k - 1],
                        **toward(other, k),
                    )
                )

    by_distance = (4, 3, 5, 2, 6, 1, 7)

    def deepen(t):
        for way in range(2):
            for k in range(1, 4):
                crosses[t, way, k].wait_recv()
            piece = part_ref[t, way, place(1 - way)] + cross_ref[t, way, 0] + cross_ref[t, way, 1] + cross_ref[t, way, 2]
            piece_ref[t, :, way] = piece.reshape(NZ, 8, LANES)
        for k in by_distance:
            peer = lax.rem(z + k, NZ)
            depths[t, k] = launch(
                remote(
                    piece_ref.at[t, peer], depth_ref.at[t, k - 1], depth_s.at[t, k - 1], depth_r.at[t, k - 1], lat=peer
                )
            )

    slots = (0, 1, 7, 2, 6, 3, 5, 4)
    slot_of = {k: slots.index(k) for k in range(NZ)}

    def finish(t):
        for k in range(1, NZ):
            depths[t, k].wait_recv()
        piece = piece_ref[t, z]
        for k in range(NZ - 1):
            piece = piece + depth_ref[t, k]
        hid_ref[core, t, x, 0] = piece
        for k in by_distance:
            agz[t, k] = launch(
                remote(
                    hid_ref.at[core, t, x, 0],
                    hid_ref.at[core, t, x, slot_of[NZ - k]],
                    agz_s.at[t, k - 1],
                    agz_r.at[t, k - 1],
                    lat=lax.rem(z + k, NZ),
                )
            )

    groups = (((0, 8),), ((0, 1), (1, 3), (3, 5), (5, 8)))
    agx, agc = {}, {}

    def spread(t, g):
        start, stop = groups[t][g]
        for k in range(1, NZ):
            if start <= slot_of[NZ - k] < stop:
                agz[t, k].wait_recv()
        spot = hid_ref.at[core, t, x, pl.ds(start, stop - start)]
        for k in (2, 1, 3):
            agx[t, g, k] = launch(remote(spot, spot, agx_s.at[t, g, k - 1], agx_r.at[t, g, k - 1], lon=lon_at(k)))
        agc[t, g, 0] = launch(remote(spot, spot, agc_s.at[t, g, 0], agc_r.at[t, g, 0], lon=sibling))

    def to_sibling(t, g):
        start, stop = groups[t][g]
        for k in (1, 3, 2):
            agx[t, g, k].wait_recv()
            spot = hid_ref.at[core, t, lax.rem(x + 4 - k, NX), pl.ds(start, stop - start)]
            agc[t, g, k] = launch(remote(spot, spot, agc_s.at[t, g, k], agc_r.at[t, g, k], lon=sibling))

    def place_rows(half, t):
        for xi in range(NX):
            for k in range(NZ):
                rows = pl.ds(pl.multiple_of(xi * 64 + lax.rem(z + k, NZ) * 8, 8), 8)
                for way in range(2):
                    cols = pl.ds(pl.multiple_of(half * 512 + t * 256 + way * LANES, LANES), LANES)
                    outhid_ref[rows, cols] = hid_ref[half, t, xi, slot_of[k], way]

    def drain(count):
        for copy in sent[:count]:
            copy.wait_send()
        del sent[:count]

    drain(len(ex) + len(to_core))
    early = [firsts[0, way, k] for way in range(2) for k in range(1, 4)]
    for copy in early:
        copy.wait_send()
    sent[:] = [copy for copy in sent if not any(copy is done for done in early)]
    first(1)
    cross(0)
    for copy in sm1:
        copy.wait_recv()
    total = sm1_ref[0]
    for k in range(1, NLON):
        total = total + sm1_ref[k]
    t1_ref[...] = total
    sm2 = [
        launch(remote(t1_ref, sm2_ref.at[z], sm2_s.at[k - 1], sm2_r.at[k - 1], lat=lax.rem(z + k, NZ)))
        for k in by_distance
    ]
    sm2_ref[z] = t1_ref[...]
    drain(len(sm1))
    deepen(0)
    cross(1)
    drain(len(firsts) // 2 + len(crosses) // 2 + len(sm2))
    finish(0)
    deepen(1)
    for copy in sm2:
        copy.wait_recv()
    total = sm2_ref[0]
    for k in range(1, NZ):
        total = total + sm2_ref[k]
    t2_ref[...] = total
    sm3 = [
        launch(remote(t2_ref, sm3_ref.at[y], sm3_s.at[k - 1], sm3_r.at[k - 1], mem=lax.rem(y + k, NY)))
        for k in range(1, NY)
    ]
    sm3_ref[y] = t2_ref[...]
    spread(0, 0)
    finish(1)
    spread(1, 0)
    drain(len(sent) - len(agz) // 2 - 4)
    for copy in sm3:
        copy.wait_recv()
    total = sm3_ref[0]
    for k in range(1, NY):
        total = total + sm3_ref[k]
    smo_ref[lon] = total
    sm4 = [
        launch(remote(smo_ref.at[lon], smo_ref.at[lon], sm4_s.at[k - 1], sm4_r.at[k - 1], lon=lax.rem(lon + k, NLON)))
        for k in range(1, NLON)
    ]
    to_sibling(0, 0)
    place_rows(core, 0)
    spread(1, 1)
    to_sibling(1, 0)
    spread(1, 2)
    to_sibling(1, 1)
    spread(1, 3)
    for copy in sm4:
        copy.wait_recv()
    for k in range(NLON):
        cols = slice(k * LANES, (k + 1) * LANES)
        outbias_ref[0:1, cols] = smo_ref[k][3:4, :]
        outgain_ref[0:1, cols] = smo_ref[k][4:5, :]
        outw_ref[:, cols] = lax.dot_general(
            tab_ref[...], smo_ref[k], (((0,), (0,)), ((), ())), precision=HIGH, preferred_element_type=F32
        )
    for k in range(4):
        agc[0, 0, k].wait_recv()
    place_rows(1 - core, 0)
    drain(len(sent) - 4)
    to_sibling(1, 2)
    to_sibling(1, 3)
    place_rows(core, 1)
    drain(len(sent))
    for g in range(4):
        for k in range(4):
            agc[1, g, k].wait_recv()
    place_rows(1 - core, 1)


def write_out(*refs):
    sems = refs[-1]
    half = len(refs) // 2
    copies = [pltpu.make_async_copy(refs[i], refs[half + i], sems.at[i]) for i in range(half)]
    for copy in copies:
        copy.start()
    for copy in copies:
        copy.wait()


def on_device(latent, norm_gain, hidden_weight, hidden_bias, output_weight, flux_table, target, land_sea, band_index):
    vmem = pl.BlockSpec(memory_space=pltpu.VMEM)
    hbm = pl.BlockSpec(memory_space=pl.ANY)
    dma = pltpu.SemaphoreType.DMA
    scratch = [
        pltpu.VMEM((CELLS, D), BF16),
        pltpu.VMEM((D, D), BF16),
        pltpu.VMEM((1, D), F32),
        pltpu.VMEM((1, D), F32),
        pltpu.VMEM((80, D), BF16),
        pltpu.VMEM((3, 80), F32),
        pltpu.VMEM((1, ROWS), F32),
        pltpu.VMEM((ROWS, COLS), jnp.int32),
        pltpu.VMEM((1, ROWS), jnp.int32),
        pltpu.VMEM((CELLS, D), BF16),
        pltpu.VMEM((CELLS, D), F32),
        pltpu.VMEM((CELLS, D), BF16),
        pltpu.VMEM((4, CELLS, 256), BF16),
        pltpu.VMEM((CELLS, LANES), F32),
        pltpu.VMEM((CELLS, LANES), F32),
        pltpu.VMEM((CELLS, LANES), F32),
        pltpu.VMEM((LANES, LANES), F32),
        pltpu.VMEM((8, D), F32),
        pltpu.VMEM((8, 80), F32),
        pltpu.VMEM((ROWS * 8, D), F32),
        pltpu.VMEM((16, D), F32),
        pltpu.VMEM((16, LANES), F32),
        pltpu.VMEM((8, D), F32),
        pltpu.VMEM((8, LANES), F32),
        pltpu.VMEM((NZ, NLON, 8, LANES), F32),
        pltpu.VMEM((2, 2, NY, NX, 64, LANES), F32),
        pltpu.VMEM((2, 2, NY, NX, 64, LANES), F32),
        pltpu.VMEM((2, 2, NY, NX, 64, LANES), F32),
        pltpu.VMEM((2, 2, 3, 4, 64, LANES), F32),
        pltpu.VMEM((2, 2, 4, 64, LANES), F32),
        pltpu.VMEM((2, 2, 3, 64, LANES), F32),
        pltpu.VMEM((2, NZ, 2, 8, LANES), F32),
        pltpu.VMEM((2, NZ - 1, 2, 8, LANES), F32),
        pltpu.VMEM((2, 2, NX, NZ, 2, 8, LANES), F32),
        pltpu.VMEM((NLON, 8, LANES), F32),
        pltpu.VMEM((NLON, 8, LANES), F32),
        pltpu.VMEM((8, LANES), F32),
        pltpu.VMEM((NZ, 8, LANES), F32),
        pltpu.VMEM((8, LANES), F32),
        pltpu.VMEM((NY, 8, LANES), F32),
        pltpu.VMEM((NLON, 8, LANES), F32),
        dma((NCHUNK,)),
        dma,
        dma((7,)),
        dma((NZ, NLON)), dma((NZ, NLON)),
        dma((2,)), dma((2,)),
        dma((2, 2, 3)), dma((2, 2, 3)),
        dma((2, 2, 3)), dma((2, 2, 3)),
        dma((2, 7)), dma((2, 7)),
        dma((2, 7)), dma((2, 7)),
        dma((2, 4, 3)), dma((2, 4, 3)),
        dma((2, 4, 4)), dma((2, 4, 4)),
        dma((7,)), dma((7,)),
        dma((7,)), dma((7,)),
        dma((3,)), dma((3,)),
        dma((7,)), dma((7,)),
    ]
    shapes = (((CELLS, D), BF16), ((D // NY, D), F32), ((80, D), F32), ((1, D), F32), ((1, D), F32))
    held = pl.pallas_call(
        kernel,
        out_shape=tuple(pltpu.VMEM(*shape) for shape in shapes),
        in_specs=[hbm] * 9,
        out_specs=(vmem,) * 5,
        scratch_shapes=scratch,
        compiler_params=pltpu.CompilerParams(
            collective_id=0, has_side_effects=True, vmem_limit_bytes=56 * 1024 * 1024
        ),
        cost_estimate=pl.CostEstimate(flops=10_000_000_000, bytes_accessed=9_000_000, transcendentals=3_000_000),
    )(
        latent.reshape(CELLS, D),
        norm_gain.reshape(1, D),
        hidden_weight,
        hidden_bias.reshape(1, D),
        output_weight.T,
        flux_table,
        target,
        land_sea,
        band_index.reshape(1, ROWS),
    )
    grad_cells, grad_hidden, grad_out, grad_gain, grad_bias = pl.pallas_call(
        write_out,
        out_shape=tuple(jax.ShapeDtypeStruct(*shape) for shape in shapes),
        in_specs=[vmem] * 5,
        out_specs=(hbm,) * 5,
        scratch_shapes=[dma((5,))],
        compiler_params=pltpu.CompilerParams(vmem_limit_bytes=1024 * 1024),
    )(*[pltpu.with_memory_space_constraint(array, pltpu.VMEM) for array in held])
    return (
        grad_cells.reshape(latent.shape),
        grad_hidden,
        grad_out.T,
        grad_gain.reshape(D),
        grad_bias.reshape(D),
    )


def solution(mesh):
    return jax.shard_map(
        on_device,
        mesh=mesh,
        in_specs=(
            P("mem", "lat", "lon", None),
            P(),
            P(),
            P(),
            P(),
            P(),
            P("mem", "lat"),
            P("lat", "lon"),
            P("lat"),
        ),
        out_specs=(P("mem", "lat", "lon", None), P("mem", None), P(), P(), P()),
        check_vma=False,
    )
```

```python
import functools
import math

import jax
import jax.numpy as jnp
from jax import lax
from jax.experimental import pallas as pl
from jax.experimental.pallas import tpu as pltpu
from jax.sharding import PartitionSpec as P

MESH = pl.DeviceIdType.MESH
F32 = jnp.float32
BF16 = jnp.bfloat16
HIGH = lax.Precision.HIGHEST

CELLS = 1536
ROWS = 12
COLS = 128
D = 1024
CHUNK = 256
NCHUNK = CELLS // CHUNK
LANES = 128
TILES = D // LANES
NX, NY, NZ, NLON = 4, 4, 8, 8


def remote(src, dst, send_sem, recv_sem, **where):
    return pltpu.make_async_remote_copy(
        src_ref=src,
        dst_ref=dst,
        send_sem=send_sem,
        recv_sem=recv_sem,
        device_id=where,
        device_id_type=MESH,
    )


def contract(left, right):
    return lax.dot_general(left, right, (((0,), (0,)), ((), ())), preferred_element_type=F32)


def kernel(
    lat_hbm, gain_hbm, w1_hbm, bias_hbm, w2_hbm, table_hbm, target_hbm, types_hbm, band_hbm,
    outlat_ref, outhid_ref, outw_ref, outgain_ref, outbias_ref,
    x_ref, w1_ref, gain_ref, bias_ref, w2_ref, table_ref, target_ref, types_ref, band_ref,
    n_ref, v_ref, u_ref, p_ref, inv_ref, coef_ref, tcol_ref, square_ref,
    q_ref, tab_ref, s_ref, b_ref, fb_ref, gacc_ref, mine_ref, ex1_ref, line_ref, ex2_ref,
    give_ref, take_ref, own_ref, first_ref, part_ref, cross_ref, piece_ref, depth_ref,
    hid_ref, sm_ref, sm1_ref, t1_ref, sm2_ref, t2_ref, sm3_ref, smo_ref,
    xsem, wsem, insem, ex1_s, ex1_r, ex2_s, ex2_r, core_s, core_r, first_s, first_r, cross_s, cross_r, depth_s, depth_r,
    agz_s, agz_r, agx_s, agx_r, agc_s, agc_r, sm1_s, sm1_r, sm2_s, sm2_r, sm3_s, sm3_r, sm4_s, sm4_r,
):
    z = lax.axis_index("lat")
    lon = lax.axis_index("lon")
    y = lax.axis_index("mem")
    x = lon // 2
    core = lon % 2

    def lon_at(step):
        return lax.rem(x + step, NX) * 2 + core

    def chunk_rows(i):
        return pl.ds(i * CHUNK, CHUNK)

    loads = [pltpu.make_async_copy(lat_hbm.at[chunk_rows(i)], x_ref.at[chunk_rows(i)], xsem.at[i]) for i in range(NCHUNK)]
    wload = pltpu.make_async_copy(w1_hbm, w1_ref, wsem)
    smalls = [
        pltpu.make_async_copy(source, target, insem.at[i])
        for i, (source, target) in enumerate(
            (
                (w2_hbm, w2_ref),
                (types_hbm, types_ref),
                (table_hbm, table_ref),
                (gain_hbm, gain_ref),
                (bias_hbm, bias_ref),
                (band_hbm, band_ref),
                (target_hbm, target_ref),
            )
        )
    ]
    loads[0].start()
    for copy in smalls:
        copy.start()
    wload.start()
    for i in range(1, NCHUNK):
        loads[i].start()

    barrier = pltpu.get_barrier_semaphore()
    for k in range(1, NLON):
        pl.semaphore_signal(barrier, inc=1, device_id={"lon": lax.rem(lon + k, NLON)}, device_id_type=MESH)
    for k in range(1, NZ):
        pl.semaphore_signal(barrier, inc=1, device_id={"lat": lax.rem(z + k, NZ)}, device_id_type=MESH)
    for k in range(1, NY):
        pl.semaphore_signal(barrier, inc=1, device_id={"mem": lax.rem(y + k, NY)}, device_id_type=MESH)

    for copy in smalls:
        copy.wait()
    tab_ref[...] = jnp.zeros_like(tab_ref)
    tab_ref[0:3, :] = table_ref[...]
    table = tab_ref[...]
    high = table.astype(BF16)
    rest = table - high.astype(F32)
    middle = rest.astype(BF16)
    w2 = w2_ref[...]
    dims = (((1,), (0,)), ((), ()))
    q_ref[...] = lax.dot_general(high, w2, dims, preferred_element_type=F32) + lax.dot_general(
        middle, w2, dims, preferred_element_type=F32
    )
    square_ref[...] = jnp.zeros_like(square_ref)
    square_ref[0:ROWS, :] = types_ref[...].astype(F32)
    turned = square_ref[...].T
    for r in range(ROWS):
        tcol_ref[r * COLS : (r + 1) * COLS, :] = jnp.broadcast_to(turned[:, r : r + 1], (COLS, LANES))

    gain = gain_ref[...]
    bias = bias_ref[...]

    def normalise(i):
        rows = chunk_rows(i)
        loads[i].wait()
        xf = x_ref[rows, :].astype(F32)
        inv = lax.rsqrt(jnp.mean(xf * xf, axis=-1, keepdims=True) + 1e-05)
        inv_ref[rows, :] = jnp.broadcast_to(inv, (CHUNK, LANES))
        n_ref[rows, :] = (xf * inv * gain).astype(BF16)

    def first_dot(i):
        rows = chunk_rows(i)
        v_ref[rows, :] = jnp.dot(n_ref[rows, :], w1_ref[...], preferred_element_type=F32)

    kind = lax.broadcasted_iota(jnp.int32, (16, COLS), 0)

    def activate(i):
        rows = chunk_rows(i)
        p = v_ref[rows, :] + bias
        act = (p * (0.5 * jnp.tanh(0.5 * p) + 0.5)).astype(BF16)
        left = kind == types_ref[2 * i : 2 * i + 1, :]
        right = (kind - 8) == types_ref[2 * i + 1 : 2 * i + 2, :]
        onehot = jnp.concatenate([left.astype(F32), right.astype(F32)], axis=1).astype(BF16)
        s_ref[i * 16 : (i + 1) * 16, :] = jnp.dot(onehot, act, preferred_element_type=F32)

    normalise(0)
    wload.wait()
    for i in range(NCHUNK):
        first_dot(i)
        if i + 1 < NCHUNK:
            normalise(i + 1)
        if i >= 1:
            activate(i - 1)
    activate(NCHUNK - 1)

    lanes16 = lax.broadcasted_iota(jnp.int32, (16, LANES), 1)
    subs16 = lax.broadcasted_iota(jnp.int32, (16, LANES), 0)
    diagonal = lanes16 == subs16
    net = jnp.sum(s_ref[...].reshape(ROWS, 8, D) * q_ref[...][None], axis=1)
    net = jnp.sum(net, axis=1, keepdims=True)
    net = jnp.concatenate([net, jnp.zeros((16 - ROWS, 1), F32)], axis=0)
    net = jnp.sum(jnp.where(diagonal, net, 0.0), axis=0, keepdims=True)
    mine_ref[...] = jnp.zeros_like(mine_ref)
    mine_ref[0:1, 0:ROWS] = band_ref[...].astype(F32)
    mine_ref[1:2, 0:ROWS] = target_ref[...]
    lane1 = lax.broadcasted_iota(jnp.int32, (1, LANES), 1)
    coslat = jnp.cos(math.pi * (mine_ref[0:1, :] / 720.0 - 0.5))
    coslat = jnp.where(lane1 < ROWS, coslat, 0.0)
    mine_ref[0:1, :] = coslat * net * (1.0 / (NLON * COLS))

    pl.semaphore_wait(barrier, (NLON - 1) + (NZ - 1) + (NY - 1))
    sent = []

    def launch(copy):
        copy.start()
        sent.append(copy)
        return copy

    by_distance = (4, 3, 5, 2, 6, 1, 7)
    ex1 = [
        launch(remote(mine_ref, ex1_ref.at[lon], ex1_s.at[k - 1], ex1_r.at[k - 1], lon=lax.rem(lon + k, NLON)))
        for k in by_distance
    ]
    ex1_ref[lon] = mine_ref[...]

    def unscaled(i):
        rows = chunk_rows(i)
        kinds = tcol_ref[rows, :]
        is_one = kinds == 1.0
        is_two = kinds == 2.0
        inner = jnp.zeros((CHUNK, LANES), F32)
        for tile in range(TILES):
            cols = slice(tile * LANES, (tile + 1) * LANES)
            before = v_ref[rows, cols]
            p = before + bias_ref[0:1, cols]
            sigma = 0.5 * jnp.tanh(0.5 * p) + 0.5
            slope = sigma + (p * sigma) * (1.0 - sigma)
            weight = jnp.where(is_one, q_ref[1:2, cols], jnp.where(is_two, q_ref[2:3, cols], q_ref[0:1, cols]))
            grad = slope * weight
            inner += grad * before
            b_ref[2 * i : 2 * i + 2, cols] = jnp.sum(grad.reshape(2, COLS, LANES), axis=1)
            u_ref[rows, cols] = grad.astype(BF16)
        inv = inv_ref[rows, :]
        inner = jnp.sum(inner, axis=1, keepdims=True)
        coef_ref[rows, :] = inv * inv * (inner * (1.0 / D))

    def back(i):
        rows = chunk_rows(i)
        v_ref[rows, :] = lax.dot_general(
            u_ref[rows, :], w1_ref[...], (((1,), (1,)), ((), ())), preferred_element_type=F32
        )

    for i in range(NCHUNK // 2):
        unscaled(i)
        if i >= 1:
            back(i - 1)
    coscol = jnp.sum(jnp.where(diagonal, coslat, 0.0), axis=1, keepdims=True) * (1.0 / (ROWS * NZ))
    for copy in ex1:
        copy.wait_recv()
    sub8 = lax.broadcasted_iota(jnp.int32, (8, LANES), 0)
    lane8 = lax.broadcasted_iota(jnp.int32, (8, LANES), 1)
    line_ref[...] = jnp.where(sub8 == 0, jnp.sum(ex1_ref[...], axis=0), mine_ref[...])
    ex2 = [
        launch(remote(line_ref, ex2_ref.at[z], ex2_s.at[k - 1], ex2_r.at[k - 1], lat=lax.rem(z + k, NZ)))
        for k in by_distance
    ]
    ex2_ref[z] = line_ref[...]
    for i in range(NCHUNK // 2, NCHUNK):
        unscaled(i)
        back(i - 1)
    back(NCHUNK - 1)
    for copy in ex2:
        copy.wait_recv()

    weighted = jnp.concatenate([ex2_ref[k][0:1, :] for k in range(NZ)], axis=0)
    targets = jnp.concatenate([ex2_ref[k][1:2, :] for k in range(NZ)], axis=0)
    count = (ROWS * NZ - ROWS * sub8 - lane8).astype(F32)
    south = jnp.sum(jnp.where(sub8 < z, weighted, 0.0), axis=0, keepdims=True)
    north = jnp.sum(jnp.where(sub8 > z, count * weighted - targets, 0.0), axis=0, keepdims=True)
    here = jnp.sum(jnp.where(sub8 == z, weighted, 0.0), axis=0, keepdims=True)
    goal = jnp.sum(jnp.where(sub8 == z, targets, 0.0), axis=0, keepdims=True)
    left_over = ROWS * NZ - ROWS * z
    both = (left_over - jnp.maximum(subs16, lanes16)).astype(F32) * here
    both = both + (left_over - subs16).astype(F32) * south + north - jnp.where(lanes16 >= subs16, goal, 0.0)
    flux = coscol * jnp.sum(both, axis=1, keepdims=True)
    fb_ref[...] = jnp.broadcast_to(flux, (16, LANES))

    def scale_tile(slot, half, t):
        for way in range(2):
            cols = pl.ds(pl.multiple_of(half * 512 + t * 256 + way * LANES, LANES), LANES)
            for r in range(ROWS):
                rows = pl.ds(r * COLS, COLS)
                p_ref[slot, rows, way * LANES : (way + 1) * LANES] = (
                    u_ref[rows, cols].astype(F32) * fb_ref[r : r + 1, :]
                ).astype(BF16)

    def hidden_tile(ref, slot, t):
        tile = contract(n_ref[...], p_ref[slot])
        for way in range(2):
            ref[t, way] = tile[:, way * LANES : (way + 1) * LANES].reshape(NY, NX, 64, LANES)

    sibling = x * 2 + 1 - core
    tiles = ((give_ref, 1 - core, 0), (own_ref, core, 0), (give_ref, 1 - core, 1), (own_ref, core, 1))

    def place(way):
        return y if way == 0 else x

    def toward(way, step):
        if way == 0:
            return {"mem": lax.rem(y + step, NY)}
        return {"lon": lon_at(step)}

    def share(t, way, owner):
        return own_ref.at[t, way, owner] if way == 0 else own_ref.at[t, way, :, owner]

    firsts = {}

    def first(t):
        to_core[t].wait_recv()
        own_ref[t] = own_ref[t] + take_ref[t]
        for k in (2, 1, 3):
            for way in range(2):
                firsts[t, way, k] = launch(
                    remote(
                        share(t, way, lax.rem(place(way) + k, 4)),
                        first_ref.at[t, way, k - 1],
                        first_s.at[t, way, k - 1],
                        first_r.at[t, way, k - 1],
                        **toward(way, k),
                    )
                )

    to_core = []
    scale_tile(0, *tiles[0][1:])
    for slot in range(4):
        ref, _, t = tiles[slot]
        hidden_tile(ref, slot, t)
        if ref is give_ref:
            to_core.append(
                launch(remote(give_ref.at[t], take_ref.at[t], core_s.at[t], core_r.at[t], lon=sibling))
            )
        if slot < 3:
            scale_tile(slot + 1, *tiles[slot + 1][1:])
        if slot == 2:
            first(0)
    first(1)

    gacc_ref[...] = jnp.zeros_like(gacc_ref)

    def latent_grad(i):
        rows = chunk_rows(i)
        flux = jnp.concatenate(
            [jnp.broadcast_to(fb_ref[2 * i + k : 2 * i + k + 1, :], (COLS, LANES)) for k in range(2)], axis=0
        )
        inv = inv_ref[rows, :] * flux
        coef = coef_ref[rows, :] * flux
        for tile in range(TILES):
            cols = slice(tile * LANES, (tile + 1) * LANES)
            xf = x_ref[rows, cols].astype(F32)
            scaled = v_ref[rows, cols] * inv
            gacc_ref[:, cols] += jnp.sum((scaled * xf).reshape(CHUNK // 8, 8, LANES), axis=0)
            outlat_ref[rows, cols] = (scaled * gain_ref[0:1, cols] - xf * coef).astype(BF16)

    for i in range(NCHUNK):
        latent_grad(i)

    small = jnp.zeros((8, D), F32)
    bias_sum = jnp.zeros((1, D), F32)
    for r in range(ROWS):
        scale = fb_ref[r : r + 1, 0:1]
        small = small + s_ref[r * 8 : (r + 1) * 8, :] * scale
        bias_sum = bias_sum + b_ref[r : r + 1, :] * scale
    gain_sum = jnp.sum(gacc_ref[...], axis=0, keepdims=True)
    row8 = lax.broadcasted_iota(jnp.int32, (8, D), 0)
    small = jnp.where(row8 == 3, bias_sum, jnp.where(row8 == 4, gain_sum, small))
    for k in range(NLON):
        sm_ref[k] = small[:, k * LANES : (k + 1) * LANES]
    sm1 = []
    for k in range(1, NLON):
        peer = lax.rem(lon + k, NLON)
        sm1.append(launch(remote(sm_ref.at[peer], sm1_ref.at[lon], sm1_s.at[k - 1], sm1_r.at[k - 1], lon=peer)))
    sm1_ref[lon] = sm_ref[lon]

    crosses, depths, agz = {}, {}, {}

    def cross(t):
        for way in range(2):
            for k in range(1, 4):
                firsts[t, way, k].wait_recv()
            part_ref[t, way] = (
                share(t, way, place(way))[...] + first_ref[t, way, 0] + first_ref[t, way, 1] + first_ref[t, way, 2]
            )
            other = 1 - way
            for k in (2, 1, 3):
                crosses[t, way, k] = launch(
                    remote(
                        part_ref.at[t, way, lax.rem(place(other) + k, 4)],
                        cross_ref.at[t, way, k - 1],
                        cross_s.at[t, way, k - 1],
                        cross_r.at[t, way, k - 1],
                        **toward(other, k),
                    )
                )

    def deepen(t):
        for way in range(2):
            for k in range(1, 4):
                crosses[t, way, k].wait_recv()
            piece = part_ref[t, way, place(1 - way)] + cross_ref[t, way, 0] + cross_ref[t, way, 1] + cross_ref[t, way, 2]
            piece_ref[t, :, way] = piece.reshape(NZ, 8, LANES)
        for k in by_distance:
            peer = lax.rem(z + k, NZ)
            depths[t, k] = launch(
                remote(
                    piece_ref.at[t, peer], depth_ref.at[t, k - 1], depth_s.at[t, k - 1], depth_r.at[t, k - 1], lat=peer
                )
            )

    slots = (0, 1, 7, 2, 6, 3, 5, 4)
    slot_of = {k: slots.index(k) for k in range(NZ)}

    def finish(t):
        for k in range(1, NZ):
            depths[t, k].wait_recv()
        piece = piece_ref[t, z]
        for k in range(NZ - 1):
            piece = piece + depth_ref[t, k]
        hid_ref[core, t, x, 0] = piece
        for k in by_distance:
            agz[t, k] = launch(
                remote(
                    hid_ref.at[core, t, x, 0],
                    hid_ref.at[core, t, x, slot_of[NZ - k]],
                    agz_s.at[t, k - 1],
                    agz_r.at[t, k - 1],
                    lat=lax.rem(z + k, NZ),
                )
            )

    groups = (((0, 5), (5, 8)), ((0, 5), (5, 8)))
    agx, agc = {}, {}

    def spread(t, g):
        start, stop = groups[t][g]
        for k in range(1, NZ):
            if start <= slot_of[NZ - k] < stop:
                agz[t, k].wait_recv()
        spot = hid_ref.at[core, t, x, pl.ds(start, stop - start)]
        for k in (2, 1, 3):
            agx[t, g, k] = launch(remote(spot, spot, agx_s.at[t, g, k - 1], agx_r.at[t, g, k - 1], lon=lon_at(k)))
        agc[t, g, 0] = launch(remote(spot, spot, agc_s.at[t, g, 0], agc_r.at[t, g, 0], lon=sibling))

    def to_sibling(t, g):
        start, stop = groups[t][g]
        for k in (1, 3, 2):
            agx[t, g, k].wait_recv()
            spot = hid_ref.at[core, t, lax.rem(x + 4 - k, NX), pl.ds(start, stop - start)]
            agc[t, g, k] = launch(remote(spot, spot, agc_s.at[t, g, k], agc_r.at[t, g, k], lon=sibling))

    def place_rows(half, t):
        for xi in range(NX):
            for k in range(NZ):
                rows = pl.ds(pl.multiple_of(xi * 64 + lax.rem(z + k, NZ) * 8, 8), 8)
                for way in range(2):
                    cols = pl.ds(pl.multiple_of(half * 512 + t * 256 + way * LANES, LANES), LANES)
                    outhid_ref[rows, cols] = hid_ref[half, t, xi, slot_of[k], way]

    def drain(count):
        for copy in sent[:count]:
            copy.wait_send()
        del sent[:count]

    drain(len(ex1) + len(ex2) + len(to_core))
    for copy in sm1:
        copy.wait_recv()
    t1_ref[...] = jnp.sum(sm1_ref[...], axis=0)
    sm2 = [
        launch(remote(t1_ref, sm2_ref.at[z], sm2_s.at[k - 1], sm2_r.at[k - 1], lat=lax.rem(z + k, NZ)))
        for k in by_distance
    ]
    sm2_ref[z] = t1_ref[...]
    cross(0)
    cross(1)
    drain(len(firsts) + len(sm1))
    for copy in sm2:
        copy.wait_recv()
    t2_ref[...] = jnp.sum(sm2_ref[...], axis=0)
    sm3 = [
        launch(remote(t2_ref, sm3_ref.at[y], sm3_s.at[k - 1], sm3_r.at[k - 1], mem=lax.rem(y + k, NY)))
        for k in range(1, NY)
    ]
    sm3_ref[y] = t2_ref[...]
    deepen(0)
    deepen(1)
    drain(len(sm2) + len(crosses))
    for copy in sm3:
        copy.wait_recv()
    smo_ref[lon] = jnp.sum(sm3_ref[...], axis=0)
    sm4 = [
        launch(remote(smo_ref.at[lon], smo_ref.at[lon], sm4_s.at[k - 1], sm4_r.at[k - 1], lon=lax.rem(lon + k, NLON)))
        for k in by_distance
    ]
    finish(0)
    finish(1)
    drain(len(sm3) + len(depths))
    for copy in sm4:
        copy.wait_recv()
    summed = jnp.concatenate([smo_ref[k] for k in range(NLON)], axis=1)
    outbias_ref[...] = summed[3:4, :]
    outgain_ref[...] = summed[4:5, :]
    outw_ref[...] = lax.dot_general(
        tab_ref[...], summed, (((0,), (0,)), ((), ())), precision=HIGH, preferred_element_type=F32
    )
    spread(0, 0)
    spread(0, 1)
    spread(1, 0)
    spread(1, 1)
    drain(len(sm4) + len(agz))
    to_sibling(0, 0)
    to_sibling(0, 1)
    place_rows(core, 0)
    to_sibling(1, 0)
    to_sibling(1, 1)
    place_rows(core, 1)
    drain(len(agx))
    for g in range(2):
        for k in range(4):
            agc[0, g, k].wait_recv()
    place_rows(1 - core, 0)
    drain(len(sent))
    for g in range(2):
        for k in range(4):
            agc[1, g, k].wait_recv()
    place_rows(1 - core, 1)


def write_out(*refs):
    sems = refs[-1]
    half = len(refs) // 2
    copies = [pltpu.make_async_copy(refs[i], refs[half + i], sems.at[i]) for i in range(half)]
    for copy in copies:
        copy.start()
    for copy in copies:
        copy.wait()


def on_device(latent, norm_gain, hidden_weight, hidden_bias, output_weight, flux_table, target, land_sea, band_index):
    vmem = pl.BlockSpec(memory_space=pltpu.VMEM)
    hbm = pl.BlockSpec(memory_space=pl.ANY)
    dma = pltpu.SemaphoreType.DMA
    scratch = [
        pltpu.VMEM((CELLS, D), BF16),
        pltpu.VMEM((D, D), BF16),
        pltpu.VMEM((1, D), F32),
        pltpu.VMEM((1, D), F32),
        pltpu.VMEM((80, D), BF16),
        pltpu.VMEM((3, 80), F32),
        pltpu.VMEM((1, ROWS), F32),
        pltpu.VMEM((ROWS, COLS), jnp.int32),
        pltpu.VMEM((1, ROWS), jnp.int32),
        pltpu.VMEM((CELLS, D), BF16),
        pltpu.VMEM((CELLS, D), F32),
        pltpu.VMEM((CELLS, D), BF16),
        pltpu.VMEM((4, CELLS, 256), BF16),
        pltpu.VMEM((CELLS, LANES), F32),
        pltpu.VMEM((CELLS, LANES), F32),
        pltpu.VMEM((CELLS, LANES), F32),
        pltpu.VMEM((LANES, LANES), F32),
        pltpu.VMEM((8, D), F32),
        pltpu.VMEM((8, 80), F32),
        pltpu.VMEM((ROWS * 8, D), F32),
        pltpu.VMEM((16, D), F32),
        pltpu.VMEM((16, LANES), F32),
        pltpu.VMEM((8, D), F32),
        pltpu.VMEM((8, LANES), F32),
        pltpu.VMEM((NLON, 8, LANES), F32),
        pltpu.VMEM((8, LANES), F32),
        pltpu.VMEM((NZ, 8, LANES), F32),
        pltpu.VMEM((2, 2, NY, NX, 64, LANES), F32),
        pltpu.VMEM((2, 2, NY, NX, 64, LANES), F32),
        pltpu.VMEM((2, 2, NY, NX, 64, LANES), F32),
        pltpu.VMEM((2, 2, 3, 4, 64, LANES), F32),
        pltpu.VMEM((2, 2, 4, 64, LANES), F32),
        pltpu.VMEM((2, 2, 3, 64, LANES), F32),
        pltpu.VMEM((2, NZ, 2, 8, LANES), F32),
        pltpu.VMEM((2, NZ - 1, 2, 8, LANES), F32),
        pltpu.VMEM((2, 2, NX, NZ, 2, 8, LANES), F32),
        pltpu.VMEM((NLON, 8, LANES), F32),
        pltpu.VMEM((NLON, 8, LANES), F32),
        pltpu.VMEM((8, LANES), F32),
        pltpu.VMEM((NZ, 8, LANES), F32),
        pltpu.VMEM((8, LANES), F32),
        pltpu.VMEM((NY, 8, LANES), F32),
        pltpu.VMEM((NLON, 8, LANES), F32),
        dma((NCHUNK,)),
        dma,
        dma((7,)),
        dma((7,)), dma((7,)),
        dma((7,)), dma((7,)),
        dma((2,)), dma((2,)),
        dma((2, 2, 3)), dma((2, 2, 3)),
        dma((2, 2, 3)), dma((2, 2, 3)),
        dma((2, 7)), dma((2, 7)),
        dma((2, 7)), dma((2, 7)),
        dma((2, 2, 3)), dma((2, 2, 3)),
        dma((2, 2, 4)), dma((2, 2, 4)),
        dma((7,)), dma((7,)),
        dma((7,)), dma((7,)),
        dma((3,)), dma((3,)),
        dma((7,)), dma((7,)),
    ]
    shapes = (((CELLS, D), BF16), ((D // NY, D), F32), ((80, D), F32), ((1, D), F32), ((1, D), F32))
    held = pl.pallas_call(
        kernel,
        out_shape=tuple(pltpu.VMEM(*shape) for shape in shapes),
        in_specs=[hbm] * 9,
        out_specs=(vmem,) * 5,
        scratch_shapes=scratch,
        compiler_params=pltpu.CompilerParams(
            collective_id=0, has_side_effects=True, vmem_limit_bytes=56 * 1024 * 1024
        ),
        cost_estimate=pl.CostEstimate(flops=10_000_000_000, bytes_accessed=9_000_000, transcendentals=3_000_000),
    )(
        latent.reshape(CELLS, D),
        norm_gain.reshape(1, D),
        hidden_weight,
        hidden_bias.reshape(1, D),
        output_weight.T,
        flux_table,
        target,
        land_sea,
        band_index.reshape(1, ROWS),
    )
    grad_cells, grad_hidden, grad_out, grad_gain, grad_bias = pl.pallas_call(
        write_out,
        out_shape=tuple(jax.ShapeDtypeStruct(*shape) for shape in shapes),
        in_specs=[vmem] * 5,
        out_specs=(hbm,) * 5,
        scratch_shapes=[dma((5,))],
        compiler_params=pltpu.CompilerParams(vmem_limit_bytes=1024 * 1024),
    )(*[pltpu.with_memory_space_constraint(array, pltpu.VMEM) for array in held])
    return (
        grad_cells.reshape(latent.shape),
        grad_hidden,
        grad_out.T,
        grad_gain.reshape(D),
        grad_bias.reshape(D),
    )


def solution(mesh):
    return jax.shard_map(
        on_device,
        mesh=mesh,
        in_specs=(
            P("mem", "lat", "lon", None),
            P(),
            P(),
            P(),
            P(),
            P(),
            P("mem", "lat"),
            P("lat", "lon"),
            P("lat"),
        ),
        out_specs=(P("mem", "lat", "lon", None), P("mem", None), P(), P(), P()),
        check_vma=False,
    )
```

```python
import functools
import math

import jax
import jax.numpy as jnp
from jax import lax
from jax.experimental import pallas as pl
from jax.experimental.pallas import tpu as pltpu
from jax.sharding import PartitionSpec as P

MESH = pl.DeviceIdType.MESH
F32 = jnp.float32
BF16 = jnp.bfloat16
HIGH = lax.Precision.HIGHEST

CELLS = 1536
ROWS = 12
COLS = 128
D = 1024
CHUNK = 256
NCHUNK = CELLS // CHUNK
LANES = 128
TILES = D // LANES
NX, NY, NZ, NLON = 4, 4, 8, 8


def remote(src, dst, send_sem, recv_sem, **where):
    return pltpu.make_async_remote_copy(
        src_ref=src,
        dst_ref=dst,
        send_sem=send_sem,
        recv_sem=recv_sem,
        device_id=where,
        device_id_type=MESH,
    )


def contract(left, right):
    return lax.dot_general(left, right, (((0,), (0,)), ((), ())), preferred_element_type=F32)


def kernel(
    lat_hbm, gain_hbm, w1_hbm, bias_hbm, w2_hbm, table_hbm, target_hbm, types_hbm, band_hbm,
    outlat_ref, outhid_ref, outw_ref, outgain_ref, outbias_ref,
    x_ref, w1_ref, gain_ref, bias_ref, w2_ref, table_ref, target_ref, types_ref, band_ref,
    n_ref, v_ref, u_ref, p_ref, inv_ref, coef_ref, tcol_ref, square_ref,
    q_ref, tab_ref, s_ref, b_ref, fb_ref, gacc_ref, mine_ref, ex1_ref, line_ref, ex2_ref,
    give_ref, take_ref, own_ref, pass_ref, plain_ref, agg_ref, part_ref, cross_ref, piece_ref, depth_ref,
    hid_ref, sm_ref, sm1_ref, t1_ref, sm2_ref, t2_ref, sm3_ref, smo_ref,
    xsem, wsem, insem, ex1_s, ex1_r, ex2_s, ex2_r, core_s, core_r, first_s, first_r, cross_s, cross_r, depth_s, depth_r,
    agz_s, agz_r, agx_s, agx_r, agc_s, agc_r, sm1_s, sm1_r, sm2_s, sm2_r, sm3_s, sm3_r, sm4_s, sm4_r,
):
    z = lax.axis_index("lat")
    lon = lax.axis_index("lon")
    y = lax.axis_index("mem")
    x = lon // 2
    core = lon % 2

    def lon_at(step):
        return lax.rem(x + step, NX) * 2 + core

    def chunk_rows(i):
        return pl.ds(i * CHUNK, CHUNK)

    loads = [pltpu.make_async_copy(lat_hbm.at[chunk_rows(i)], x_ref.at[chunk_rows(i)], xsem.at[i]) for i in range(NCHUNK)]
    wloads = [
        pltpu.make_async_copy(w1_hbm.at[pl.ds(i * 256, 256)], w1_ref.at[pl.ds(i * 256, 256)], wsem.at[i]) for i in range(4)
    ]
    smalls = [
        pltpu.make_async_copy(source, target, insem.at[i])
        for i, (source, target) in enumerate(
            (
                (w2_hbm, w2_ref),
                (types_hbm, types_ref),
                (table_hbm, table_ref),
                (gain_hbm, gain_ref),
                (bias_hbm, bias_ref),
                (band_hbm, band_ref),
                (target_hbm, target_ref),
            )
        )
    ]
    loads[0].start()
    for copy in smalls:
        copy.start()
    for copy in wloads:
        copy.start()
    for i in range(1, NCHUNK):
        loads[i].start()

    barrier = pltpu.get_barrier_semaphore()
    for k in range(1, NLON):
        pl.semaphore_signal(barrier, inc=1, device_id={"lon": lax.rem(lon + k, NLON)}, device_id_type=MESH)
    for k in range(1, NZ):
        pl.semaphore_signal(barrier, inc=1, device_id={"lat": lax.rem(z + k, NZ)}, device_id_type=MESH)
    for k in range(1, NY):
        pl.semaphore_signal(barrier, inc=1, device_id={"mem": lax.rem(y + k, NY)}, device_id_type=MESH)

    def tables():
        tab_ref[...] = jnp.zeros_like(tab_ref)
        tab_ref[0:3, :] = table_ref[...]
        table = tab_ref[...]
        high = table.astype(BF16)
        rest = table - high.astype(F32)
        middle = rest.astype(BF16)
        w2 = w2_ref[...]
        dims = (((1,), (0,)), ((), ()))
        q_ref[...] = lax.dot_general(high, w2, dims, preferred_element_type=F32) + lax.dot_general(
            middle, w2, dims, preferred_element_type=F32
        )
        square_ref[...] = jnp.zeros_like(square_ref)
        square_ref[0:ROWS, :] = types_ref[...].astype(F32)
        turned = square_ref[...].T
        for r in range(ROWS):
            tcol_ref[r * COLS : (r + 1) * COLS, :] = jnp.broadcast_to(turned[:, r : r + 1], (COLS, LANES))

    for copy in smalls:
        copy.wait()
    gain = gain_ref[...]
    bias = bias_ref[...]

    def normalise(i):
        rows = chunk_rows(i)
        loads[i].wait()
        xf = x_ref[rows, :].astype(F32)
        inv = lax.rsqrt(jnp.mean(xf * xf, axis=-1, keepdims=True) + 1e-05)
        inv_ref[rows, :] = jnp.broadcast_to(inv, (CHUNK, LANES))
        n_ref[rows, :] = (xf * inv * gain).astype(BF16)

    def first_dot(i):
        rows = chunk_rows(i)
        v_ref[rows, :] = jnp.dot(n_ref[rows, :], w1_ref[...], preferred_element_type=F32)

    kind = lax.broadcasted_iota(jnp.int32, (16, COLS), 0)

    def activate(i):
        rows = chunk_rows(i)
        p = v_ref[rows, :] + bias
        act = (p * (0.5 * jnp.tanh(0.5 * p) + 0.5)).astype(BF16)
        left = kind == types_ref[2 * i : 2 * i + 1, :]
        right = (kind - 8) == types_ref[2 * i + 1 : 2 * i + 2, :]
        onehot = jnp.concatenate([left.astype(F32), right.astype(F32)], axis=1).astype(BF16)
        s_ref[i * 16 : (i + 1) * 16, :] = jnp.dot(onehot, act, preferred_element_type=F32)

    normalise(0)
    for copy in wloads:
        copy.wait()
    for i in range(NCHUNK):
        first_dot(i)
        if i + 1 < NCHUNK:
            normalise(i + 1)
        if i == 0:
            tables()
        if i >= 1:
            activate(i - 1)
    activate(NCHUNK - 1)

    lanes16 = lax.broadcasted_iota(jnp.int32, (16, LANES), 1)
    subs16 = lax.broadcasted_iota(jnp.int32, (16, LANES), 0)
    diagonal = lanes16 == subs16
    net = jnp.sum(s_ref[...].reshape(ROWS, 8, D) * q_ref[...][None], axis=1)
    net = jnp.sum(net, axis=1, keepdims=True)
    net = jnp.concatenate([net, jnp.zeros((16 - ROWS, 1), F32)], axis=0)
    net = jnp.sum(jnp.where(diagonal, net, 0.0), axis=0, keepdims=True)
    mine_ref[...] = jnp.zeros_like(mine_ref)
    mine_ref[0:1, 0:ROWS] = band_ref[...].astype(F32)
    mine_ref[1:2, 0:ROWS] = target_ref[...]
    lane1 = lax.broadcasted_iota(jnp.int32, (1, LANES), 1)
    coslat = jnp.cos(math.pi * (mine_ref[0:1, :] / 720.0 - 0.5))
    coslat = jnp.where(lane1 < ROWS, coslat, 0.0)
    mine_ref[0:1, :] = coslat * net * (1.0 / (NLON * COLS))

    pl.semaphore_wait(barrier, (NLON - 1) + (NZ - 1) + (NY - 1))
    sent = []

    def launch(copy):
        copy.start()
        sent.append(copy)
        return copy

    by_distance = (4, 3, 5, 2, 6, 1, 7)
    ex1 = [
        launch(remote(mine_ref, ex1_ref.at[lon], ex1_s.at[k - 1], ex1_r.at[k - 1], lon=lax.rem(lon + k, NLON)))
        for k in by_distance
    ]
    ex1_ref[lon] = mine_ref[...]

    def unscaled(i):
        rows = chunk_rows(i)
        kinds = tcol_ref[rows, :]
        is_one = kinds == 1.0
        is_two = kinds == 2.0
        inner = jnp.zeros((CHUNK, LANES), F32)
        for tile in range(TILES):
            cols = slice(tile * LANES, (tile + 1) * LANES)
            before = v_ref[rows, cols]
            p = before + bias_ref[0:1, cols]
            sigma = 0.5 * jnp.tanh(0.5 * p) + 0.5
            slope = sigma + (p * sigma) * (1.0 - sigma)
            weight = jnp.where(is_one, q_ref[1:2, cols], jnp.where(is_two, q_ref[2:3, cols], q_ref[0:1, cols]))
            grad = slope * weight
            inner += grad * before
            b_ref[2 * i : 2 * i + 2, cols] = jnp.sum(grad.reshape(2, COLS, LANES), axis=1)
            u_ref[rows, cols] = grad.astype(BF16)
        inv = inv_ref[rows, :]
        inner = jnp.sum(inner, axis=1, keepdims=True)
        coef_ref[rows, :] = inv * inv * (inner * (1.0 / D))

    def back(i):
        rows = chunk_rows(i)
        v_ref[rows, :] = lax.dot_general(
            u_ref[rows, :], w1_ref[...], (((1,), (1,)), ((), ())), preferred_element_type=F32
        )

    for i in range(NCHUNK // 2):
        unscaled(i)
        if i >= 1:
            back(i - 1)
    coscol = jnp.sum(jnp.where(diagonal, coslat, 0.0), axis=1, keepdims=True) * (1.0 / (ROWS * NZ))
    for copy in ex1:
        copy.wait_recv()
    sub8 = lax.broadcasted_iota(jnp.int32, (8, LANES), 0)
    lane8 = lax.broadcasted_iota(jnp.int32, (8, LANES), 1)
    line_ref[...] = jnp.where(sub8 == 0, jnp.sum(ex1_ref[...], axis=0), mine_ref[...])
    ex2 = [
        launch(remote(line_ref, ex2_ref.at[z], ex2_s.at[k - 1], ex2_r.at[k - 1], lat=lax.rem(z + k, NZ)))
        for k in by_distance
    ]
    ex2_ref[z] = line_ref[...]
    for i in range(NCHUNK // 2, NCHUNK):
        unscaled(i)
        back(i - 1)
    back(NCHUNK - 1)
    for copy in ex2:
        copy.wait_recv()

    weighted = jnp.concatenate([ex2_ref[k][0:1, :] for k in range(NZ)], axis=0)
    targets = jnp.concatenate([ex2_ref[k][1:2, :] for k in range(NZ)], axis=0)
    count = (ROWS * NZ - ROWS * sub8 - lane8).astype(F32)
    south = jnp.sum(jnp.where(sub8 < z, weighted, 0.0), axis=0, keepdims=True)
    north = jnp.sum(jnp.where(sub8 > z, count * weighted - targets, 0.0), axis=0, keepdims=True)
    here = jnp.sum(jnp.where(sub8 == z, weighted, 0.0), axis=0, keepdims=True)
    goal = jnp.sum(jnp.where(sub8 == z, targets, 0.0), axis=0, keepdims=True)
    left_over = ROWS * NZ - ROWS * z
    both = (left_over - jnp.maximum(subs16, lanes16)).astype(F32) * here
    both = both + (left_over - subs16).astype(F32) * south + north - jnp.where(lanes16 >= subs16, goal, 0.0)
    flux = coscol * jnp.sum(both, axis=1, keepdims=True)
    fb_ref[...] = jnp.broadcast_to(flux, (16, LANES))

    def scale_tile(slot, half, t):
        for way in range(2):
            cols = pl.ds(pl.multiple_of(half * 512 + t * 256 + way * LANES, LANES), LANES)
            for r in range(ROWS):
                rows = pl.ds(r * COLS, COLS)
                p_ref[slot, rows, way * LANES : (way + 1) * LANES] = (
                    u_ref[rows, cols].astype(F32) * fb_ref[r : r + 1, :]
                ).astype(BF16)

    def hidden_tile(ref, slot, t):
        tile = contract(n_ref[...], p_ref[slot])
        for way in range(2):
            ref[t, way] = tile[:, way * LANES : (way + 1) * LANES].reshape(NY, NX, 64, LANES)

    sibling = x * 2 + 1 - core
    tiles = ((give_ref, 1 - core, 0), (own_ref, core, 0), (give_ref, 1 - core, 1), (own_ref, core, 1))

    def place(way):
        return y if way == 0 else x

    def toward(way, step):
        if way == 0:
            return {"mem": lax.rem(y + step, NY)}
        return {"lon": lon_at(step)}

    def half(t, way, owner, which):
        rows = pl.ds(32 * which, 32)
        return own_ref.at[t, way, owner, :, rows] if way == 0 else own_ref.at[t, way, :, owner, rows]

    passes, plains, aggs = {}, {}, {}

    def hop(table, t, way, which, step, owner, target, sem):
        table[t, way, which] = launch(
            remote(
                half(t, way, owner, which),
                target.at[t, way, which],
                first_s.at[t, way, sem],
                first_r.at[t, way, sem],
                **toward(way, step),
            )
        )

    def first(t):
        to_core[t].wait_recv()
        own_ref[t] = own_ref[t] + take_ref[t]
        for way in range(2):
            opposite = lax.rem(place(way) + 2, 4)
            hop(passes, t, way, 0, 1, opposite, pass_ref, 0)
            hop(passes, t, way, 1, 3, opposite, pass_ref, 1)
        for way in range(2):
            hop(plains, t, way, 1, 1, lax.rem(place(way) + 1, 4), plain_ref, 2)
            hop(plains, t, way, 0, 3, lax.rem(place(way) + 3, 4), plain_ref, 3)

    def ring(t):
        for way in range(2):
            for which, step in ((0, 1), (1, 3)):
                owner = lax.rem(place(way) + step, 4)
                passes[t, way, which].wait_recv()
                mid = half(t, way, owner, which)
                mid[...] = mid[...] + pass_ref[t, way, which]
                hop(aggs, t, way, which, step, owner, agg_ref, 4 + which)

    to_core = []
    scale_tile(0, *tiles[0][1:])
    for slot in range(4):
        ref, _, t = tiles[slot]
        hidden_tile(ref, slot, t)
        if ref is give_ref:
            to_core.append(
                launch(remote(give_ref.at[t], take_ref.at[t], core_s.at[t], core_r.at[t], lon=sibling))
            )
        if slot < 3:
            scale_tile(slot + 1, *tiles[slot + 1][1:])
        if slot == 2:
            pass
            first(0)
    first(1)

    gacc_ref[...] = jnp.zeros_like(gacc_ref)

    def latent_grad(i):
        rows = chunk_rows(i)
        flux = jnp.concatenate(
            [jnp.broadcast_to(fb_ref[2 * i + k : 2 * i + k + 1, :], (COLS, LANES)) for k in range(2)], axis=0
        )
        inv = inv_ref[rows, :] * flux
        coef = coef_ref[rows, :] * flux
        for tile in range(TILES):
            cols = slice(tile * LANES, (tile + 1) * LANES)
            xf = x_ref[rows, cols].astype(F32)
            scaled = v_ref[rows, cols] * inv
            gacc_ref[:, cols] += jnp.sum((scaled * xf).reshape(CHUNK // 8, 8, LANES), axis=0)
            outlat_ref[rows, cols] = (scaled * gain_ref[0:1, cols] - xf * coef).astype(BF16)

    for i in range(NCHUNK):
        latent_grad(i)

    small = jnp.zeros((8, D), F32)
    bias_sum = jnp.zeros((1, D), F32)
    for r in range(ROWS):
        scale = fb_ref[r : r + 1, 0:1]
        small = small + s_ref[r * 8 : (r + 1) * 8, :] * scale
        bias_sum = bias_sum + b_ref[r : r + 1, :] * scale
    gain_sum = jnp.sum(gacc_ref[...], axis=0, keepdims=True)
    row8 = lax.broadcasted_iota(jnp.int32, (8, D), 0)
    small = jnp.where(row8 == 3, bias_sum, jnp.where(row8 == 4, gain_sum, small))
    for k in range(NLON):
        sm_ref[k] = small[:, k * LANES : (k + 1) * LANES]
    sm1 = []
    for k in range(1, NLON):
        peer = lax.rem(lon + k, NLON)
        sm1.append(launch(remote(sm_ref.at[peer], sm1_ref.at[lon], sm1_s.at[k - 1], sm1_r.at[k - 1], lon=peer)))
    sm1_ref[lon] = sm_ref[lon]

    crosses, depths, agz = {}, {}, {}

    def cross(t):
        for way in range(2):
            for which in range(2):
                plains[t, way, which].wait_recv()
                aggs[t, way, which].wait_recv()
                part_ref[t, way, :, 32 * which : 32 * (which + 1)] = (
                    half(t, way, place(way), which)[...] + plain_ref[t, way, which] + agg_ref[t, way, which]
                )
            other = 1 - way
            for k in (2, 1, 3):
                crosses[t, way, k] = launch(
                    remote(
                        part_ref.at[t, way, lax.rem(place(other) + k, 4)],
                        cross_ref.at[t, way, k - 1],
                        cross_s.at[t, way, k - 1],
                        cross_r.at[t, way, k - 1],
                        **toward(other, k),
                    )
                )

    def deepen(t):
        for way in range(2):
            for k in range(1, 4):
                crosses[t, way, k].wait_recv()
            piece = part_ref[t, way, place(1 - way)] + cross_ref[t, way, 0] + cross_ref[t, way, 1] + cross_ref[t, way, 2]
            piece_ref[t, :, way] = piece.reshape(NZ, 8, LANES)
        for k in by_distance:
            peer = lax.rem(z + k, NZ)
            depths[t, k] = launch(
                remote(
                    piece_ref.at[t, peer], depth_ref.at[t, k - 1], depth_s.at[t, k - 1], depth_r.at[t, k - 1], lat=peer
                )
            )

    slots = (0, 1, 7, 2, 6, 3, 5, 4)
    slot_of = {k: slots.index(k) for k in range(NZ)}

    def finish(t):
        for k in range(1, NZ):
            depths[t, k].wait_recv()
        piece = piece_ref[t, z]
        for k in range(NZ - 1):
            piece = piece + depth_ref[t, k]
        hid_ref[core, t, x, 0] = piece
        for k in by_distance:
            agz[t, k] = launch(
                remote(
                    hid_ref.at[core, t, x, 0],
                    hid_ref.at[core, t, x, slot_of[NZ - k]],
                    agz_s.at[t, k - 1],
                    agz_r.at[t, k - 1],
                    lat=lax.rem(z + k, NZ),
                )
            )

    groups = (((0, 5), (5, 8)), ((0, 5), (5, 8)))
    agx, agc = {}, {}

    def spread(t, g):
        start, stop = groups[t][g]
        for k in range(1, NZ):
            if start <= slot_of[NZ - k] < stop:
                agz[t, k].wait_recv()
        spot = hid_ref.at[core, t, x, pl.ds(start, stop - start)]
        for k in (2, 1, 3):
            agx[t, g, k] = launch(remote(spot, spot, agx_s.at[t, g, k - 1], agx_r.at[t, g, k - 1], lon=lon_at(k)))
        agc[t, g, 0] = launch(remote(spot, spot, agc_s.at[t, g, 0], agc_r.at[t, g, 0], lon=sibling))

    def to_sibling(t, g):
        start, stop = groups[t][g]
        for k in (1, 3, 2):
            agx[t, g, k].wait_recv()
            spot = hid_ref.at[core, t, lax.rem(x + 4 - k, NX), pl.ds(start, stop - start)]
            agc[t, g, k] = launch(remote(spot, spot, agc_s.at[t, g, k], agc_r.at[t, g, k], lon=sibling))

    def place_rows(half, t):
        for xi in range(NX):
            for k in range(NZ):
                rows = pl.ds(pl.multiple_of(xi * 64 + lax.rem(z + k, NZ) * 8, 8), 8)
                for way in range(2):
                    cols = pl.ds(pl.multiple_of(half * 512 + t * 256 + way * LANES, LANES), LANES)
                    outhid_ref[rows, cols] = hid_ref[half, t, xi, slot_of[k], way]

    def drain(count):
        for copy in sent[:count]:
            copy.wait_send()
        del sent[:count]

    ring(0)
    ring(1)
    drain(len(ex1) + len(ex2) + len(to_core))
    cross(0)
    cross(1)
    for copy in sm1:
        copy.wait_recv()
    t1_ref[...] = jnp.sum(sm1_ref[...], axis=0)
    sm2 = [
        launch(remote(t1_ref, sm2_ref.at[z], sm2_s.at[k - 1], sm2_r.at[k - 1], lat=lax.rem(z + k, NZ)))
        for k in by_distance
    ]
    sm2_ref[z] = t1_ref[...]
    drain(len(passes) + len(plains) + len(sm1) + len(aggs))
    deepen(0)
    deepen(1)
    for copy in sm2:
        copy.wait_recv()
    t2_ref[...] = jnp.sum(sm2_ref[...], axis=0)
    sm3 = [
        launch(remote(t2_ref, sm3_ref.at[y], sm3_s.at[k - 1], sm3_r.at[k - 1], mem=lax.rem(y + k, NY)))
        for k in range(1, NY)
    ]
    sm3_ref[y] = t2_ref[...]
    drain(len(crosses) + len(sm2))
    finish(0)
    finish(1)
    for copy in sm3:
        copy.wait_recv()
    smo_ref[lon] = jnp.sum(sm3_ref[...], axis=0)
    sm4 = [
        launch(remote(smo_ref.at[lon], smo_ref.at[lon], sm4_s.at[k - 1], sm4_r.at[k - 1], lon=lax.rem(lon + k, NLON)))
        for k in by_distance
    ]
    drain(len(depths) + len(sm3))
    spread(0, 0)
    spread(0, 1)
    spread(1, 0)
    spread(1, 1)
    for copy in sm4:
        copy.wait_recv()
    summed = jnp.concatenate([smo_ref[k] for k in range(NLON)], axis=1)
    outbias_ref[...] = summed[3:4, :]
    outgain_ref[...] = summed[4:5, :]
    outw_ref[...] = lax.dot_general(
        tab_ref[...], summed, (((0,), (0,)), ((), ())), precision=HIGH, preferred_element_type=F32
    )
    drain(len(agz) + len(sm4))
    to_sibling(0, 0)
    to_sibling(0, 1)
    place_rows(core, 0)
    to_sibling(1, 0)
    to_sibling(1, 1)
    place_rows(core, 1)
    drain(len(agx))
    for g in range(2):
        for k in range(4):
            agc[0, g, k].wait_recv()
    place_rows(1 - core, 0)
    drain(len(sent))
    for g in range(2):
        for k in range(4):
            agc[1, g, k].wait_recv()
    place_rows(1 - core, 1)


def write_out(*refs):
    sems = refs[-1]
    half = len(refs) // 2
    copies = []
    for source, target in zip(refs[:half], refs[half:-1]):
        rows = source.shape[0]
        step = min(rows, 256 if source.dtype == BF16 else 64)
        for start in range(0, rows - rows % step, step):
            part = pl.ds(start, step) if step < rows else slice(None)
            copies.append(pltpu.make_async_copy(source.at[part], target.at[part], sems.at[len(copies)]))
        if rows % step:
            part = pl.ds(rows - rows % step, rows % step)
            copies.append(pltpu.make_async_copy(source.at[part], target.at[part], sems.at[len(copies)]))
    for copy in copies:
        copy.start()
    for copy in copies:
        copy.wait()


def on_device(latent, norm_gain, hidden_weight, hidden_bias, output_weight, flux_table, target, land_sea, band_index):
    vmem = pl.BlockSpec(memory_space=pltpu.VMEM)
    hbm = pl.BlockSpec(memory_space=pl.ANY)
    dma = pltpu.SemaphoreType.DMA
    scratch = [
        pltpu.VMEM((CELLS, D), BF16),
        pltpu.VMEM((D, D), BF16),
        pltpu.VMEM((1, D), F32),
        pltpu.VMEM((1, D), F32),
        pltpu.VMEM((80, D), BF16),
        pltpu.VMEM((3, 80), F32),
        pltpu.VMEM((1, ROWS), F32),
        pltpu.VMEM((ROWS, COLS), jnp.int32),
        pltpu.VMEM((1, ROWS), jnp.int32),
        pltpu.VMEM((CELLS, D), BF16),
        pltpu.VMEM((CELLS, D), F32),
        pltpu.VMEM((CELLS, D), BF16),
        pltpu.VMEM((4, CELLS, 256), BF16),
        pltpu.VMEM((CELLS, LANES), F32),
        pltpu.VMEM((CELLS, LANES), F32),
        pltpu.VMEM((CELLS, LANES), F32),
        pltpu.VMEM((LANES, LANES), F32),
        pltpu.VMEM((8, D), F32),
        pltpu.VMEM((8, 80), F32),
        pltpu.VMEM((ROWS * 8, D), F32),
        pltpu.VMEM((16, D), F32),
        pltpu.VMEM((16, LANES), F32),
        pltpu.VMEM((8, D), F32),
        pltpu.VMEM((8, LANES), F32),
        pltpu.VMEM((NLON, 8, LANES), F32),
        pltpu.VMEM((8, LANES), F32),
        pltpu.VMEM((NZ, 8, LANES), F32),
        pltpu.VMEM((2, 2, NY, NX, 64, LANES), F32),
        pltpu.VMEM((2, 2, NY, NX, 64, LANES), F32),
        pltpu.VMEM((2, 2, NY, NX, 64, LANES), F32),
        pltpu.VMEM((2, 2, 2, 4, 32, LANES), F32),
        pltpu.VMEM((2, 2, 2, 4, 32, LANES), F32),
        pltpu.VMEM((2, 2, 2, 4, 32, LANES), F32),
        pltpu.VMEM((2, 2, 4, 64, LANES), F32),
        pltpu.VMEM((2, 2, 3, 64, LANES), F32),
        pltpu.VMEM((2, NZ, 2, 8, LANES), F32),
        pltpu.VMEM((2, NZ - 1, 2, 8, LANES), F32),
        pltpu.VMEM((2, 2, NX, NZ, 2, 8, LANES), F32),
        pltpu.VMEM((NLON, 8, LANES), F32),
        pltpu.VMEM((NLON, 8, LANES), F32),
        pltpu.VMEM((8, LANES), F32),
        pltpu.VMEM((NZ, 8, LANES), F32),
        pltpu.VMEM((8, LANES), F32),
        pltpu.VMEM((NY, 8, LANES), F32),
        pltpu.VMEM((NLON, 8, LANES), F32),
        dma((NCHUNK,)),
        dma((4,)),
        dma((7,)),
        dma((7,)), dma((7,)),
        dma((7,)), dma((7,)),
        dma((2,)), dma((2,)),
        dma((2, 2, 6)), dma((2, 2, 6)),
        dma((2, 2, 3)), dma((2, 2, 3)),
        dma((2, 7)), dma((2, 7)),
        dma((2, 7)), dma((2, 7)),
        dma((2, 2, 3)), dma((2, 2, 3)),
        dma((2, 2, 4)), dma((2, 2, 4)),
        dma((7,)), dma((7,)),
        dma((7,)), dma((7,)),
        dma((3,)), dma((3,)),
        dma((7,)), dma((7,)),
    ]
    shapes = (((CELLS, D), BF16), ((D // NY, D), F32), ((80, D), F32), ((1, D), F32), ((1, D), F32))
    held = pl.pallas_call(
        kernel,
        out_shape=tuple(pltpu.VMEM(*shape) for shape in shapes),
        in_specs=[hbm] * 9,
        out_specs=(vmem,) * 5,
        scratch_shapes=scratch,
        compiler_params=pltpu.CompilerParams(
            collective_id=0, has_side_effects=True, vmem_limit_bytes=56 * 1024 * 1024
        ),
        cost_estimate=pl.CostEstimate(flops=10_000_000_000, bytes_accessed=9_000_000, transcendentals=3_000_000),
    )(
        latent.reshape(CELLS, D),
        norm_gain.reshape(1, D),
        hidden_weight,
        hidden_bias.reshape(1, D),
        output_weight.T,
        flux_table,
        target,
        land_sea,
        band_index.reshape(1, ROWS),
    )
    grad_cells, grad_hidden, grad_out, grad_gain, grad_bias = pl.pallas_call(
        write_out,
        out_shape=tuple(jax.ShapeDtypeStruct(*shape) for shape in shapes),
        in_specs=[vmem] * 5,
        out_specs=(hbm,) * 5,
        scratch_shapes=[dma((16,))],
        compiler_params=pltpu.CompilerParams(vmem_limit_bytes=1024 * 1024),
    )(*[pltpu.with_memory_space_constraint(array, pltpu.VMEM) for array in held])
    return (
        grad_cells.reshape(latent.shape),
        grad_hidden,
        grad_out.T,
        grad_gain.reshape(D),
        grad_bias.reshape(D),
    )


def solution(mesh):
    return jax.shard_map(
        on_device,
        mesh=mesh,
        in_specs=(
            P("mem", "lat", "lon", None),
            P(),
            P(),
            P(),
            P(),
            P(),
            P("mem", "lat"),
            P("lat", "lon"),
            P("lat"),
        ),
        out_specs=(P("mem", "lat", "lon", None), P("mem", None), P(), P(), P()),
        check_vma=False,
    )
```

```python
import functools
import math

import jax
import jax.numpy as jnp
from jax import lax
from jax.experimental import pallas as pl
from jax.experimental.pallas import tpu as pltpu
from jax.sharding import PartitionSpec as P

MESH = pl.DeviceIdType.MESH
F32 = jnp.float32
BF16 = jnp.bfloat16
HIGH = lax.Precision.HIGHEST

CELLS = 1536
ROWS = 12
COLS = 128
D = 1024
CHUNK = 256
NCHUNK = CELLS // CHUNK
LANES = 128
TILES = D // LANES
NX, NY, NZ, NLON = 4, 4, 8, 8


def remote(src, dst, send_sem, recv_sem, **where):
    return pltpu.make_async_remote_copy(
        src_ref=src,
        dst_ref=dst,
        send_sem=send_sem,
        recv_sem=recv_sem,
        device_id=where,
        device_id_type=MESH,
    )


def contract(left, right):
    return lax.dot_general(left, right, (((0,), (0,)), ((), ())), preferred_element_type=F32)


def kernel(
    lat_hbm, gain_hbm, w1_hbm, bias_hbm, w2_hbm, table_hbm, target_hbm, types_hbm, band_hbm,
    outlat_ref, outhid_ref, outw_ref, outgain_ref, outbias_ref,
    x_ref, w1_ref, gain_ref, bias_ref, w2_ref, table_ref, target_ref, types_ref, band_ref,
    n_ref, v_ref, u_ref, p_ref, inv_ref, coef_ref, tcol_ref, square_ref,
    q_ref, tab_ref, s_ref, b_ref, fb_ref, gacc_ref, mine_ref, ex1_ref, line_ref, ex2_ref,
    give_ref, take_ref, own_ref, pass_ref, plain_ref, agg_ref, part_ref, cross_ref, piece_ref, depth_ref,
    hid_ref, sm_ref, sm1_ref, t1_ref, sm2_ref, t2_ref, sm3_ref, smo_ref,
    xsem, wsem, insem, ex1_s, ex1_r, ex2_s, ex2_r, core_s, core_r, first_s, first_r, cross_s, cross_r, depth_s, depth_r,
    agz_s, agz_r, agx_s, agx_r, agc_s, agc_r, sm1_s, sm1_r, sm2_s, sm2_r, sm3_s, sm3_r, sm4_s, sm4_r,
):
    z = lax.axis_index("lat")
    lon = lax.axis_index("lon")
    y = lax.axis_index("mem")
    x = lon // 2
    core = lon % 2

    def lon_at(step):
        return lax.rem(x + step, NX) * 2 + core

    def chunk_rows(i):
        return pl.ds(i * CHUNK, CHUNK)

    loads = [pltpu.make_async_copy(lat_hbm.at[chunk_rows(i)], x_ref.at[chunk_rows(i)], xsem.at[i]) for i in range(NCHUNK)]
    wloads = [
        pltpu.make_async_copy(w1_hbm.at[pl.ds(i * 256, 256)], w1_ref.at[pl.ds(i * 256, 256)], wsem.at[i]) for i in range(4)
    ]
    smalls = [
        pltpu.make_async_copy(source, target, insem.at[i])
        for i, (source, target) in enumerate(
            (
                (w2_hbm, w2_ref),
                (types_hbm, types_ref),
                (table_hbm, table_ref),
                (gain_hbm, gain_ref),
                (bias_hbm, bias_ref),
                (band_hbm, band_ref),
                (target_hbm, target_ref),
            )
        )
    ]
    loads[0].start()
    for copy in smalls:
        copy.start()
    for copy in wloads:
        copy.start()
    for i in range(1, NCHUNK):
        loads[i].start()

    barrier = pltpu.get_barrier_semaphore()
    for k in range(1, NLON):
        pl.semaphore_signal(barrier, inc=1, device_id={"lon": lax.rem(lon + k, NLON)}, device_id_type=MESH)
    for k in range(1, NZ):
        pl.semaphore_signal(barrier, inc=1, device_id={"lat": lax.rem(z + k, NZ)}, device_id_type=MESH)
    for k in range(1, NY):
        pl.semaphore_signal(barrier, inc=1, device_id={"mem": lax.rem(y + k, NY)}, device_id_type=MESH)

    def tables():
        tab_ref[...] = jnp.zeros_like(tab_ref)
        tab_ref[0:3, :] = table_ref[...]
        table = tab_ref[...]
        high = table.astype(BF16)
        rest = table - high.astype(F32)
        middle = rest.astype(BF16)
        w2 = w2_ref[...]
        dims = (((1,), (0,)), ((), ()))
        q_ref[...] = lax.dot_general(high, w2, dims, preferred_element_type=F32) + lax.dot_general(
            middle, w2, dims, preferred_element_type=F32
        )
        square_ref[...] = jnp.zeros_like(square_ref)
        square_ref[0:ROWS, :] = types_ref[...].astype(F32)
        turned = square_ref[...].T
        for r in range(ROWS):
            tcol_ref[r * COLS : (r + 1) * COLS, :] = jnp.broadcast_to(turned[:, r : r + 1], (COLS, LANES))

    for copy in smalls:
        copy.wait()
    gain = gain_ref[...]
    bias = bias_ref[...]

    def normalise(i):
        rows = chunk_rows(i)
        xf = x_ref[rows, :].astype(F32)
        inv = lax.rsqrt(jnp.mean(xf * xf, axis=-1, keepdims=True) + 1e-05)
        inv_ref[rows, :] = jnp.broadcast_to(inv, (CHUNK, LANES))
        n_ref[rows, :] = (xf * inv * gain).astype(BF16)

    def first_dot(i):
        rows = chunk_rows(i)
        v_ref[rows, :] = jnp.dot(n_ref[rows, :], w1_ref[...], preferred_element_type=F32)

    kind = lax.broadcasted_iota(jnp.int32, (16, COLS), 0)

    def activate(i):
        rows = chunk_rows(i)
        p = v_ref[rows, :] + bias
        act = (p * (0.5 * jnp.tanh(0.5 * p) + 0.5)).astype(BF16)
        left = kind == types_ref[2 * i : 2 * i + 1, :]
        right = (kind - 8) == types_ref[2 * i + 1 : 2 * i + 2, :]
        onehot = jnp.concatenate([left.astype(F32), right.astype(F32)], axis=1).astype(BF16)
        s_ref[i * 16 : (i + 1) * 16, :] = jnp.dot(onehot, act, preferred_element_type=F32)

    loads[0].wait()
    normalise(0)
    for copy in wloads:
        copy.wait()
    for i in range(NCHUNK):
        if i + 1 < NCHUNK:
            loads[i + 1].wait()
        first_dot(i)
        if i + 1 < NCHUNK:
            normalise(i + 1)
        if i == 0:
            tables()
        if i >= 1:
            activate(i - 1)
    activate(NCHUNK - 1)

    lanes16 = lax.broadcasted_iota(jnp.int32, (16, LANES), 1)
    subs16 = lax.broadcasted_iota(jnp.int32, (16, LANES), 0)
    diagonal = lanes16 == subs16
    net = jnp.sum(s_ref[...].reshape(ROWS, 8, D) * q_ref[...][None], axis=1)
    net = jnp.sum(net, axis=1, keepdims=True)
    net = jnp.concatenate([net, jnp.zeros((16 - ROWS, 1), F32)], axis=0)
    net = jnp.sum(jnp.where(diagonal, net, 0.0), axis=0, keepdims=True)
    mine_ref[...] = jnp.zeros_like(mine_ref)
    mine_ref[0:1, 0:ROWS] = band_ref[...].astype(F32)
    mine_ref[1:2, 0:ROWS] = target_ref[...]
    lane1 = lax.broadcasted_iota(jnp.int32, (1, LANES), 1)
    coslat = jnp.cos(math.pi * (mine_ref[0:1, :] / 720.0 - 0.5))
    coslat = jnp.where(lane1 < ROWS, coslat, 0.0)
    mine_ref[0:1, :] = coslat * net * (1.0 / (NLON * COLS))

    pl.semaphore_wait(barrier, (NLON - 1) + (NZ - 1) + (NY - 1))
    sent = []

    def launch(copy):
        copy.start()
        sent.append(copy)
        return copy

    by_distance = (4, 3, 5, 2, 6, 1, 7)
    ex1 = [
        launch(remote(mine_ref, ex1_ref.at[lon], ex1_s.at[k - 1], ex1_r.at[k - 1], lon=lax.rem(lon + k, NLON)))
        for k in by_distance
    ]
    ex1_ref[lon] = mine_ref[...]

    def unscaled(i):
        rows = chunk_rows(i)
        kinds = tcol_ref[rows, :]
        is_one = kinds == 1.0
        is_two = kinds == 2.0
        inner = jnp.zeros((CHUNK, LANES), F32)
        for tile in range(TILES):
            cols = slice(tile * LANES, (tile + 1) * LANES)
            before = v_ref[rows, cols]
            p = before + bias_ref[0:1, cols]
            sigma = 0.5 * jnp.tanh(0.5 * p) + 0.5
            slope = sigma + (p * sigma) * (1.0 - sigma)
            weight = jnp.where(is_one, q_ref[1:2, cols], jnp.where(is_two, q_ref[2:3, cols], q_ref[0:1, cols]))
            grad = slope * weight
            inner += grad * before
            b_ref[2 * i : 2 * i + 2, cols] = jnp.sum(grad.reshape(2, COLS, LANES), axis=1)
            u_ref[rows, cols] = grad.astype(BF16)
        inv = inv_ref[rows, :]
        inner = jnp.sum(inner, axis=1, keepdims=True)
        coef_ref[rows, :] = inv * inv * (inner * (1.0 / D))

    def back(i):
        rows = chunk_rows(i)
        v_ref[rows, :] = lax.dot_general(
            u_ref[rows, :], w1_ref[...], (((1,), (1,)), ((), ())), preferred_element_type=F32
        )

    for i in range(NCHUNK // 2):
        unscaled(i)
        if i >= 1:
            back(i - 1)
    coscol = jnp.sum(jnp.where(diagonal, coslat, 0.0), axis=1, keepdims=True) * (1.0 / (ROWS * NZ))
    for copy in ex1:
        copy.wait_recv()
    sub8 = lax.broadcasted_iota(jnp.int32, (8, LANES), 0)
    lane8 = lax.broadcasted_iota(jnp.int32, (8, LANES), 1)
    line_ref[...] = jnp.where(sub8 == 0, jnp.sum(ex1_ref[...], axis=0), mine_ref[...])
    ex2 = [
        launch(remote(line_ref, ex2_ref.at[z], ex2_s.at[k - 1], ex2_r.at[k - 1], lat=lax.rem(z + k, NZ)))
        for k in by_distance
    ]
    ex2_ref[z] = line_ref[...]
    for i in range(NCHUNK // 2, NCHUNK):
        unscaled(i)
        back(i - 1)
    back(NCHUNK - 1)
    for copy in ex2:
        copy.wait_recv()

    weighted = jnp.concatenate([ex2_ref[k][0:1, :] for k in range(NZ)], axis=0)
    targets = jnp.concatenate([ex2_ref[k][1:2, :] for k in range(NZ)], axis=0)
    count = (ROWS * NZ - ROWS * sub8 - lane8).astype(F32)
    south = jnp.sum(jnp.where(sub8 < z, weighted, 0.0), axis=0, keepdims=True)
    north = jnp.sum(jnp.where(sub8 > z, count * weighted - targets, 0.0), axis=0, keepdims=True)
    here = jnp.sum(jnp.where(sub8 == z, weighted, 0.0), axis=0, keepdims=True)
    goal = jnp.sum(jnp.where(sub8 == z, targets, 0.0), axis=0, keepdims=True)
    left_over = ROWS * NZ - ROWS * z
    both = (left_over - jnp.maximum(subs16, lanes16)).astype(F32) * here
    both = both + (left_over - subs16).astype(F32) * south + north - jnp.where(lanes16 >= subs16, goal, 0.0)
    flux = coscol * jnp.sum(both, axis=1, keepdims=True)
    fb_ref[...] = jnp.broadcast_to(flux, (16, LANES))

    def scale_tile(slot, half, t):
        for way in range(2):
            cols = pl.ds(pl.multiple_of(half * 512 + t * 256 + way * LANES, LANES), LANES)
            for r in range(ROWS):
                rows = pl.ds(r * COLS, COLS)
                p_ref[slot, rows, way * LANES : (way + 1) * LANES] = (
                    u_ref[rows, cols].astype(F32) * fb_ref[r : r + 1, :]
                ).astype(BF16)

    def hidden_tile(ref, slot, t, part):
        tile = contract(n_ref[:, part * 512 : (part + 1) * 512], p_ref[slot])
        for way in range(2):
            ref[t, way, 2 * part : 2 * part + 2] = tile[:, way * LANES : (way + 1) * LANES].reshape(2, NX, 64, LANES)

    sibling = x * 2 + 1 - core
    tiles = ((give_ref, 1 - core, 0), (own_ref, core, 0), (give_ref, 1 - core, 1), (own_ref, core, 1))

    def place(way):
        return y if way == 0 else x

    def toward(way, step):
        if way == 0:
            return {"mem": lax.rem(y + step, NY)}
        return {"lon": lon_at(step)}

    def half(t, way, owner, which):
        rows = pl.ds(32 * which, 32)
        return own_ref.at[t, way, owner, :, rows] if way == 0 else own_ref.at[t, way, :, owner, rows]

    passes, plains, aggs = {}, {}, {}

    def hop(table, t, way, which, step, owner, target, sem):
        table[t, way, which] = launch(
            remote(
                half(t, way, owner, which),
                target.at[t, way, which],
                first_s.at[t, way, sem],
                first_r.at[t, way, sem],
                **toward(way, step),
            )
        )

    def first(t):
        for part in range(2):
            to_core[t, part].wait_recv()
        own_ref[t] = own_ref[t] + take_ref[t]
        for way in range(2):
            opposite = lax.rem(place(way) + 2, 4)
            hop(passes, t, way, 0, 1, opposite, pass_ref, 0)
            hop(passes, t, way, 1, 3, opposite, pass_ref, 1)
        for way in range(2):
            hop(plains, t, way, 1, 1, lax.rem(place(way) + 1, 4), plain_ref, 2)
            hop(plains, t, way, 0, 3, lax.rem(place(way) + 3, 4), plain_ref, 3)

    def ring(t):
        for way in range(2):
            for which, step in ((0, 1), (1, 3)):
                owner = lax.rem(place(way) + step, 4)
                passes[t, way, which].wait_recv()
                mid = half(t, way, owner, which)
                mid[...] = mid[...] + pass_ref[t, way, which]
                hop(aggs, t, way, which, step, owner, agg_ref, 4 + which)

    to_core = {}
    scale_tile(0, *tiles[0][1:])
    for slot in range(4):
        ref, _, t = tiles[slot]
        for part in range(2):
            hidden_tile(ref, slot, t, part)
            if part == 0 and slot < 3:
                scale_tile(slot + 1, *tiles[slot + 1][1:])
            if ref is give_ref:
                y_half = pl.ds(2 * part, 2)
                to_core[t, part] = launch(
                    remote(
                        give_ref.at[t, :, y_half],
                        take_ref.at[t, :, y_half],
                        core_s.at[t, part],
                        core_r.at[t, part],
                        lon=sibling,
                    )
                )
        if slot == 2:
            first(0)
    first(1)

    gacc_ref[...] = jnp.zeros_like(gacc_ref)

    def latent_grad(i):
        rows = chunk_rows(i)
        flux = jnp.concatenate(
            [jnp.broadcast_to(fb_ref[2 * i + k : 2 * i + k + 1, :], (COLS, LANES)) for k in range(2)], axis=0
        )
        inv = inv_ref[rows, :] * flux
        coef = coef_ref[rows, :] * flux
        for tile in range(TILES):
            cols = slice(tile * LANES, (tile + 1) * LANES)
            xf = x_ref[rows, cols].astype(F32)
            scaled = v_ref[rows, cols] * inv
            gacc_ref[:, cols] += jnp.sum((scaled * xf).reshape(CHUNK // 8, 8, LANES), axis=0)
            outlat_ref[rows, cols] = (scaled * gain_ref[0:1, cols] - xf * coef).astype(BF16)

    for i in range(NCHUNK):
        latent_grad(i)

    small = jnp.zeros((8, D), F32)
    bias_sum = jnp.zeros((1, D), F32)
    for r in range(ROWS):
        scale = fb_ref[r : r + 1, 0:1]
        small = small + s_ref[r * 8 : (r + 1) * 8, :] * scale
        bias_sum = bias_sum + b_ref[r : r + 1, :] * scale
    gain_sum = jnp.sum(gacc_ref[...], axis=0, keepdims=True)
    row8 = lax.broadcasted_iota(jnp.int32, (8, D), 0)
    small = jnp.where(row8 == 3, bias_sum, jnp.where(row8 == 4, gain_sum, small))
    for k in range(NLON):
        sm_ref[k] = small[:, k * LANES : (k + 1) * LANES]
    sm1 = []
    for k in range(1, NLON):
        peer = lax.rem(lon + k, NLON)
        sm1.append(launch(remote(sm_ref.at[peer], sm1_ref.at[lon], sm1_s.at[k - 1], sm1_r.at[k - 1], lon=peer)))
    sm1_ref[lon] = sm_ref[lon]

    crosses, depths, agz = {}, {}, {}

    def cross(t):
        for way in range(2):
            for which in range(2):
                plains[t, way, which].wait_recv()
                aggs[t, way, which].wait_recv()
                part_ref[t, way, :, 32 * which : 32 * (which + 1)] = (
                    half(t, way, place(way), which)[...] + plain_ref[t, way, which] + agg_ref[t, way, which]
                )
            other = 1 - way
            for k in (2, 1, 3):
                crosses[t, way, k] = launch(
                    remote(
                        part_ref.at[t, way, lax.rem(place(other) + k, 4)],
                        cross_ref.at[t, way, k - 1],
                        cross_s.at[t, way, k - 1],
                        cross_r.at[t, way, k - 1],
                        **toward(other, k),
                    )
                )

    def deepen(t):
        for way in range(2):
            for k in range(1, 4):
                crosses[t, way, k].wait_recv()
            piece = part_ref[t, way, place(1 - way)] + cross_ref[t, way, 0] + cross_ref[t, way, 1] + cross_ref[t, way, 2]
            piece_ref[t, :, way] = piece.reshape(NZ, 8, LANES)
        for k in by_distance:
            peer = lax.rem(z + k, NZ)
            depths[t, k] = launch(
                remote(
                    piece_ref.at[t, peer], depth_ref.at[t, k - 1], depth_s.at[t, k - 1], depth_r.at[t, k - 1], lat=peer
                )
            )

    slots = (0, 1, 7, 2, 6, 3, 5, 4)
    slot_of = {k: slots.index(k) for k in range(NZ)}

    def finish(t):
        for k in range(1, NZ):
            depths[t, k].wait_recv()
        piece = piece_ref[t, z]
        for k in range(NZ - 1):
            piece = piece + depth_ref[t, k]
        hid_ref[core, t, x, 0] = piece
        for k in by_distance:
            agz[t, k] = launch(
                remote(
                    hid_ref.at[core, t, x, 0],
                    hid_ref.at[core, t, x, slot_of[NZ - k]],
                    agz_s.at[t, k - 1],
                    agz_r.at[t, k - 1],
                    lat=lax.rem(z + k, NZ),
                )
            )

    groups = (((0, 5), (5, 8)), ((0, 5), (5, 8)))
    agx, agc = {}, {}

    def spread(t, g):
        start, stop = groups[t][g]
        for k in range(1, NZ):
            if start <= slot_of[NZ - k] < stop:
                agz[t, k].wait_recv()
        spot = hid_ref.at[core, t, x, pl.ds(start, stop - start)]
        for k in (2, 1, 3):
            agx[t, g, k] = launch(remote(spot, spot, agx_s.at[t, g, k - 1], agx_r.at[t, g, k - 1], lon=lon_at(k)))
        agc[t, g, 0] = launch(remote(spot, spot, agc_s.at[t, g, 0], agc_r.at[t, g, 0], lon=sibling))

    def to_sibling(t, g):
        start, stop = groups[t][g]
        for k in (1, 3, 2):
            agx[t, g, k].wait_recv()
            spot = hid_ref.at[core, t, lax.rem(x + 4 - k, NX), pl.ds(start, stop - start)]
            agc[t, g, k] = launch(remote(spot, spot, agc_s.at[t, g, k], agc_r.at[t, g, k], lon=sibling))

    def place_rows(half, t):
        for xi in range(NX):
            for k in range(NZ):
                rows = pl.ds(pl.multiple_of(xi * 64 + lax.rem(z + k, NZ) * 8, 8), 8)
                for way in range(2):
                    cols = pl.ds(pl.multiple_of(half * 512 + t * 256 + way * LANES, LANES), LANES)
                    outhid_ref[rows, cols] = hid_ref[half, t, xi, slot_of[k], way]

    def drain(count):
        for copy in sent[:count]:
            copy.wait_send()
        del sent[:count]

    ring(0)
    ring(1)
    drain(len(ex1) + len(ex2) + len(to_core))
    cross(0)
    cross(1)
    for copy in sm1:
        copy.wait_recv()
    t1_ref[...] = jnp.sum(sm1_ref[...], axis=0)
    sm2 = [
        launch(remote(t1_ref, sm2_ref.at[z], sm2_s.at[k - 1], sm2_r.at[k - 1], lat=lax.rem(z + k, NZ)))
        for k in by_distance
    ]
    sm2_ref[z] = t1_ref[...]
    drain(len(passes) + len(plains) + len(sm1) + len(aggs))
    deepen(0)
    deepen(1)
    for copy in sm2:
        copy.wait_recv()
    t2_ref[...] = jnp.sum(sm2_ref[...], axis=0)
    sm3 = [
        launch(remote(t2_ref, sm3_ref.at[y], sm3_s.at[k - 1], sm3_r.at[k - 1], mem=lax.rem(y + k, NY)))
        for k in range(1, NY)
    ]
    sm3_ref[y] = t2_ref[...]
    drain(len(crosses) + len(sm2))
    finish(0)
    finish(1)
    for copy in sm3:
        copy.wait_recv()
    smo_ref[lon] = jnp.sum(sm3_ref[...], axis=0)
    sm4 = [
        launch(remote(smo_ref.at[lon], smo_ref.at[lon], sm4_s.at[k - 1], sm4_r.at[k - 1], lon=lax.rem(lon + k, NLON)))
        for k in by_distance
    ]
    drain(len(depths) + len(sm3))
    spread(0, 0)
    spread(0, 1)
    spread(1, 0)
    spread(1, 1)
    for copy in sm4:
        copy.wait_recv()
    summed = jnp.concatenate([smo_ref[k] for k in range(NLON)], axis=1)
    outbias_ref[...] = summed[3:4, :]
    outgain_ref[...] = summed[4:5, :]
    outw_ref[...] = lax.dot_general(
        tab_ref[...], summed, (((0,), (0,)), ((), ())), precision=HIGH, preferred_element_type=F32
    )
    drain(len(agz) + len(sm4))
    to_sibling(0, 0)
    to_sibling(0, 1)
    place_rows(core, 0)
    to_sibling(1, 0)
    to_sibling(1, 1)
    place_rows(core, 1)
    drain(len(agx))
    for g in range(2):
        for k in range(4):
            agc[0, g, k].wait_recv()
    place_rows(1 - core, 0)
    drain(len(sent))
    for g in range(2):
        for k in range(4):
            agc[1, g, k].wait_recv()
    place_rows(1 - core, 1)


def write_out(*refs):
    sems = refs[-1]
    half = len(refs) // 2
    copies = []
    for source, target in zip(refs[:half], refs[half:-1]):
        rows = source.shape[0]
        step = min(rows, 256 if source.dtype == BF16 else 64)
        for start in range(0, rows - rows % step, step):
            part = pl.ds(start, step) if step < rows else slice(None)
            copies.append(pltpu.make_async_copy(source.at[part], target.at[part], sems.at[len(copies)]))
        if rows % step:
            part = pl.ds(rows - rows % step, rows % step)
            copies.append(pltpu.make_async_copy(source.at[part], target.at[part], sems.at[len(copies)]))
    for copy in copies:
        copy.start()
    for copy in copies:
        copy.wait()


def on_device(latent, norm_gain, hidden_weight, hidden_bias, output_weight, flux_table, target, land_sea, band_index):
    vmem = pl.BlockSpec(memory_space=pltpu.VMEM)
    hbm = pl.BlockSpec(memory_space=pl.ANY)
    dma = pltpu.SemaphoreType.DMA
    scratch = [
        pltpu.VMEM((CELLS, D), BF16),
        pltpu.VMEM((D, D), BF16),
        pltpu.VMEM((1, D), F32),
        pltpu.VMEM((1, D), F32),
        pltpu.VMEM((80, D), BF16),
        pltpu.VMEM((3, 80), F32),
        pltpu.VMEM((1, ROWS), F32),
        pltpu.VMEM((ROWS, COLS), jnp.int32),
        pltpu.VMEM((1, ROWS), jnp.int32),
        pltpu.VMEM((CELLS, D), BF16),
        pltpu.VMEM((CELLS, D), F32),
        pltpu.VMEM((CELLS, D), BF16),
        pltpu.VMEM((4, CELLS, 256), BF16),
        pltpu.VMEM((CELLS, LANES), F32),
        pltpu.VMEM((CELLS, LANES), F32),
        pltpu.VMEM((CELLS, LANES), F32),
        pltpu.VMEM((LANES, LANES), F32),
        pltpu.VMEM((8, D), F32),
        pltpu.VMEM((8, 80), F32),
        pltpu.VMEM((ROWS * 8, D), F32),
        pltpu.VMEM((16, D), F32),
        pltpu.VMEM((16, LANES), F32),
        pltpu.VMEM((8, D), F32),
        pltpu.VMEM((8, LANES), F32),
        pltpu.VMEM((NLON, 8, LANES), F32),
        pltpu.VMEM((8, LANES), F32),
        pltpu.VMEM((NZ, 8, LANES), F32),
        pltpu.VMEM((2, 2, NY, NX, 64, LANES), F32),
        pltpu.VMEM((2, 2, NY, NX, 64, LANES), F32),
        pltpu.VMEM((2, 2, NY, NX, 64, LANES), F32),
        pltpu.VMEM((2, 2, 2, 4, 32, LANES), F32),
        pltpu.VMEM((2, 2, 2, 4, 32, LANES), F32),
        pltpu.VMEM((2, 2, 2, 4, 32, LANES), F32),
        pltpu.VMEM((2, 2, 4, 64, LANES), F32),
        pltpu.VMEM((2, 2, 3, 64, LANES), F32),
        pltpu.VMEM((2, NZ, 2, 8, LANES), F32),
        pltpu.VMEM((2, NZ - 1, 2, 8, LANES), F32),
        pltpu.VMEM((2, 2, NX, NZ, 2, 8, LANES), F32),
        pltpu.VMEM((NLON, 8, LANES), F32),
        pltpu.VMEM((NLON, 8, LANES), F32),
        pltpu.VMEM((8, LANES), F32),
        pltpu.VMEM((NZ, 8, LANES), F32),
        pltpu.VMEM((8, LANES), F32),
        pltpu.VMEM((NY, 8, LANES), F32),
        pltpu.VMEM((NLON, 8, LANES), F32),
        dma((NCHUNK,)),
        dma((4,)),
        dma((7,)),
        dma((7,)), dma((7,)),
        dma((7,)), dma((7,)),
        dma((2, 2)), dma((2, 2)),
        dma((2, 2, 6)), dma((2, 2, 6)),
        dma((2, 2, 3)), dma((2, 2, 3)),
        dma((2, 7)), dma((2, 7)),
        dma((2, 7)), dma((2, 7)),
        dma((2, 2, 3)), dma((2, 2, 3)),
        dma((2, 2, 4)), dma((2, 2, 4)),
        dma((7,)), dma((7,)),
        dma((7,)), dma((7,)),
        dma((3,)), dma((3,)),
        dma((7,)), dma((7,)),
    ]
    shapes = (((CELLS, D), BF16), ((D // NY, D), F32), ((80, D), F32), ((1, D), F32), ((1, D), F32))
    held = pl.pallas_call(
        kernel,
        out_shape=tuple(pltpu.VMEM(*shape) for shape in shapes),
        in_specs=[hbm] * 9,
        out_specs=(vmem,) * 5,
        scratch_shapes=scratch,
        compiler_params=pltpu.CompilerParams(
            collective_id=0, has_side_effects=True, vmem_limit_bytes=56 * 1024 * 1024
        ),
        cost_estimate=pl.CostEstimate(flops=10_000_000_000, bytes_accessed=9_000_000, transcendentals=3_000_000),
    )(
        latent.reshape(CELLS, D),
        norm_gain.reshape(1, D),
        hidden_weight,
        hidden_bias.reshape(1, D),
        output_weight.T,
        flux_table,
        target,
        land_sea,
        band_index.reshape(1, ROWS),
    )
    grad_cells, grad_hidden, grad_out, grad_gain, grad_bias = pl.pallas_call(
        write_out,
        out_shape=tuple(jax.ShapeDtypeStruct(*shape) for shape in shapes),
        in_specs=[vmem] * 5,
        out_specs=(hbm,) * 5,
        scratch_shapes=[dma((16,))],
        compiler_params=pltpu.CompilerParams(vmem_limit_bytes=1024 * 1024),
    )(*[pltpu.with_memory_space_constraint(array, pltpu.VMEM) for array in held])
    return (
        grad_cells.reshape(latent.shape),
        grad_hidden,
        grad_out.T,
        grad_gain.reshape(D),
        grad_bias.reshape(D),
    )


def solution(mesh):
    return jax.shard_map(
        on_device,
        mesh=mesh,
        in_specs=(
            P("mem", "lat", "lon", None),
            P(),
            P(),
            P(),
            P(),
            P(),
            P("mem", "lat"),
            P("lat", "lon"),
            P("lat"),
        ),
        out_specs=(P("mem", "lat", "lon", None), P("mem", None), P(), P(), P()),
        check_vma=False,
    )
```

```python
import functools
import math

import jax
import jax.numpy as jnp
from jax import lax
from jax.experimental import pallas as pl
from jax.experimental.pallas import tpu as pltpu
from jax.sharding import PartitionSpec as P

MESH = pl.DeviceIdType.MESH
F32 = jnp.float32
BF16 = jnp.bfloat16
HIGH = lax.Precision.HIGHEST

CELLS = 1536
ROWS = 12
COLS = 128
D = 1024
CHUNK = 256
NCHUNK = CELLS // CHUNK
LANES = 128
TILES = D // LANES
NX, NY, NZ, NLON = 4, 4, 8, 8


def remote(src, dst, send_sem, recv_sem, **where):
    return pltpu.make_async_remote_copy(
        src_ref=src,
        dst_ref=dst,
        send_sem=send_sem,
        recv_sem=recv_sem,
        device_id=where,
        device_id_type=MESH,
    )


def contract(left, right):
    return lax.dot_general(left, right, (((0,), (0,)), ((), ())), preferred_element_type=F32)


def kernel(
    lat_hbm, gain_hbm, w1_hbm, bias_hbm, w2_hbm, table_hbm, target_hbm, types_hbm, band_hbm,
    outlat_ref, outhid_ref, outw_ref, outgain_ref, outbias_ref,
    x_ref, w1_ref, gain_ref, bias_ref, w2_ref, table_ref, target_ref, types_ref, band_ref,
    n_ref, v_ref, u_ref, p_ref, inv_ref, coef_ref, tcol_ref, square_ref,
    q_ref, tab_ref, s_ref, b_ref, fb_ref, gacc_ref, mine_ref, ex1_ref, line_ref, ex2_ref,
    give_ref, take_ref, own_ref, pass_ref, plain_ref, agg_ref, part_ref, cross_ref, piece_ref, depth_ref,
    hid_ref, sm_ref, sm1_ref, t1_ref, sm2_ref, t2_ref, sm3_ref, smo_ref,
    xsem, wsem, insem, ex1_s, ex1_r, ex2_s, ex2_r, core_s, core_r, first_s, first_r, cross_s, cross_r, depth_s, depth_r,
    agz_s, agz_r, agx_s, agx_r, agc_s, agc_r, sm1_s, sm1_r, sm2_s, sm2_r, sm3_s, sm3_r, sm4_s, sm4_r,
):
    z = lax.axis_index("lat")
    lon = lax.axis_index("lon")
    y = lax.axis_index("mem")
    x = lon // 2
    core = lon % 2

    def lon_at(step):
        return lax.rem(x + step, NX) * 2 + core

    def chunk_rows(i):
        return pl.ds(i * CHUNK, CHUNK)

    loads = [pltpu.make_async_copy(lat_hbm.at[chunk_rows(i)], x_ref.at[chunk_rows(i)], xsem.at[i]) for i in range(NCHUNK)]
    wloads = [
        pltpu.make_async_copy(w1_hbm.at[pl.ds(i * 256, 256)], w1_ref.at[pl.ds(i * 256, 256)], wsem.at[i]) for i in range(4)
    ]
    smalls = [
        pltpu.make_async_copy(source, target, insem.at[i])
        for i, (source, target) in enumerate(
            (
                (w2_hbm, w2_ref),
                (types_hbm, types_ref),
                (table_hbm, table_ref),
                (gain_hbm, gain_ref),
                (bias_hbm, bias_ref),
                (band_hbm, band_ref),
                (target_hbm, target_ref),
            )
        )
    ]
    loads[0].start()
    for copy in smalls:
        copy.start()
    for copy in wloads:
        copy.start()
    for i in range(1, NCHUNK):
        loads[i].start()

    barrier = pltpu.get_barrier_semaphore()
    for k in range(1, NLON):
        pl.semaphore_signal(barrier, inc=1, device_id={"lon": lax.rem(lon + k, NLON)}, device_id_type=MESH)
    for k in range(1, NZ):
        pl.semaphore_signal(barrier, inc=1, device_id={"lat": lax.rem(z + k, NZ)}, device_id_type=MESH)
    for k in range(1, NY):
        pl.semaphore_signal(barrier, inc=1, device_id={"mem": lax.rem(y + k, NY)}, device_id_type=MESH)

    def tables():
        tab_ref[...] = jnp.zeros_like(tab_ref)
        tab_ref[0:3, :] = table_ref[...]
        table = tab_ref[...]
        high = table.astype(BF16)
        rest = table - high.astype(F32)
        middle = rest.astype(BF16)
        w2 = w2_ref[...]
        dims = (((1,), (0,)), ((), ()))
        q_ref[...] = lax.dot_general(high, w2, dims, preferred_element_type=F32) + lax.dot_general(
            middle, w2, dims, preferred_element_type=F32
        )
        square_ref[...] = jnp.zeros_like(square_ref)
        square_ref[0:ROWS, :] = types_ref[...].astype(F32)
        turned = square_ref[...].T
        for r in range(ROWS):
            tcol_ref[r * COLS : (r + 1) * COLS, :] = jnp.broadcast_to(turned[:, r : r + 1], (COLS, LANES))

    for copy in smalls:
        copy.wait()
    gain = gain_ref[...]
    bias = bias_ref[...]

    def normalise(i):
        rows = chunk_rows(i)
        xf = x_ref[rows, :].astype(F32)
        inv = lax.rsqrt(jnp.mean(xf * xf, axis=-1, keepdims=True) + 1e-05)
        inv_ref[rows, :] = jnp.broadcast_to(inv, (CHUNK, LANES))
        n_ref[rows, :] = (xf * inv * gain).astype(BF16)

    def first_dot(i):
        rows = chunk_rows(i)
        v_ref[rows, :] = jnp.dot(n_ref[rows, :], w1_ref[...], preferred_element_type=F32)

    kind = lax.broadcasted_iota(jnp.int32, (16, COLS), 0)

    def activate(i):
        rows = chunk_rows(i)
        p = v_ref[rows, :] + bias
        act = (p * (0.5 * jnp.tanh(0.5 * p) + 0.5)).astype(BF16)
        left = kind == types_ref[2 * i : 2 * i + 1, :]
        right = (kind - 8) == types_ref[2 * i + 1 : 2 * i + 2, :]
        onehot = jnp.concatenate([left.astype(F32), right.astype(F32)], axis=1).astype(BF16)
        s_ref[i * 16 : (i + 1) * 16, :] = jnp.dot(onehot, act, preferred_element_type=F32)

    loads[0].wait()
    normalise(0)
    for copy in wloads:
        copy.wait()
    for i in range(NCHUNK):
        if i + 1 < NCHUNK:
            loads[i + 1].wait()
        first_dot(i)
        if i + 1 < NCHUNK:
            normalise(i + 1)
        if i == 0:
            tables()
        if i >= 1:
            activate(i - 1)
    activate(NCHUNK - 1)

    lanes16 = lax.broadcasted_iota(jnp.int32, (16, LANES), 1)
    subs16 = lax.broadcasted_iota(jnp.int32, (16, LANES), 0)
    diagonal = lanes16 == subs16
    net = jnp.sum(s_ref[...].reshape(ROWS, 8, D) * q_ref[...][None], axis=1)
    net = jnp.sum(net, axis=1, keepdims=True)
    net = jnp.concatenate([net, jnp.zeros((16 - ROWS, 1), F32)], axis=0)
    net = jnp.sum(jnp.where(diagonal, net, 0.0), axis=0, keepdims=True)
    mine_ref[...] = jnp.zeros_like(mine_ref)
    mine_ref[0:1, 0:ROWS] = band_ref[...].astype(F32)
    mine_ref[1:2, 0:ROWS] = target_ref[...]
    lane1 = lax.broadcasted_iota(jnp.int32, (1, LANES), 1)
    coslat = jnp.cos(math.pi * (mine_ref[0:1, :] / 720.0 - 0.5))
    coslat = jnp.where(lane1 < ROWS, coslat, 0.0)
    mine_ref[0:1, :] = coslat * net * (1.0 / (NLON * COLS))

    pl.semaphore_wait(barrier, (NLON - 1) + (NZ - 1) + (NY - 1))
    sent = []

    def launch(copy):
        copy.start()
        sent.append(copy)
        return copy

    by_distance = (4, 3, 5, 2, 6, 1, 7)
    ex1 = [
        launch(remote(mine_ref, ex1_ref.at[lon], ex1_s.at[k - 1], ex1_r.at[k - 1], lon=lax.rem(lon + k, NLON)))
        for k in by_distance
    ]
    ex1_ref[lon] = mine_ref[...]

    def unscaled(i):
        rows = chunk_rows(i)
        kinds = tcol_ref[rows, :]
        is_one = kinds == 1.0
        is_two = kinds == 2.0
        inner = jnp.zeros((CHUNK, LANES), F32)
        for tile in range(TILES):
            cols = slice(tile * LANES, (tile + 1) * LANES)
            before = v_ref[rows, cols]
            p = before + bias_ref[0:1, cols]
            sigma = 0.5 * jnp.tanh(0.5 * p) + 0.5
            slope = sigma + (p * sigma) * (1.0 - sigma)
            weight = jnp.where(is_one, q_ref[1:2, cols], jnp.where(is_two, q_ref[2:3, cols], q_ref[0:1, cols]))
            grad = slope * weight
            inner += grad * before
            b_ref[2 * i : 2 * i + 2, cols] = jnp.sum(grad.reshape(2, COLS, LANES), axis=1)
            u_ref[rows, cols] = grad.astype(BF16)
        inv = inv_ref[rows, :]
        inner = jnp.sum(inner, axis=1, keepdims=True)
        coef_ref[rows, :] = inv * inv * (inner * (1.0 / D))

    def back(i):
        rows = chunk_rows(i)
        v_ref[rows, :] = lax.dot_general(
            u_ref[rows, :], w1_ref[...], (((1,), (1,)), ((), ())), preferred_element_type=F32
        )

    for i in range(NCHUNK // 2):
        unscaled(i)
        if i >= 1:
            back(i - 1)
    coscol = jnp.sum(jnp.where(diagonal, coslat, 0.0), axis=1, keepdims=True) * (1.0 / (ROWS * NZ))
    for copy in ex1:
        copy.wait_recv()
    sub8 = lax.broadcasted_iota(jnp.int32, (8, LANES), 0)
    lane8 = lax.broadcasted_iota(jnp.int32, (8, LANES), 1)
    line_ref[...] = jnp.where(sub8 == 0, jnp.sum(ex1_ref[...], axis=0), mine_ref[...])
    ex2 = [
        launch(remote(line_ref, ex2_ref.at[z], ex2_s.at[k - 1], ex2_r.at[k - 1], lat=lax.rem(z + k, NZ)))
        for k in by_distance
    ]
    ex2_ref[z] = line_ref[...]
    for i in range(NCHUNK // 2, NCHUNK):
        unscaled(i)
        back(i - 1)
    back(NCHUNK - 1)
    for copy in ex2:
        copy.wait_recv()

    weighted = jnp.concatenate([ex2_ref[k][0:1, :] for k in range(NZ)], axis=0)
    targets = jnp.concatenate([ex2_ref[k][1:2, :] for k in range(NZ)], axis=0)
    count = (ROWS * NZ - ROWS * sub8 - lane8).astype(F32)
    south = jnp.sum(jnp.where(sub8 < z, weighted, 0.0), axis=0, keepdims=True)
    north = jnp.sum(jnp.where(sub8 > z, count * weighted - targets, 0.0), axis=0, keepdims=True)
    here = jnp.sum(jnp.where(sub8 == z, weighted, 0.0), axis=0, keepdims=True)
    goal = jnp.sum(jnp.where(sub8 == z, targets, 0.0), axis=0, keepdims=True)
    left_over = ROWS * NZ - ROWS * z
    both = (left_over - jnp.maximum(subs16, lanes16)).astype(F32) * here
    both = both + (left_over - subs16).astype(F32) * south + north - jnp.where(lanes16 >= subs16, goal, 0.0)
    flux = coscol * jnp.sum(both, axis=1, keepdims=True)
    fb_ref[...] = jnp.broadcast_to(flux, (16, LANES))

    def scale_tile(slot, half, t):
        for way in range(2):
            cols = pl.ds(pl.multiple_of(half * 512 + t * 256 + way * LANES, LANES), LANES)
            for r in range(ROWS):
                rows = pl.ds(r * COLS, COLS)
                p_ref[slot, rows, way * LANES : (way + 1) * LANES] = (
                    u_ref[rows, cols].astype(F32) * fb_ref[r : r + 1, :]
                ).astype(BF16)

    def hidden_tile(ref, slot, t, part):
        tile = contract(n_ref[:, part * 512 : (part + 1) * 512], p_ref[slot])
        for way in range(2):
            ref[t, way, 2 * part : 2 * part + 2] = tile[:, way * LANES : (way + 1) * LANES].reshape(2, NX, 64, LANES)

    sibling = x * 2 + 1 - core
    tiles = ((give_ref, 1 - core, 0), (own_ref, core, 0), (give_ref, 1 - core, 1), (own_ref, core, 1))

    def place(way):
        return y if way == 0 else x

    def toward(way, step):
        if way == 0:
            return {"mem": lax.rem(y + step, NY)}
        return {"lon": lon_at(step)}

    def half(t, way, owner, which):
        rows = pl.ds(32 * which, 32)
        return own_ref.at[t, way, owner, :, rows] if way == 0 else own_ref.at[t, way, :, owner, rows]

    passes, plains, aggs = {}, {}, {}

    def hop(table, t, way, which, step, owner, target, sem):
        table[t, way, which] = launch(
            remote(
                half(t, way, owner, which),
                target.at[t, way, which],
                first_s.at[t, way, sem],
                first_r.at[t, way, sem],
                **toward(way, step),
            )
        )

    def first(t):
        for part in range(2):
            to_core[t, part].wait_recv()
        own_ref[t] = own_ref[t] + take_ref[t]
        for way in range(2):
            opposite = lax.rem(place(way) + 2, 4)
            hop(passes, t, way, 0, 1, opposite, pass_ref, 0)
            hop(passes, t, way, 1, 3, opposite, pass_ref, 1)
        for way in range(2):
            hop(plains, t, way, 1, 1, lax.rem(place(way) + 1, 4), plain_ref, 2)
            hop(plains, t, way, 0, 3, lax.rem(place(way) + 3, 4), plain_ref, 3)

    def ring(t):
        for way in range(2):
            for which, step in ((0, 1), (1, 3)):
                owner = lax.rem(place(way) + step, 4)
                passes[t, way, which].wait_recv()
                mid = half(t, way, owner, which)
                mid[...] = mid[...] + pass_ref[t, way, which]
                hop(aggs, t, way, which, step, owner, agg_ref, 4 + which)

    to_core = {}
    scale_tile(0, *tiles[0][1:])
    for slot in range(4):
        ref, _, t = tiles[slot]
        for part in range(2):
            hidden_tile(ref, slot, t, part)
            if part == 0 and slot < 3:
                scale_tile(slot + 1, *tiles[slot + 1][1:])
            if ref is give_ref:
                y_half = pl.ds(2 * part, 2)
                to_core[t, part] = launch(
                    remote(
                        give_ref.at[t, :, y_half],
                        take_ref.at[t, :, y_half],
                        core_s.at[t, part],
                        core_r.at[t, part],
                        lon=sibling,
                    )
                )
        if slot == 2:
            first(0)
    first(1)

    gacc_ref[...] = jnp.zeros_like(gacc_ref)

    def latent_grad(i):
        rows = chunk_rows(i)
        flux = jnp.concatenate(
            [jnp.broadcast_to(fb_ref[2 * i + k : 2 * i + k + 1, :], (COLS, LANES)) for k in range(2)], axis=0
        )
        inv = inv_ref[rows, :] * flux
        coef = coef_ref[rows, :] * flux
        for tile in range(TILES):
            cols = slice(tile * LANES, (tile + 1) * LANES)
            xf = x_ref[rows, cols].astype(F32)
            scaled = v_ref[rows, cols] * inv
            gacc_ref[:, cols] += jnp.sum((scaled * xf).reshape(CHUNK // 8, 8, LANES), axis=0)
            outlat_ref[rows, cols] = (scaled * gain_ref[0:1, cols] - xf * coef).astype(BF16)

    for i in range(NCHUNK):
        latent_grad(i)
        if i == NCHUNK - 2:
            ring(0)

    small = jnp.zeros((8, D), F32)
    bias_sum = jnp.zeros((1, D), F32)
    for r in range(ROWS):
        scale = fb_ref[r : r + 1, 0:1]
        small = small + s_ref[r * 8 : (r + 1) * 8, :] * scale
        bias_sum = bias_sum + b_ref[r : r + 1, :] * scale
    gain_sum = jnp.sum(gacc_ref[...], axis=0, keepdims=True)
    row8 = lax.broadcasted_iota(jnp.int32, (8, D), 0)
    small = jnp.where(row8 == 3, bias_sum, jnp.where(row8 == 4, gain_sum, small))
    for k in range(NLON):
        sm_ref[k] = small[:, k * LANES : (k + 1) * LANES]
    sm1 = []
    for k in range(1, NLON):
        peer = lax.rem(lon + k, NLON)
        sm1.append(launch(remote(sm_ref.at[peer], sm1_ref.at[lon], sm1_s.at[k - 1], sm1_r.at[k - 1], lon=peer)))
    sm1_ref[lon] = sm_ref[lon]

    crosses, depths, agz = {}, {}, {}

    def cross(t):
        for way in range(2):
            for which in range(2):
                plains[t, way, which].wait_recv()
                aggs[t, way, which].wait_recv()
                part_ref[t, way, :, 32 * which : 32 * (which + 1)] = (
                    half(t, way, place(way), which)[...] + plain_ref[t, way, which] + agg_ref[t, way, which]
                )
            other = 1 - way
            for k in (2, 1, 3):
                crosses[t, way, k] = launch(
                    remote(
                        part_ref.at[t, way, lax.rem(place(other) + k, 4)],
                        cross_ref.at[t, way, k - 1],
                        cross_s.at[t, way, k - 1],
                        cross_r.at[t, way, k - 1],
                        **toward(other, k),
                    )
                )

    def deepen(t):
        for way in range(2):
            for k in range(1, 4):
                crosses[t, way, k].wait_recv()
            piece = part_ref[t, way, place(1 - way)] + cross_ref[t, way, 0] + cross_ref[t, way, 1] + cross_ref[t, way, 2]
            piece_ref[t, :, way] = piece.reshape(NZ, 8, LANES)
        for k in by_distance:
            peer = lax.rem(z + k, NZ)
            depths[t, k] = launch(
                remote(
                    piece_ref.at[t, peer], depth_ref.at[t, k - 1], depth_s.at[t, k - 1], depth_r.at[t, k - 1], lat=peer
                )
            )

    slots = (0, 1, 7, 2, 6, 3, 5, 4)
    slot_of = {k: slots.index(k) for k in range(NZ)}

    def finish(t):
        for k in range(1, NZ):
            depths[t, k].wait_recv()
        piece = piece_ref[t, z]
        for k in range(NZ - 1):
            piece = piece + depth_ref[t, k]
        hid_ref[core, t, x, 0] = piece
        for k in by_distance:
            agz[t, k] = launch(
                remote(
                    hid_ref.at[core, t, x, 0],
                    hid_ref.at[core, t, x, slot_of[NZ - k]],
                    agz_s.at[t, k - 1],
                    agz_r.at[t, k - 1],
                    lat=lax.rem(z + k, NZ),
                )
            )

    groups = (((0, 5), (5, 8)), ((0, 5), (5, 8)))
    agx, agc = {}, {}

    def spread(t, g):
        start, stop = groups[t][g]
        for k in range(1, NZ):
            if start <= slot_of[NZ - k] < stop:
                agz[t, k].wait_recv()
        spot = hid_ref.at[core, t, x, pl.ds(start, stop - start)]
        for k in (2, 1, 3):
            agx[t, g, k] = launch(remote(spot, spot, agx_s.at[t, g, k - 1], agx_r.at[t, g, k - 1], lon=lon_at(k)))
        agc[t, g, 0] = launch(remote(spot, spot, agc_s.at[t, g, 0], agc_r.at[t, g, 0], lon=sibling))

    def to_sibling(t, g):
        start, stop = groups[t][g]
        for k in (1, 3, 2):
            agx[t, g, k].wait_recv()
            spot = hid_ref.at[core, t, lax.rem(x + 4 - k, NX), pl.ds(start, stop - start)]
            agc[t, g, k] = launch(remote(spot, spot, agc_s.at[t, g, k], agc_r.at[t, g, k], lon=sibling))

    def place_rows(half, t, g):
        start, stop = groups[t][g]
        for xi in range(NX):
            for k in (k for k in range(NZ) if start <= slot_of[k] < stop):
                rows = pl.ds(pl.multiple_of(xi * 64 + lax.rem(z + k, NZ) * 8, 8), 8)
                for way in range(2):
                    cols = pl.ds(pl.multiple_of(half * 512 + t * 256 + way * LANES, LANES), LANES)
                    outhid_ref[rows, cols] = hid_ref[half, t, xi, slot_of[k], way]

    def drain(count):
        for copy in sent[:count]:
            copy.wait_send()
        del sent[:count]

    ring(1)
    drain(len(ex1) + len(ex2) + len(to_core))
    cross(0)
    cross(1)
    for copy in sm1:
        copy.wait_recv()
    t1_ref[...] = jnp.sum(sm1_ref[...], axis=0)
    sm2 = [
        launch(remote(t1_ref, sm2_ref.at[z], sm2_s.at[k - 1], sm2_r.at[k - 1], lat=lax.rem(z + k, NZ)))
        for k in by_distance
    ]
    sm2_ref[z] = t1_ref[...]
    drain(len(passes) + len(plains) + len(sm1) + len(aggs))
    deepen(0)
    deepen(1)
    for copy in sm2:
        copy.wait_recv()
    t2_ref[...] = jnp.sum(sm2_ref[...], axis=0)
    sm3 = [
        launch(remote(t2_ref, sm3_ref.at[y], sm3_s.at[k - 1], sm3_r.at[k - 1], mem=lax.rem(y + k, NY)))
        for k in range(1, NY)
    ]
    sm3_ref[y] = t2_ref[...]
    drain(len(crosses) + len(sm2))
    finish(0)
    finish(1)
    for copy in sm3:
        copy.wait_recv()
    smo_ref[lon] = jnp.sum(sm3_ref[...], axis=0)
    sm4 = [
        launch(remote(smo_ref.at[lon], smo_ref.at[lon], sm4_s.at[k - 1], sm4_r.at[k - 1], lon=lax.rem(lon + k, NLON)))
        for k in by_distance
    ]
    drain(len(depths) + len(sm3))
    spread(0, 0)
    spread(0, 1)
    spread(1, 0)
    spread(1, 1)
    for copy in sm4:
        copy.wait_recv()
    summed = jnp.concatenate([smo_ref[k] for k in range(NLON)], axis=1)
    outbias_ref[...] = summed[3:4, :]
    outgain_ref[...] = summed[4:5, :]
    outw_ref[...] = lax.dot_general(
        tab_ref[...], summed, (((0,), (0,)), ((), ())), precision=HIGH, preferred_element_type=F32
    )
    drain(len(agz) + len(sm4))
    to_sibling(0, 0)
    to_sibling(0, 1)
    for g in range(2):
        place_rows(core, 0, g)
    to_sibling(1, 0)
    to_sibling(1, 1)
    drain(len(agx))
    for g in range(2):
        for k in range(4):
            agc[0, g, k].wait_recv()
        place_rows(1 - core, 0, g)
    for g in range(2):
        place_rows(core, 1, g)
    drain(len(sent))
    for g in range(2):
        for k in range(4):
            agc[1, g, k].wait_recv()
        place_rows(1 - core, 1, g)


def write_out(*refs):
    sems = refs[-1]
    half = len(refs) // 2
    copies = []
    for source, target in zip(refs[:half], refs[half:-1]):
        rows = source.shape[0]
        step = min(rows, 256 if source.dtype == BF16 else 64)
        for start in range(0, rows - rows % step, step):
            part = pl.ds(start, step) if step < rows else slice(None)
            copies.append(pltpu.make_async_copy(source.at[part], target.at[part], sems.at[len(copies)]))
        if rows % step:
            part = pl.ds(rows - rows % step, rows % step)
            copies.append(pltpu.make_async_copy(source.at[part], target.at[part], sems.at[len(copies)]))
    for copy in copies:
        copy.start()
    for copy in copies:
        copy.wait()


def on_device(latent, norm_gain, hidden_weight, hidden_bias, output_weight, flux_table, target, land_sea, band_index):
    vmem = pl.BlockSpec(memory_space=pltpu.VMEM)
    hbm = pl.BlockSpec(memory_space=pl.ANY)
    dma = pltpu.SemaphoreType.DMA
    scratch = [
        pltpu.VMEM((CELLS, D), BF16),
        pltpu.VMEM((D, D), BF16),
        pltpu.VMEM((1, D), F32),
        pltpu.VMEM((1, D), F32),
        pltpu.VMEM((80, D), BF16),
        pltpu.VMEM((3, 80), F32),
        pltpu.VMEM((1, ROWS), F32),
        pltpu.VMEM((ROWS, COLS), jnp.int32),
        pltpu.VMEM((1, ROWS), jnp.int32),
        pltpu.VMEM((CELLS, D), BF16),
        pltpu.VMEM((CELLS, D), F32),
        pltpu.VMEM((CELLS, D), BF16),
        pltpu.VMEM((4, CELLS, 256), BF16),
        pltpu.VMEM((CELLS, LANES), F32),
        pltpu.VMEM((CELLS, LANES), F32),
        pltpu.VMEM((CELLS, LANES), F32),
        pltpu.VMEM((LANES, LANES), F32),
        pltpu.VMEM((8, D), F32),
        pltpu.VMEM((8, 80), F32),
        pltpu.VMEM((ROWS * 8, D), F32),
        pltpu.VMEM((16, D), F32),
        pltpu.VMEM((16, LANES), F32),
        pltpu.VMEM((8, D), F32),
        pltpu.VMEM((8, LANES), F32),
        pltpu.VMEM((NLON, 8, LANES), F32),
        pltpu.VMEM((8, LANES), F32),
        pltpu.VMEM((NZ, 8, LANES), F32),
        pltpu.VMEM((2, 2, NY, NX, 64, LANES), F32),
        pltpu.VMEM((2, 2, NY, NX, 64, LANES), F32),
        pltpu.VMEM((2, 2, NY, NX, 64, LANES), F32),
        pltpu.VMEM((2, 2, 2, 4, 32, LANES), F32),
        pltpu.VMEM((2, 2, 2, 4, 32, LANES), F32),
        pltpu.VMEM((2, 2, 2, 4, 32, LANES), F32),
        pltpu.VMEM((2, 2, 4, 64, LANES), F32),
        pltpu.VMEM((2, 2, 3, 64, LANES), F32),
        pltpu.VMEM((2, NZ, 2, 8, LANES), F32),
        pltpu.VMEM((2, NZ - 1, 2, 8, LANES), F32),
        pltpu.VMEM((2, 2, NX, NZ, 2, 8, LANES), F32),
        pltpu.VMEM((NLON, 8, LANES), F32),
        pltpu.VMEM((NLON, 8, LANES), F32),
        pltpu.VMEM((8, LANES), F32),
        pltpu.VMEM((NZ, 8, LANES), F32),
        pltpu.VMEM((8, LANES), F32),
        pltpu.VMEM((NY, 8, LANES), F32),
        pltpu.VMEM((NLON, 8, LANES), F32),
        dma((NCHUNK,)),
        dma((4,)),
        dma((7,)),
        dma((7,)), dma((7,)),
        dma((7,)), dma((7,)),
        dma((2, 2)), dma((2, 2)),
        dma((2, 2, 6)), dma((2, 2, 6)),
        dma((2, 2, 3)), dma((2, 2, 3)),
        dma((2, 7)), dma((2, 7)),
        dma((2, 7)), dma((2, 7)),
        dma((2, 2, 3)), dma((2, 2, 3)),
        dma((2, 2, 4)), dma((2, 2, 4)),
        dma((7,)), dma((7,)),
        dma((7,)), dma((7,)),
        dma((3,)), dma((3,)),
        dma((7,)), dma((7,)),
    ]
    shapes = (((CELLS, D), BF16), ((D // NY, D), F32), ((80, D), F32), ((1, D), F32), ((1, D), F32))
    held = pl.pallas_call(
        kernel,
        out_shape=tuple(pltpu.VMEM(*shape) for shape in shapes),
        in_specs=[hbm] * 9,
        out_specs=(vmem,) * 5,
        scratch_shapes=scratch,
        compiler_params=pltpu.CompilerParams(
            collective_id=0, has_side_effects=True, vmem_limit_bytes=56 * 1024 * 1024
        ),
        cost_estimate=pl.CostEstimate(flops=10_000_000_000, bytes_accessed=9_000_000, transcendentals=3_000_000),
    )(
        latent.reshape(CELLS, D),
        norm_gain.reshape(1, D),
        hidden_weight,
        hidden_bias.reshape(1, D),
        output_weight.T,
        flux_table,
        target,
        land_sea,
        band_index.reshape(1, ROWS),
    )
    grad_cells, grad_hidden, grad_out, grad_gain, grad_bias = pl.pallas_call(
        write_out,
        out_shape=tuple(jax.ShapeDtypeStruct(*shape) for shape in shapes),
        in_specs=[vmem] * 5,
        out_specs=(hbm,) * 5,
        scratch_shapes=[dma((16,))],
        compiler_params=pltpu.CompilerParams(vmem_limit_bytes=1024 * 1024),
    )(*[pltpu.with_memory_space_constraint(array, pltpu.VMEM) for array in held])
    return (
        grad_cells.reshape(latent.shape),
        grad_hidden,
        grad_out.T,
        grad_gain.reshape(D),
        grad_bias.reshape(D),
    )


def solution(mesh):
    return jax.shard_map(
        on_device,
        mesh=mesh,
        in_specs=(
            P("mem", "lat", "lon", None),
            P(),
            P(),
            P(),
            P(),
            P(),
            P("mem", "lat"),
            P("lat", "lon"),
            P("lat"),
        ),
        out_specs=(P("mem", "lat", "lon", None), P("mem", None), P(), P(), P()),
        check_vma=False,
    )
```

```python
import functools
import math

import jax
import jax.numpy as jnp
from jax import lax
from jax.experimental import pallas as pl
from jax.experimental.pallas import tpu as pltpu
from jax.sharding import PartitionSpec as P

MESH = pl.DeviceIdType.MESH
F32 = jnp.float32
BF16 = jnp.bfloat16
HIGH = lax.Precision.HIGHEST

CELLS = 1536
ROWS = 12
COLS = 128
D = 1024
CHUNK = 256
NCHUNK = CELLS // CHUNK
LANES = 128
TILES = D // LANES
NX, NY, NZ, NLON = 4, 4, 8, 8


def remote(src, dst, send_sem, recv_sem, **where):
    return pltpu.make_async_remote_copy(
        src_ref=src,
        dst_ref=dst,
        send_sem=send_sem,
        recv_sem=recv_sem,
        device_id=where,
        device_id_type=MESH,
    )


def contract(left, right):
    return lax.dot_general(left, right, (((0,), (0,)), ((), ())), preferred_element_type=F32)


def kernel(
    lat_hbm, gain_hbm, w1_hbm, bias_hbm, w2_hbm, table_hbm, target_hbm, types_hbm, band_hbm,
    outlat_ref, outhid_ref, outw_ref, outgain_ref, outbias_ref,
    x_ref, w1_ref, gain_ref, bias_ref, w2_ref, table_ref, target_ref, types_ref, band_ref,
    n_ref, v_ref, u_ref, p_ref, inv_ref, coef_ref, tcol_ref, square_ref,
    q_ref, tab_ref, s_ref, b_ref, fb_ref, gacc_ref, mine_ref, ex1_ref, line_ref, ex2_ref,
    give_ref, take_ref, own_ref, pass_ref, plain_ref, agg_ref, part_ref, cross_ref, piece_ref, depth_ref,
    hid_ref, sm_ref, sm1_ref, t1_ref, sm2_ref, t2_ref, sm3_ref, smo_ref,
    xsem, wsem, insem, ex1_s, ex1_r, ex2_s, ex2_r, core_s, core_r, first_s, first_r, cross_s, cross_r, depth_s, depth_r,
    agz_s, agz_r, agx_s, agx_r, agc_s, agc_r, sm1_s, sm1_r, sm2_s, sm2_r, sm3_s, sm3_r, sm4_s, sm4_r,
):
    z = lax.axis_index("lat")
    lon = lax.axis_index("lon")
    y = lax.axis_index("mem")
    x = lon // 2
    core = lon % 2

    def lon_at(step):
        return lax.rem(x + step, NX) * 2 + core

    def chunk_rows(i):
        return pl.ds(i * CHUNK, CHUNK)

    loads = [pltpu.make_async_copy(lat_hbm.at[chunk_rows(i)], x_ref.at[chunk_rows(i)], xsem.at[i]) for i in range(NCHUNK)]
    wloads = [
        pltpu.make_async_copy(w1_hbm.at[pl.ds(i * 256, 256)], w1_ref.at[pl.ds(i * 256, 256)], wsem.at[i]) for i in range(4)
    ]
    smalls = [
        pltpu.make_async_copy(source, target, insem.at[i])
        for i, (source, target) in enumerate(
            (
                (w2_hbm, w2_ref),
                (types_hbm, types_ref),
                (table_hbm, table_ref),
                (gain_hbm, gain_ref),
                (bias_hbm, bias_ref),
                (band_hbm, band_ref),
                (target_hbm, target_ref),
            )
        )
    ]
    loads[0].start()
    for copy in smalls:
        copy.start()
    for copy in wloads:
        copy.start()
    for i in range(1, NCHUNK):
        loads[i].start()

    barrier = pltpu.get_barrier_semaphore()
    for k in range(1, NLON):
        pl.semaphore_signal(barrier, inc=1, device_id={"lon": lax.rem(lon + k, NLON)}, device_id_type=MESH)
    for k in range(1, NZ):
        pl.semaphore_signal(barrier, inc=1, device_id={"lat": lax.rem(z + k, NZ)}, device_id_type=MESH)
    for k in range(1, NY):
        pl.semaphore_signal(barrier, inc=1, device_id={"mem": lax.rem(y + k, NY)}, device_id_type=MESH)

    def tables():
        tab_ref[...] = jnp.zeros_like(tab_ref)
        tab_ref[0:3, :] = table_ref[...]
        table = tab_ref[...]
        high = table.astype(BF16)
        rest = table - high.astype(F32)
        middle = rest.astype(BF16)
        w2 = w2_ref[...]
        dims = (((1,), (0,)), ((), ()))
        q_ref[...] = lax.dot_general(high, w2, dims, preferred_element_type=F32) + lax.dot_general(
            middle, w2, dims, preferred_element_type=F32
        )
        square_ref[...] = jnp.zeros_like(square_ref)
        square_ref[0:ROWS, :] = types_ref[...].astype(F32)
        turned = square_ref[...].T
        for r in range(ROWS):
            tcol_ref[r * COLS : (r + 1) * COLS, :] = jnp.broadcast_to(turned[:, r : r + 1], (COLS, LANES))

    for copy in smalls:
        copy.wait()
    gain = gain_ref[...]
    bias = bias_ref[...]

    def normalise(i):
        rows = chunk_rows(i)
        xf = x_ref[rows, :].astype(F32)
        inv = lax.rsqrt(jnp.mean(xf * xf, axis=-1, keepdims=True) + 1e-05)
        inv_ref[rows, :] = jnp.broadcast_to(inv, (CHUNK, LANES))
        n_ref[rows, :] = (xf * inv * gain).astype(BF16)

    def first_dot(i):
        rows = chunk_rows(i)
        v_ref[rows, :] = jnp.dot(n_ref[rows, :], w1_ref[...], preferred_element_type=F32)

    kind = lax.broadcasted_iota(jnp.int32, (16, COLS), 0)

    def activate(i):
        rows = chunk_rows(i)
        p = v_ref[rows, :] + bias
        act = (p * (0.5 * jnp.tanh(0.5 * p) + 0.5)).astype(BF16)
        left = kind == types_ref[2 * i : 2 * i + 1, :]
        right = (kind - 8) == types_ref[2 * i + 1 : 2 * i + 2, :]
        onehot = jnp.concatenate([left.astype(F32), right.astype(F32)], axis=1).astype(BF16)
        s_ref[i * 16 : (i + 1) * 16, :] = jnp.dot(onehot, act, preferred_element_type=F32)

    loads[0].wait()
    normalise(0)
    for copy in wloads:
        copy.wait()
    for i in range(NCHUNK):
        if i + 1 < NCHUNK:
            loads[i + 1].wait()
        first_dot(i)
        if i + 1 < NCHUNK:
            normalise(i + 1)
        if i == 0:
            tables()
        if i >= 1:
            activate(i - 1)
    activate(NCHUNK - 1)

    lanes16 = lax.broadcasted_iota(jnp.int32, (16, LANES), 1)
    subs16 = lax.broadcasted_iota(jnp.int32, (16, LANES), 0)
    diagonal = lanes16 == subs16
    net = jnp.sum(s_ref[...].reshape(ROWS, 8, D) * q_ref[...][None], axis=1)
    net = jnp.sum(net, axis=1, keepdims=True)
    net = jnp.concatenate([net, jnp.zeros((16 - ROWS, 1), F32)], axis=0)
    net = jnp.sum(jnp.where(diagonal, net, 0.0), axis=0, keepdims=True)
    mine_ref[...] = jnp.zeros_like(mine_ref)
    mine_ref[0:1, 0:ROWS] = band_ref[...].astype(F32)
    mine_ref[1:2, 0:ROWS] = target_ref[...]
    lane1 = lax.broadcasted_iota(jnp.int32, (1, LANES), 1)
    coslat = jnp.cos(math.pi * (mine_ref[0:1, :] / 720.0 - 0.5))
    coslat = jnp.where(lane1 < ROWS, coslat, 0.0)
    mine_ref[0:1, :] = coslat * net * (1.0 / (NLON * COLS))

    pl.semaphore_wait(barrier, (NLON - 1) + (NZ - 1) + (NY - 1))
    sent = []

    def launch(copy):
        copy.start()
        sent.append(copy)
        return copy

    by_distance = (4, 3, 5, 2, 6, 1, 7)
    ex1 = [
        launch(remote(mine_ref, ex1_ref.at[lon], ex1_s.at[k - 1], ex1_r.at[k - 1], lon=lax.rem(lon + k, NLON)))
        for k in by_distance
    ]
    ex1_ref[lon] = mine_ref[...]

    def unscaled(i):
        rows = chunk_rows(i)
        kinds = tcol_ref[rows, :]
        is_one = kinds == 1.0
        is_two = kinds == 2.0
        inner = jnp.zeros((CHUNK, LANES), F32)
        for tile in range(TILES):
            cols = slice(tile * LANES, (tile + 1) * LANES)
            before = v_ref[rows, cols]
            p = before + bias_ref[0:1, cols]
            sigma = 0.5 * jnp.tanh(0.5 * p) + 0.5
            slope = sigma + (p * sigma) * (1.0 - sigma)
            weight = jnp.where(is_one, q_ref[1:2, cols], jnp.where(is_two, q_ref[2:3, cols], q_ref[0:1, cols]))
            grad = slope * weight
            inner += grad * before
            b_ref[2 * i : 2 * i + 2, cols] = jnp.sum(grad.reshape(2, COLS, LANES), axis=1)
            u_ref[rows, cols] = grad.astype(BF16)
        inv = inv_ref[rows, :]
        inner = jnp.sum(inner, axis=1, keepdims=True)
        coef_ref[rows, :] = inv * inv * (inner * (1.0 / D))

    def back(i):
        rows = chunk_rows(i)
        v_ref[rows, :] = lax.dot_general(
            u_ref[rows, :], w1_ref[...], (((1,), (1,)), ((), ())), preferred_element_type=F32
        )

    for i in range(NCHUNK // 2):
        unscaled(i)
        if i >= 1:
            back(i - 1)
    coscol = jnp.sum(jnp.where(diagonal, coslat, 0.0), axis=1, keepdims=True) * (1.0 / (ROWS * NZ))
    for copy in ex1:
        copy.wait_recv()
    sub8 = lax.broadcasted_iota(jnp.int32, (8, LANES), 0)
    lane8 = lax.broadcasted_iota(jnp.int32, (8, LANES), 1)
    line_ref[...] = jnp.where(sub8 == 0, jnp.sum(ex1_ref[...], axis=0), mine_ref[...])
    ex2 = [
        launch(remote(line_ref, ex2_ref.at[z], ex2_s.at[k - 1], ex2_r.at[k - 1], lat=lax.rem(z + k, NZ)))
        for k in by_distance
    ]
    ex2_ref[z] = line_ref[...]
    for i in range(NCHUNK // 2, NCHUNK):
        unscaled(i)
        back(i - 1)
    back(NCHUNK - 1)
    for copy in ex2:
        copy.wait_recv()

    weighted = jnp.concatenate([ex2_ref[k][0:1, :] for k in range(NZ)], axis=0)
    targets = jnp.concatenate([ex2_ref[k][1:2, :] for k in range(NZ)], axis=0)
    count = (ROWS * NZ - ROWS * sub8 - lane8).astype(F32)
    south = jnp.sum(jnp.where(sub8 < z, weighted, 0.0), axis=0, keepdims=True)
    north = jnp.sum(jnp.where(sub8 > z, count * weighted - targets, 0.0), axis=0, keepdims=True)
    here = jnp.sum(jnp.where(sub8 == z, weighted, 0.0), axis=0, keepdims=True)
    goal = jnp.sum(jnp.where(sub8 == z, targets, 0.0), axis=0, keepdims=True)
    left_over = ROWS * NZ - ROWS * z
    both = (left_over - jnp.maximum(subs16, lanes16)).astype(F32) * here
    both = both + (left_over - subs16).astype(F32) * south + north - jnp.where(lanes16 >= subs16, goal, 0.0)
    flux = coscol * jnp.sum(both, axis=1, keepdims=True)
    fb_ref[...] = jnp.broadcast_to(flux, (16, LANES))

    def scale_tile(slot, half, t):
        for way in range(2):
            cols = pl.ds(pl.multiple_of(half * 512 + t * 256 + way * LANES, LANES), LANES)
            for r in range(ROWS):
                rows = pl.ds(r * COLS, COLS)
                p_ref[slot, rows, way * LANES : (way + 1) * LANES] = (
                    u_ref[rows, cols].astype(F32) * fb_ref[r : r + 1, :]
                ).astype(BF16)

    def hidden_tile(ref, slot, t, part):
        tile = contract(n_ref[:, part * 512 : (part + 1) * 512], p_ref[slot])
        for way in range(2):
            ref[t, way, 2 * part : 2 * part + 2] = tile[:, way * LANES : (way + 1) * LANES].reshape(2, NX, 64, LANES)

    sibling = x * 2 + 1 - core
    tiles = ((give_ref, 1 - core, 0), (own_ref, core, 0), (give_ref, 1 - core, 1), (own_ref, core, 1))

    def place(way):
        return y if way == 0 else x

    def toward(way, step):
        if way == 0:
            return {"mem": lax.rem(y + step, NY)}
        return {"lon": lon_at(step)}

    def half(t, way, owner, which):
        rows = pl.ds(32 * which, 32)
        return own_ref.at[t, way, owner, :, rows] if way == 0 else own_ref.at[t, way, :, owner, rows]

    passes, plains, aggs = {}, {}, {}

    def hop(table, t, way, which, step, owner, target, sem):
        table[t, way, which] = launch(
            remote(
                half(t, way, owner, which),
                target.at[t, way, which],
                first_s.at[t, way, sem],
                first_r.at[t, way, sem],
                **toward(way, step),
            )
        )

    def first(t):
        for part in range(2):
            to_core[t, part].wait_recv()
        def add(way, step):
            owner = lax.rem(place(way) + step, 4)
            block = (t, way, owner) if way == 0 else (t, way, slice(None), owner)
            own_ref[block] = own_ref[block] + take_ref[block]

        for way in range(2):
            opposite = lax.rem(place(way) + 2, 4)
            add(way, 2)
            hop(passes, t, way, 0, 1, opposite, pass_ref, 0)
            hop(passes, t, way, 1, 3, opposite, pass_ref, 1)
        for way in range(2):
            for step in (1, 3, 0):
                add(way, step)
            hop(plains, t, way, 1, 1, lax.rem(place(way) + 1, 4), plain_ref, 2)
            hop(plains, t, way, 0, 3, lax.rem(place(way) + 3, 4), plain_ref, 3)

    def ring(t):
        for way in range(2):
            for which, step in ((0, 1), (1, 3)):
                owner = lax.rem(place(way) + step, 4)
                passes[t, way, which].wait_recv()
                mid = half(t, way, owner, which)
                mid[...] = mid[...] + pass_ref[t, way, which]
                hop(aggs, t, way, which, step, owner, agg_ref, 4 + which)

    to_core = {}
    scale_tile(0, *tiles[0][1:])
    for slot in range(4):
        ref, _, t = tiles[slot]
        for part in range(2):
            hidden_tile(ref, slot, t, part)
            if part == 0 and slot < 3:
                scale_tile(slot + 1, *tiles[slot + 1][1:])
            if ref is give_ref:
                y_half = pl.ds(2 * part, 2)
                to_core[t, part] = launch(
                    remote(
                        give_ref.at[t, :, y_half],
                        take_ref.at[t, :, y_half],
                        core_s.at[t, part],
                        core_r.at[t, part],
                        lon=sibling,
                    )
                )
        if slot == 2:
            first(0)
    first(1)

    gacc_ref[...] = jnp.zeros_like(gacc_ref)

    def latent_grad(i):
        rows = chunk_rows(i)
        flux = jnp.concatenate(
            [jnp.broadcast_to(fb_ref[2 * i + k : 2 * i + k + 1, :], (COLS, LANES)) for k in range(2)], axis=0
        )
        inv = inv_ref[rows, :] * flux
        coef = coef_ref[rows, :] * flux
        for tile in range(TILES):
            cols = slice(tile * LANES, (tile + 1) * LANES)
            xf = x_ref[rows, cols].astype(F32)
            scaled = v_ref[rows, cols] * inv
            gacc_ref[:, cols] += jnp.sum((scaled * xf).reshape(CHUNK // 8, 8, LANES), axis=0)
            outlat_ref[rows, cols] = (scaled * gain_ref[0:1, cols] - xf * coef).astype(BF16)

    for i in range(NCHUNK):
        latent_grad(i)
        if i == NCHUNK - 2:
            ring(0)

    small = jnp.zeros((8, D), F32)
    bias_sum = jnp.zeros((1, D), F32)
    for r in range(ROWS):
        scale = fb_ref[r : r + 1, 0:1]
        small = small + s_ref[r * 8 : (r + 1) * 8, :] * scale
        bias_sum = bias_sum + b_ref[r : r + 1, :] * scale
    gain_sum = jnp.sum(gacc_ref[...], axis=0, keepdims=True)
    row8 = lax.broadcasted_iota(jnp.int32, (8, D), 0)
    small = jnp.where(row8 == 3, bias_sum, jnp.where(row8 == 4, gain_sum, small))
    for k in range(NLON):
        sm_ref[k] = small[:, k * LANES : (k + 1) * LANES]
    sm1 = []
    for k in range(1, NLON):
        peer = lax.rem(lon + k, NLON)
        sm1.append(launch(remote(sm_ref.at[peer], sm1_ref.at[lon], sm1_s.at[k - 1], sm1_r.at[k - 1], lon=peer)))
    sm1_ref[lon] = sm_ref[lon]

    crosses, depths, agz = {}, {}, {}

    def cross(t):
        for way in range(2):
            for which in range(2):
                plains[t, way, which].wait_recv()
                aggs[t, way, which].wait_recv()
                part_ref[t, way, :, 32 * which : 32 * (which + 1)] = (
                    half(t, way, place(way), which)[...] + plain_ref[t, way, which] + agg_ref[t, way, which]
                )
            other = 1 - way
            for k in (2, 1, 3):
                crosses[t, way, k] = launch(
                    remote(
                        part_ref.at[t, way, lax.rem(place(other) + k, 4)],
                        cross_ref.at[t, way, k - 1],
                        cross_s.at[t, way, k - 1],
                        cross_r.at[t, way, k - 1],
                        **toward(other, k),
                    )
                )

    def deepen(t):
        for way in range(2):
            for k in range(1, 4):
                crosses[t, way, k].wait_recv()
            piece = part_ref[t, way, place(1 - way)] + cross_ref[t, way, 0] + cross_ref[t, way, 1] + cross_ref[t, way, 2]
            piece_ref[t, :, way] = piece.reshape(NZ, 8, LANES)
        for k in by_distance:
            peer = lax.rem(z + k, NZ)
            depths[t, k] = launch(
                remote(
                    piece_ref.at[t, peer], depth_ref.at[t, k - 1], depth_s.at[t, k - 1], depth_r.at[t, k - 1], lat=peer
                )
            )

    slots = (0, 1, 7, 2, 6, 3, 5, 4)
    slot_of = {k: slots.index(k) for k in range(NZ)}

    def finish(t):
        for k in range(1, NZ):
            depths[t, k].wait_recv()
        piece = piece_ref[t, z]
        for k in range(NZ - 1):
            piece = piece + depth_ref[t, k]
        hid_ref[core, t, x, 0] = piece
        for k in by_distance:
            agz[t, k] = launch(
                remote(
                    hid_ref.at[core, t, x, 0],
                    hid_ref.at[core, t, x, slot_of[NZ - k]],
                    agz_s.at[t, k - 1],
                    agz_r.at[t, k - 1],
                    lat=lax.rem(z + k, NZ),
                )
            )

    groups = (((0, 5), (5, 8)), ((0, 5), (5, 8)))
    agx, agc = {}, {}

    def spread(t, g):
        start, stop = groups[t][g]
        for k in range(1, NZ):
            if start <= slot_of[NZ - k] < stop:
                agz[t, k].wait_recv()
        spot = hid_ref.at[core, t, x, pl.ds(start, stop - start)]
        for k in (2, 1, 3):
            agx[t, g, k] = launch(remote(spot, spot, agx_s.at[t, g, k - 1], agx_r.at[t, g, k - 1], lon=lon_at(k)))
        agc[t, g, 0] = launch(remote(spot, spot, agc_s.at[t, g, 0], agc_r.at[t, g, 0], lon=sibling))

    def to_sibling(t, g):
        start, stop = groups[t][g]
        for k in (1, 3, 2):
            agx[t, g, k].wait_recv()
            spot = hid_ref.at[core, t, lax.rem(x + 4 - k, NX), pl.ds(start, stop - start)]
            agc[t, g, k] = launch(remote(spot, spot, agc_s.at[t, g, k], agc_r.at[t, g, k], lon=sibling))

    def place_rows(half, t, g):
        start, stop = groups[t][g]
        for xi in range(NX):
            for k in (k for k in range(NZ) if start <= slot_of[k] < stop):
                rows = pl.ds(pl.multiple_of(xi * 64 + lax.rem(z + k, NZ) * 8, 8), 8)
                for way in range(2):
                    cols = pl.ds(pl.multiple_of(half * 512 + t * 256 + way * LANES, LANES), LANES)
                    outhid_ref[rows, cols] = hid_ref[half, t, xi, slot_of[k], way]

    def drain(count):
        for copy in sent[:count]:
            copy.wait_send()
        del sent[:count]

    ring(1)
    drain(len(ex1) + len(ex2) + len(to_core))
    cross(0)
    cross(1)
    for copy in sm1:
        copy.wait_recv()
    t1_ref[...] = jnp.sum(sm1_ref[...], axis=0)
    sm2 = [
        launch(remote(t1_ref, sm2_ref.at[z], sm2_s.at[k - 1], sm2_r.at[k - 1], lat=lax.rem(z + k, NZ)))
        for k in by_distance
    ]
    sm2_ref[z] = t1_ref[...]
    drain(len(passes) + len(plains) + len(sm1) + len(aggs))
    deepen(0)
    deepen(1)
    for copy in sm2:
        copy.wait_recv()
    t2_ref[...] = jnp.sum(sm2_ref[...], axis=0)
    sm3 = [
        launch(remote(t2_ref, sm3_ref.at[y], sm3_s.at[k - 1], sm3_r.at[k - 1], mem=lax.rem(y + k, NY)))
        for k in range(1, NY)
    ]
    sm3_ref[y] = t2_ref[...]
    drain(len(crosses) + len(sm2))
    finish(0)
    finish(1)
    for copy in sm3:
        copy.wait_recv()
    smo_ref[lon] = jnp.sum(sm3_ref[...], axis=0)
    sm4 = [
        launch(remote(smo_ref.at[lon], smo_ref.at[lon], sm4_s.at[k - 1], sm4_r.at[k - 1], lon=lax.rem(lon + k, NLON)))
        for k in by_distance
    ]
    drain(len(depths) + len(sm3))
    spread(0, 0)
    spread(0, 1)
    spread(1, 0)
    spread(1, 1)
    for copy in sm4:
        copy.wait_recv()
    summed = jnp.concatenate([smo_ref[k] for k in range(NLON)], axis=1)
    outbias_ref[...] = summed[3:4, :]
    outgain_ref[...] = summed[4:5, :]
    outw_ref[...] = lax.dot_general(
        tab_ref[...], summed, (((0,), (0,)), ((), ())), precision=HIGH, preferred_element_type=F32
    )
    drain(len(agz) + len(sm4))
    to_sibling(0, 0)
    to_sibling(0, 1)
    for g in range(2):
        place_rows(core, 0, g)
    to_sibling(1, 0)
    to_sibling(1, 1)
    drain(len(agx))
    for g in range(2):
        for k in range(4):
            agc[0, g, k].wait_recv()
        place_rows(1 - core, 0, g)
    for g in range(2):
        place_rows(core, 1, g)
    drain(len(sent))
    for g in range(2):
        for k in range(4):
            agc[1, g, k].wait_recv()
        place_rows(1 - core, 1, g)


def write_out(*refs):
    sems = refs[-1]
    half = len(refs) // 2
    copies = []
    for source, target in zip(refs[:half], refs[half:-1]):
        rows = source.shape[0]
        step = min(rows, 256 if source.dtype == BF16 else 64)
        for start in range(0, rows - rows % step, step):
            part = pl.ds(start, step) if step < rows else slice(None)
            copies.append(pltpu.make_async_copy(source.at[part], target.at[part], sems.at[len(copies)]))
        if rows % step:
            part = pl.ds(rows - rows % step, rows % step)
            copies.append(pltpu.make_async_copy(source.at[part], target.at[part], sems.at[len(copies)]))
    for copy in copies:
        copy.start()
    for copy in copies:
        copy.wait()


def on_device(latent, norm_gain, hidden_weight, hidden_bias, output_weight, flux_table, target, land_sea, band_index):
    vmem = pl.BlockSpec(memory_space=pltpu.VMEM)
    hbm = pl.BlockSpec(memory_space=pl.ANY)
    dma = pltpu.SemaphoreType.DMA
    scratch = [
        pltpu.VMEM((CELLS, D), BF16),
        pltpu.VMEM((D, D), BF16),
        pltpu.VMEM((1, D), F32),
        pltpu.VMEM((1, D), F32),
        pltpu.VMEM((80, D), BF16),
        pltpu.VMEM((3, 80), F32),
        pltpu.VMEM((1, ROWS), F32),
        pltpu.VMEM((ROWS, COLS), jnp.int32),
        pltpu.VMEM((1, ROWS), jnp.int32),
        pltpu.VMEM((CELLS, D), BF16),
        pltpu.VMEM((CELLS, D), F32),
        pltpu.VMEM((CELLS, D), BF16),
        pltpu.VMEM((4, CELLS, 256), BF16),
        pltpu.VMEM((CELLS, LANES), F32),
        pltpu.VMEM((CELLS, LANES), F32),
        pltpu.VMEM((CELLS, LANES), F32),
        pltpu.VMEM((LANES, LANES), F32),
        pltpu.VMEM((8, D), F32),
        pltpu.VMEM((8, 80), F32),
        pltpu.VMEM((ROWS * 8, D), F32),
        pltpu.VMEM((16, D), F32),
        pltpu.VMEM((16, LANES), F32),
        pltpu.VMEM((8, D), F32),
        pltpu.VMEM((8, LANES), F32),
        pltpu.VMEM((NLON, 8, LANES), F32),
        pltpu.VMEM((8, LANES), F32),
        pltpu.VMEM((NZ, 8, LANES), F32),
        pltpu.VMEM((2, 2, NY, NX, 64, LANES), F32),
        pltpu.VMEM((2, 2, NY, NX, 64, LANES), F32),
        pltpu.VMEM((2, 2, NY, NX, 64, LANES), F32),
        pltpu.VMEM((2, 2, 2, 4, 32, LANES), F32),
        pltpu.VMEM((2, 2, 2, 4, 32, LANES), F32),
        pltpu.VMEM((2, 2, 2, 4, 32, LANES), F32),
        pltpu.VMEM((2, 2, 4, 64, LANES), F32),
        pltpu.VMEM((2, 2, 3, 64, LANES), F32),
        pltpu.VMEM((2, NZ, 2, 8, LANES), F32),
        pltpu.VMEM((2, NZ - 1, 2, 8, LANES), F32),
        pltpu.VMEM((2, 2, NX, NZ, 2, 8, LANES), F32),
        pltpu.VMEM((NLON, 8, LANES), F32),
        pltpu.VMEM((NLON, 8, LANES), F32),
        pltpu.VMEM((8, LANES), F32),
        pltpu.VMEM((NZ, 8, LANES), F32),
        pltpu.VMEM((8, LANES), F32),
        pltpu.VMEM((NY, 8, LANES), F32),
        pltpu.VMEM((NLON, 8, LANES), F32),
        dma((NCHUNK,)),
        dma((4,)),
        dma((7,)),
        dma((7,)), dma((7,)),
        dma((7,)), dma((7,)),
        dma((2, 2)), dma((2, 2)),
        dma((2, 2, 6)), dma((2, 2, 6)),
        dma((2, 2, 3)), dma((2, 2, 3)),
        dma((2, 7)), dma((2, 7)),
        dma((2, 7)), dma((2, 7)),
        dma((2, 2, 3)), dma((2, 2, 3)),
        dma((2, 2, 4)), dma((2, 2, 4)),
        dma((7,)), dma((7,)),
        dma((7,)), dma((7,)),
        dma((3,)), dma((3,)),
        dma((7,)), dma((7,)),
    ]
    shapes = (((CELLS, D), BF16), ((D // NY, D), F32), ((80, D), F32), ((1, D), F32), ((1, D), F32))
    held = pl.pallas_call(
        kernel,
        out_shape=tuple(pltpu.VMEM(*shape) for shape in shapes),
        in_specs=[hbm] * 9,
        out_specs=(vmem,) * 5,
        scratch_shapes=scratch,
        compiler_params=pltpu.CompilerParams(
            collective_id=0, has_side_effects=True, vmem_limit_bytes=56 * 1024 * 1024
        ),
        cost_estimate=pl.CostEstimate(flops=10_000_000_000, bytes_accessed=9_000_000, transcendentals=3_000_000),
    )(
        latent.reshape(CELLS, D),
        norm_gain.reshape(1, D),
        hidden_weight,
        hidden_bias.reshape(1, D),
        output_weight.T,
        flux_table,
        target,
        land_sea,
        band_index.reshape(1, ROWS),
    )
    grad_cells, grad_hidden, grad_out, grad_gain, grad_bias = pl.pallas_call(
        write_out,
        out_shape=tuple(jax.ShapeDtypeStruct(*shape) for shape in shapes),
        in_specs=[vmem] * 5,
        out_specs=(hbm,) * 5,
        scratch_shapes=[dma((16,))],
        compiler_params=pltpu.CompilerParams(vmem_limit_bytes=1024 * 1024),
    )(*[pltpu.with_memory_space_constraint(array, pltpu.VMEM) for array in held])
    return (
        grad_cells.reshape(latent.shape),
        grad_hidden,
        grad_out.T,
        grad_gain.reshape(D),
        grad_bias.reshape(D),
    )


def solution(mesh):
    return jax.shard_map(
        on_device,
        mesh=mesh,
        in_specs=(
            P("mem", "lat", "lon", None),
            P(),
            P(),
            P(),
            P(),
            P(),
            P("mem", "lat"),
            P("lat", "lon"),
            P("lat"),
        ),
        out_specs=(P("mem", "lat", "lon", None), P("mem", None), P(), P(), P()),
        check_vma=False,
    )
```
